32 devices in a mesh: dp: 8 (over y, x, core), seq: 4 (over z).
Axes of the slice: x: 2, y: 2, z: 4, core: 2. Of those that a mesh axis runs over, the one named last changes fastest.
Arguments:
- clips: bfloat16 [16, 8, 14, 14, 512], P('dp', 'seq'), may hold values from -6 to 6
- out_grad: bfloat16 [16, 8, 14, 14, 512], P('dp', 'seq'), may hold values from -6 to 6
- clip_order: int32 [8, 2], P('dp'), may hold values from 0 to 1, each once within a row
- region_label: int32 [4, 392], replicated, may hold values from 0 to 3
- rel_index: int32 [392, 392], replicated, may hold values from 0 to 2534
- norm1_gain: bfloat16 [512], P(('dp', 'seq')), may hold values from 0.5 to 1.5
- norm1_bias: bfloat16 [512], P(('dp', 'seq')), may hold values from -3 to 3
- qkv_weight: bfloat16 [512, 1536], P(('dp', 'seq')), may hold values from -0.25 to 0.25
- qv_bias: bfloat16 [2, 512], P(None, ('dp', 'seq')), may hold values from -3 to 3
- bias_table: bfloat16 [16, 2535], P('seq'), may hold values from -3 to 3
- proj_weight: bfloat16 [512, 512], P(('dp', 'seq')), may hold values from -1.5 to 1.5
- proj_bias: bfloat16 [512], P(('dp', 'seq')), may hold values from -3 to 3
- norm2_gain: bfloat16 [512], P(('dp', 'seq')), may hold values from 0.5 to 1.5
- norm2_bias: bfloat16 [512], P(('dp', 'seq')), may hold values from -3 to 3
- fc1_weight: bfloat16 [512, 2048], P(('dp', 'seq')), may hold values from -0.25 to 0.25
- fc1_bias: bfloat16 [2048], P(('dp', 'seq')), may hold values from -3 to 3
- fc2_weight: bfloat16 [2048, 512], P(('dp', 'seq')), may hold values from -0.1875 to 0.1875
- fc2_bias: bfloat16 [512], P(('dp', 'seq')), may hold values from -3 to 3
Outputs:
- output: bfloat16 [16, 8, 14, 14, 512], P('dp', 'seq')
- clips_grad: bfloat16 [16, 8, 14, 14, 512], P('dp', 'seq')
- norm1_gain_grad: float32 [512], P(('dp', 'seq'))
- norm1_bias_grad: float32 [512], P(('dp', 'seq'))
- qkv_weight_grad: float32 [512, 1536], P(('dp', 'seq'))
- qv_bias_grad: float32 [2, 512], P(None, ('dp', 'seq'))
- bias_table_grad: float32 [16, 2535], P('seq')
- proj_weight_grad: float32 [512, 512], P(('dp', 'seq'))
- proj_bias_grad: float32 [512], P(('dp', 'seq'))
- norm2_gain_grad: float32 [512], P(('dp', 'seq'))
- norm2_bias_grad: float32 [512], P(('dp', 'seq'))
- fc1_weight_grad: float32 [512, 2048], P(('dp', 'seq'))
- fc1_bias_grad: float32 [2048], P(('dp', 'seq'))
- fc2_weight_grad: float32 [2048, 512], P(('dp', 'seq'))
- fc2_bias_grad: float32 [512], P(('dp', 'seq'))
The draws below stay inside these ranges and needn't reach their ends.
Inputs may be any that keep to these rules, and one draw needn't show every extreme that they name: `clip_order`: each row is a permutation of 0 to 1.
All inputs are finite; a program needn't handle non-finite values.
Results may differ from the reference program's by a relative error of at most 0.011.
Values may be sent and summed in bfloat16 or wider, within the bound.
A program may use at most 256 MiB of HBM per device.

```python
import jax
import jax.numpy as jnp
from jax import lax

C = 512
NH = 16
HD = 32
FF = 2048
WIN_T = 8
WIN_S = 7
SHIFT_T = 4
SHIFT_S = 3
FR = 8
SIDE = 14
CLIPS_DEV = 2
CLIPS = 16
NWIN = 4
WT = 392
TBL = 2535
N_DP = 8


def touch_ends(values, key, low, largest):
    longest = values.shape.index(max(values.shape))
    spots = []
    for shift in (0, 1):
        where = [jax.random.randint(jax.random.fold_in(key, axis), (), 0, length) for axis, length in enumerate(values.shape)]
        where[longest] = (where[longest] + shift) % values.shape[longest]
        spots.append(tuple(where))
    return values.at[spots[0]].set(low).at[spots[1]].set(largest)


def block_levels(own_key, dims, pieces, least, largest):
    level = 1.0
    for dim, blocks in pieces:
        steps = jax.random.uniform(jax.random.fold_in(jax.random.fold_in(own_key, 6), dim), (blocks,), jnp.float32, least / len(pieces), largest / len(pieces))
        level = level * jnp.repeat(jnp.exp(steps), dims[dim] // blocks).reshape((-1,) + (1,) * (len(dims) - 1 - dim))
    return level


def gaussian(key, shape, width, reach, cuts=(), kind=jnp.bfloat16):
    entries = width * jax.random.normal(key, shape, jnp.float32)
    if cuts:
        entries = entries * block_levels(key, shape, cuts, -0.22, 0.18)
    return jnp.clip(entries, -reach, reach).astype(kind)


def setup_inputs(seed: int = 0) -> dict:
    seeds = jax.random.split(jax.random.key(seed), 19)
    return {
        "clips": gaussian(seeds[0], (CLIPS, FR, SIDE, SIDE, C), 1.0, 6.0, ((0, 8), (1, 4))),
        "out_grad": gaussian(seeds[1], (CLIPS, FR, SIDE, SIDE, C), 1.0, 6.0, ((0, 8), (1, 4))),
        "clip_order": jax.vmap(lambda own: jax.random.permutation(own, CLIPS_DEV))(jax.random.split(seeds[2], N_DP)).reshape((N_DP, CLIPS_DEV)).astype(jnp.int32),
        "region_label": touch_ends(jax.random.randint(seeds[3], (NWIN, WT), 0, 4), jax.random.fold_in(seeds[3], 1), 0, 3).astype(jnp.int32),
        "rel_index": touch_ends(jax.random.randint(seeds[4], (WT, WT), 0, TBL), jax.random.fold_in(seeds[4], 1), 0, TBL - 1).astype(jnp.int32),
        "norm1_gain": jnp.clip(1.0 + 0.1 * jax.random.normal(seeds[5], (C,), jnp.float32), 0.5, 1.5).astype(jnp.bfloat16),
        "norm1_bias": gaussian(seeds[6], (C,), 0.3, 3.0, ((0, 32),)),
        "qkv_weight": gaussian(seeds[7], (C, 3 * C), C ** -0.5, 0.25, ((0, 32),)),
        "qv_bias": gaussian(seeds[8], (2, C), 0.5, 3.0, ((1, 32),)),
        "bias_table": gaussian(seeds[9], (NH, TBL), 0.5, 3.0, ((0, 4),)),
        "proj_weight": gaussian(seeds[10], (C, C), (C // 32) ** -0.5, 1.5, ((0, 32),)),
        "proj_bias": gaussian(seeds[11], (C,), 0.3, 3.0, ((0, 32),)),
        "norm2_gain": jnp.clip(1.0 + 0.1 * jax.random.normal(seeds[12], (C,), jnp.float32), 0.5, 1.5).astype(jnp.bfloat16),
        "norm2_bias": gaussian(seeds[13], (C,), 0.3, 3.0, ((0, 32),)),
        "fc1_weight": gaussian(seeds[14], (C, FF), C ** -0.5, 0.25, ((0, 32),)),
        "fc1_bias": gaussian(seeds[15], (FF,), 0.5, 3.0, ((0, 32),)),
        "fc2_weight": gaussian(seeds[16], (FF, C), (FF // 2) ** -0.5, 0.1875, ((0, 32),)),
        "fc2_bias": gaussian(seeds[17], (C,), 0.3, 3.0, ((0, 32),)),
    }


@jax.custom_vjp
def low(v):
    return lax.optimization_barrier(v.astype(jnp.bfloat16)).astype(jnp.float32)

@jax.custom_vjp
def low_back(v):
    return v

def low_keep(v):
    return (low(v), None)

def low_pass(kept, grad):
    return (grad,)

def back_keep(v):
    return (v, None)

def back_low(kept, grad):
    return (low(grad),)
low.defvjp(low_keep, low_pass)
low_back.defvjp(back_keep, back_low)
highest = lax.Precision.HIGHEST
eps_norm = 1e-05

def layer_norm(values, norm_gain, norm_shift):
    average = lax.optimization_barrier(jnp.mean(values, axis=-1, keepdims=True))
    centred = values - average
    variance = lax.optimization_barrier(jnp.mean(centred * centred, axis=-1, keepdims=True))
    return centred * lax.rsqrt(variance + eps_norm) * norm_gain + norm_shift

def window_split(field):
    rolled = jnp.roll(field, (-SHIFT_T, -SHIFT_S, -SHIFT_S), (0, 1, 2))
    blocks = rolled.reshape(FR // WIN_T, WIN_T, SIDE // WIN_S, WIN_S, SIDE // WIN_S, WIN_S, -1)
    return blocks.transpose(0, 2, 4, 1, 3, 5, 6).reshape(NWIN, WT, -1)

def window_merge(windows):
    blocks = windows.reshape(FR // WIN_T, SIDE // WIN_S, SIDE // WIN_S, WIN_T, WIN_S, WIN_S, -1)
    field = blocks.transpose(0, 3, 1, 4, 2, 5, 6).reshape(FR, SIDE, SIDE, -1)
    return jnp.roll(field, (SHIFT_T, SHIFT_S, SHIFT_S), (0, 1, 2))

def clip_forward(weight_set, one_clip, keep_mask, rel_index):
    norm1_gain, norm1_bias, qkv_weight, qv_bias, bias_table, proj_weight, proj_bias, norm2_gain, norm2_bias, fc1_weight, fc1_bias, fc2_weight, fc2_bias = weight_set
    token_rows = one_clip.reshape(-1, C)
    normed = low(layer_norm(token_rows, norm1_gain, norm1_bias))
    query_rows = low_back(low(jnp.dot(normed, qkv_weight[:, :C], precision=highest) + qv_bias[0]))
    key_rows = low_back(low(jnp.dot(normed, qkv_weight[:, C:2 * C], precision=highest)))
    value_rows = low_back(low(jnp.dot(normed, qkv_weight[:, 2 * C:], precision=highest) + qv_bias[1]))

    def to_heads(field_rows):
        return window_split(field_rows.reshape(FR, SIDE, SIDE, C)).reshape(NWIN, WT, NH, HD)
    rel_bias = jnp.take(bias_table, rel_index, axis=1)
    scores = jnp.einsum('wihd,wjhd->whij', to_heads(query_rows), to_heads(key_rows), precision=highest)
    scores = scores * HD ** (-0.5) + rel_bias[None]
    scores = low_back(jnp.where(keep_mask[:, None], scores, -1e+30))
    probabilities = jax.nn.softmax(scores, axis=-1)
    attended = jnp.einsum('whij,wjhd->wihd', low(probabilities), to_heads(value_rows), precision=highest)
    attended = low_back(low(attended))
    merged = window_merge(attended.reshape(NWIN, WT, C)).reshape(-1, C)
    branch = low_back(jnp.dot(merged, proj_weight, precision=highest) + proj_bias)
    middle = token_rows + branch
    normed_mid = low(layer_norm(middle, norm2_gain, norm2_bias))
    hidden = low_back(jnp.dot(normed_mid, fc1_weight, precision=highest) + fc1_bias)
    active = low(jax.nn.gelu(hidden, approximate=False))
    result = low_back(jnp.dot(active, fc2_weight, precision=highest) + fc2_bias)
    return (middle + result).reshape(one_clip.shape)

def reference(clips, out_grad, clip_order, region_label, rel_index, norm1_gain, norm1_bias, qkv_weight, qv_bias, bias_table, proj_weight, proj_bias, norm2_gain, norm2_bias, fc1_weight, fc1_bias, fc2_weight, fc2_bias):
    slot_order = (jnp.arange(N_DP, dtype=jnp.int32)[:, None] * CLIPS_DEV + clip_order).reshape(-1).astype(jnp.int32)
    keep_mask = region_label[:, :, None] == region_label[:, None, :]
    weight_list = (norm1_gain, norm1_bias, qkv_weight, qv_bias, bias_table, proj_weight, proj_bias, norm2_gain, norm2_bias, fc1_weight, fc1_bias, fc2_weight, fc2_bias)
    weight_set = tuple((weight_array.astype(jnp.float32) for weight_array in weight_list))

    def forward(source, weights_in):
        picked = jnp.take(source, slot_order, axis=0)
        clip_step = jax.checkpoint(lambda one_clip: clip_forward(weights_in, one_clip, keep_mask, rel_index))
        return lax.map(clip_step, picked)
    output, pullback = jax.vjp(forward, clips.astype(jnp.float32), weight_set)
    clips_grad, weight_grads = pullback(out_grad.astype(jnp.float32))
    grad_g1, grad_b1, grad_qkv, grad_qv, grad_table, grad_proj_w, grad_proj_b, grad_g2, grad_b2, grad_fc1_w, grad_fc1_b, grad_fc2_w, grad_fc2_b = weight_grads
    return (output.astype(jnp.bfloat16), clips_grad.astype(jnp.bfloat16), grad_g1, grad_b1, grad_qkv, grad_qv, grad_table, grad_proj_w, grad_proj_b, grad_g2, grad_b2, grad_fc1_w, grad_fc1_b, grad_fc2_w, grad_fc2_b)
```

```python
import functools
import math

import jax
import jax.numpy as jnp
import numpy as np
from jax import lax
from jax.experimental import pallas as pl
from jax.experimental.pallas import tpu as pltpu
from jax.sharding import PartitionSpec as P

HD = 32
WIN_T = 8
WIN_S = 7
SHIFT_T = 4
SHIFT_S = 3
FR = 8
SIDE = 14
MICRO = 2
NWIN = 4
WT = 392
TBL = 2535


eps_norm = 1e-05


def layer_norm(values, norm_gain, norm_shift):
    average = jnp.mean(values, axis=-1, keepdims=True)
    centred = values - average
    variance = jnp.mean(centred * centred, axis=-1, keepdims=True)
    return centred * lax.rsqrt(variance + eps_norm) * norm_gain + norm_shift


def gelu_exact(values):
    return jax.nn.gelu(values, approximate=False)


def matmul(left_side, right_side):
    return jnp.dot(left_side, right_side, preferred_element_type=jnp.float32)


def window_split(field):
    rolled = jnp.roll(field, (-SHIFT_T, -SHIFT_S, -SHIFT_S), (0, 1, 2))
    blocks = rolled.reshape(FR // WIN_T, WIN_T, SIDE // WIN_S, WIN_S, SIDE // WIN_S, WIN_S, -1)
    return blocks.transpose(0, 2, 4, 1, 3, 5, 6).reshape(NWIN, WT, -1)


def window_merge(windows):
    blocks = windows.reshape(FR // WIN_T, SIDE // WIN_S, SIDE // WIN_S, WIN_T, WIN_S, WIN_S, -1)
    field = blocks.transpose(0, 3, 1, 4, 2, 5, 6).reshape(FR, SIDE, SIDE, -1)
    return jnp.roll(field, (SHIFT_T, SHIFT_S, SHIFT_S), (0, 1, 2))


def to_heads(field_rows):
    feature_count = field_rows.shape[-1]
    windows = window_split(field_rows.reshape(FR, SIDE, SIDE, feature_count))
    return windows.reshape(NWIN, WT, feature_count // HD, HD)


def from_heads(windows):
    feature_count = windows.shape[-1] * windows.shape[-2]
    merged = window_merge(windows.reshape(NWIN, WT, feature_count))
    return merged.reshape(-1, feature_count)


def window_scores(query_win, key_win, rel_bias, keep_mask):
    scores = jnp.einsum("wihd,wjhd->whij", query_win, key_win, preferred_element_type=jnp.float32)
    scores = scores * HD ** (-0.5) + rel_bias[None]
    return jnp.where(keep_mask[:, None], scores, -1e30)


def attend_clip(query_rows, key_rows, value_rows, rel_bias, keep_mask):
    scores = window_scores(to_heads(query_rows), to_heads(key_rows), rel_bias, keep_mask)
    row_max = jnp.max(scores, axis=-1, keepdims=True)
    exponent = jnp.exp(scores - row_max)
    row_total = jnp.sum(exponent, axis=-1, keepdims=True)
    probabilities = (exponent / row_total).astype(jnp.bfloat16)
    attended = jnp.einsum(
        "whij,wjhd->wihd", probabilities, to_heads(value_rows), preferred_element_type=jnp.float32
    ).astype(jnp.bfloat16)
    return (from_heads(attended), (row_max + jnp.log(row_total))[..., 0])


def attend_back(query_rows, key_rows, value_rows, grad_rows, log_total, rel_bias, keep_mask):
    query_win = to_heads(query_rows)
    key_win = to_heads(key_rows)
    value_win = to_heads(value_rows)
    grad_win = to_heads(grad_rows)
    scores = window_scores(query_win, key_win, rel_bias, keep_mask)
    probabilities = jnp.exp(scores - log_total[..., None])
    grad_probs = jnp.einsum(
        "wihd,wjhd->whij", grad_win, value_win, preferred_element_type=jnp.float32
    )
    row_inner = jnp.sum(probabilities * grad_probs, axis=-1, keepdims=True)
    grad_scores = (probabilities * (grad_probs - row_inner)).astype(jnp.bfloat16)
    score_scale = HD ** (-0.5)
    grad_query = (
        jnp.einsum("whij,wjhd->wihd", grad_scores, key_win, preferred_element_type=jnp.float32)
        * score_scale
    )
    grad_key = (
        jnp.einsum("whij,wihd->wjhd", grad_scores, query_win, preferred_element_type=jnp.float32)
        * score_scale
    )
    grad_value = jnp.einsum(
        "whij,wihd->wjhd",
        probabilities.astype(jnp.bfloat16),
        grad_win,
        preferred_element_type=jnp.float32,
    )
    bias_term = jnp.sum(grad_scores.astype(jnp.float32), axis=0)
    return (
        from_heads(grad_query).astype(jnp.bfloat16),
        from_heads(grad_key).astype(jnp.bfloat16),
        from_heads(grad_value).astype(jnp.bfloat16),
        bias_term,
    )


def layer_pass(source, cot_block, full_weights, rel_bias, keep_mask):
    (
        norm_in_gain,
        norm_in_shift,
        qkv_w,
        qv_b,
        proj_w,
        proj_b,
        norm_mid_gain,
        norm_mid_shift,
        fc1_w,
        fc1_b,
        fc2_w,
        fc2_b,
    ) = full_weights
    clip_count = source.shape[0]
    model_width = source.shape[-1]
    shaped = (clip_count, -1, model_width)
    token_rows = source.reshape(-1, model_width).astype(jnp.float32)
    normed, norm_in_back = jax.vjp(
        layer_norm, token_rows, norm_in_gain.astype(jnp.float32), norm_in_shift.astype(jnp.float32)
    )
    normed_low = normed.astype(jnp.bfloat16)
    projected = matmul(normed_low, qkv_w)
    qv_float = qv_b.astype(jnp.float32)
    query_rows = (projected[:, :model_width] + qv_float[0]).astype(jnp.bfloat16)
    key_rows = projected[:, model_width : 2 * model_width].astype(jnp.bfloat16)
    value_rows = (projected[:, 2 * model_width :] + qv_float[1]).astype(jnp.bfloat16)
    parts = (
        lax.all_to_all(query_rows.reshape(shaped), "seq", split_axis=2, concat_axis=1, tiled=True),
        lax.all_to_all(key_rows.reshape(shaped), "seq", split_axis=2, concat_axis=1, tiled=True),
        lax.all_to_all(value_rows.reshape(shaped), "seq", split_axis=2, concat_axis=1, tiled=True),
    )
    merged_heads, log_total = lax.map(
        lambda clip_parts: attend_clip(*clip_parts, rel_bias, keep_mask), parts
    )
    attended_heads, log_total, query_heads, key_heads, value_heads = (
        merged_heads,
        log_total,
        parts[0],
        parts[1],
        parts[2],
    )
    attended = lax.all_to_all(
        attended_heads, "seq", split_axis=1, concat_axis=2, tiled=True
    ).reshape(-1, model_width)
    branch = matmul(attended, proj_w) + proj_b.astype(jnp.float32)
    middle = token_rows + branch
    normed_mid, norm_mid_back = jax.vjp(
        layer_norm, middle, norm_mid_gain.astype(jnp.float32), norm_mid_shift.astype(jnp.float32)
    )
    normed_mid_low = normed_mid.astype(jnp.bfloat16)
    hidden = matmul(normed_mid_low, fc1_w) + fc1_b.astype(jnp.float32)
    active, gelu_back = jax.vjp(gelu_exact, hidden)
    active_low = active.astype(jnp.bfloat16)
    result = matmul(active_low, fc2_w) + fc2_b.astype(jnp.float32)
    output = (middle + result).astype(jnp.bfloat16).reshape(source.shape)
    grad_low = cot_block.reshape(-1, model_width)
    grad_float = grad_low.astype(jnp.float32)
    grad_fc2_w = matmul(active_low.T, grad_low)
    grad_fc2_b = jnp.sum(grad_float, axis=0)
    grad_active = matmul(grad_low, fc2_w.T)
    grad_hidden = gelu_back(grad_active)[0].astype(jnp.bfloat16)
    grad_fc1_w = matmul(normed_mid_low.T, grad_hidden)
    grad_fc1_b = jnp.sum(grad_hidden.astype(jnp.float32), axis=0)
    grad_normed_mid = matmul(grad_hidden, fc1_w.T)
    grad_mid_part, grad_mid_gain, grad_mid_shift = norm_mid_back(grad_normed_mid)
    grad_middle = grad_float + grad_mid_part
    grad_branch = grad_middle.astype(jnp.bfloat16)
    grad_proj_w = matmul(attended.T, grad_branch)
    grad_proj_b = jnp.sum(grad_branch.astype(jnp.float32), axis=0)
    grad_attended = matmul(grad_branch, proj_w.T).astype(jnp.bfloat16)
    grad_heads = lax.all_to_all(
        grad_attended.reshape(shaped), "seq", split_axis=2, concat_axis=1, tiled=True
    )
    grad_query, grad_key, grad_value, bias_terms = lax.map(
        lambda clip_parts: attend_back(*clip_parts, rel_bias, keep_mask),
        (query_heads, key_heads, value_heads, grad_heads, log_total),
    )
    grad_query, grad_key, grad_value = (
        lax.all_to_all(grad_query, "seq", split_axis=1, concat_axis=2, tiled=True),
        lax.all_to_all(grad_key, "seq", split_axis=1, concat_axis=2, tiled=True),
        lax.all_to_all(grad_value, "seq", split_axis=1, concat_axis=2, tiled=True),
    )
    grad_query = grad_query.reshape(-1, model_width)
    grad_value = grad_value.reshape(-1, model_width)
    grad_projected = jnp.concatenate(
        [grad_query, grad_key.reshape(-1, model_width), grad_value], axis=1
    )
    grad_qkv_w = matmul(normed_low.T, grad_projected)
    grad_qv_b = jnp.stack(
        [
            jnp.sum(grad_query.astype(jnp.float32), axis=0),
            jnp.sum(grad_value.astype(jnp.float32), axis=0),
        ]
    )
    grad_normed = matmul(grad_projected, qkv_w.T)
    grad_rows_part, grad_in_gain, grad_in_shift = norm_in_back(grad_normed)
    grad_source = (grad_middle + grad_rows_part).astype(jnp.bfloat16).reshape(source.shape)
    grad_terms = (
        grad_in_gain,
        grad_in_shift,
        grad_qkv_w,
        grad_qv_b,
        grad_proj_w,
        grad_proj_b,
        grad_mid_gain,
        grad_mid_shift,
        grad_fc1_w,
        grad_fc1_b,
        grad_fc2_w,
        grad_fc2_b,
    )
    return (output, grad_source, grad_terms, jnp.sum(bias_terms, axis=0))


def shards(
    clips,
    out_grad,
    clip_order,
    region_label,
    rel_index,
    norm1_gain,
    norm1_bias,
    qkv_weight,
    qv_bias,
    bias_table,
    proj_weight,
    proj_bias,
    norm2_gain,
    norm2_bias,
    fc1_weight,
    fc1_bias,
    fc2_weight,
    fc2_bias,
):
    clip_count = clips.shape[0] // MICRO
    slot_order = clip_order[0]
    keep_mask = region_label[:, :, None] == region_label[:, None, :]
    rel_bias = jnp.take(bias_table.astype(jnp.float32), rel_index, axis=1)
    shard_set = (
        norm1_gain,
        norm1_bias,
        qkv_weight,
        qv_bias,
        proj_weight,
        proj_bias,
        norm2_gain,
        norm2_bias,
        fc1_weight,
        fc1_bias,
        fc2_weight,
        fc2_bias,
    )
    grad_sums = tuple((jnp.zeros(weight_shard.shape, jnp.float32) for weight_shard in shard_set))
    bias_sum = jnp.zeros(rel_bias.shape, jnp.float32)
    outputs = []
    source_grads = []
    for micro_index in range(MICRO):
        picked_slots = lax.dynamic_slice_in_dim(slot_order, micro_index * clip_count, clip_count)
        source = jnp.take(clips, picked_slots, axis=0)
        cot_block = out_grad[micro_index * clip_count : (micro_index + 1) * clip_count]
        full_weights = (
            lax.all_gather(norm1_gain, ("dp", "seq"), axis=0, tiled=True),
            lax.all_gather(norm1_bias, ("dp", "seq"), axis=0, tiled=True),
            lax.all_gather(qkv_weight, ("dp", "seq"), axis=0, tiled=True),
            lax.all_gather(qv_bias, ("dp", "seq"), axis=1, tiled=True),
            lax.all_gather(proj_weight, ("dp", "seq"), axis=0, tiled=True),
            lax.all_gather(proj_bias, ("dp", "seq"), axis=0, tiled=True),
            lax.all_gather(norm2_gain, ("dp", "seq"), axis=0, tiled=True),
            lax.all_gather(norm2_bias, ("dp", "seq"), axis=0, tiled=True),
            lax.all_gather(fc1_weight, ("dp", "seq"), axis=0, tiled=True),
            lax.all_gather(fc1_bias, ("dp", "seq"), axis=0, tiled=True),
            lax.all_gather(fc2_weight, ("dp", "seq"), axis=0, tiled=True),
            lax.all_gather(fc2_bias, ("dp", "seq"), axis=0, tiled=True),
        )
        output, grad_source, grad_terms, bias_term = layer_pass(
            source, cot_block, full_weights, rel_bias, keep_mask
        )
        grad_terms = (
            lax.psum_scatter(grad_terms[0], ("dp", "seq"), scatter_dimension=0, tiled=True),
            lax.psum_scatter(grad_terms[1], ("dp", "seq"), scatter_dimension=0, tiled=True),
            lax.psum_scatter(grad_terms[2], ("dp", "seq"), scatter_dimension=0, tiled=True),
            lax.psum_scatter(grad_terms[3], ("dp", "seq"), scatter_dimension=1, tiled=True),
            lax.psum_scatter(grad_terms[4], ("dp", "seq"), scatter_dimension=0, tiled=True),
            lax.psum_scatter(grad_terms[5], ("dp", "seq"), scatter_dimension=0, tiled=True),
            lax.psum_scatter(grad_terms[6], ("dp", "seq"), scatter_dimension=0, tiled=True),
            lax.psum_scatter(grad_terms[7], ("dp", "seq"), scatter_dimension=0, tiled=True),
            lax.psum_scatter(grad_terms[8], ("dp", "seq"), scatter_dimension=0, tiled=True),
            lax.psum_scatter(grad_terms[9], ("dp", "seq"), scatter_dimension=0, tiled=True),
            lax.psum_scatter(grad_terms[10], ("dp", "seq"), scatter_dimension=0, tiled=True),
            lax.psum_scatter(grad_terms[11], ("dp", "seq"), scatter_dimension=0, tiled=True),
        )
        grad_sums = tuple((previous + fresh for previous, fresh in zip(grad_sums, grad_terms)))
        bias_sum = bias_sum + bias_term
        outputs.append(output)
        source_grads.append(grad_source)
    flat_terms = bias_sum.reshape(bias_sum.shape[0], -1).T
    table_terms = jax.ops.segment_sum(flat_terms, rel_index.reshape(-1), num_segments=TBL).T
    table_grad = lax.psum(table_terms, "dp")
    output_all = jnp.concatenate(outputs, axis=0)
    clips_grad = jnp.zeros_like(clips).at[slot_order].set(jnp.concatenate(source_grads, axis=0))
    return (
        output_all,
        clips_grad,
        grad_sums[0],
        grad_sums[1],
        grad_sums[2],
        grad_sums[3],
        table_grad,
        grad_sums[4],
        grad_sums[5],
        grad_sums[6],
        grad_sums[7],
        grad_sums[8],
        grad_sums[9],
        grad_sums[10],
        grad_sums[11],
    )


EPS = 1e-5
LOG2E = math.log2(math.e)
LN2 = math.log(2.0)
SCALE = HD**-0.5
MASKED = -1e30
bf = jnp.bfloat16
f32 = jnp.float32
i32 = jnp.int32
MESH = pl.DeviceIdType.MESH
VM = pltpu.VMEM
DMA = pltpu.SemaphoreType.DMA

CL = 2
NS = 4
RP = 400
RT = CL * RP
KP = 512
C = 512
NHEAD = 16
TA = 10
TB = 256
SHARD = (16, 16, 16, 64)
WIDTH = (1536, 512, 2048, 512)
PARTS = ((0, 4), (4, 3))


def nn(a, b):
    return jnp.dot(a, b, preferred_element_type=f32)


def nt(a, b):
    return lax.dot_general(a, b, (((1,), (1,)), ((), ())), preferred_element_type=f32)


def tn(a, b):
    return lax.dot_general(a, b, (((0,), (0,)), ((), ())), preferred_element_type=f32)


def norm_parts(v):
    mu = jnp.mean(v, axis=-1, keepdims=True)
    c = v - mu
    r = lax.rsqrt(jnp.mean(c * c, axis=-1, keepdims=True) + EPS)
    return c * r, r


class Place:
    def __init__(self):
        dp, self.z = lax.axis_index("dp"), lax.axis_index("seq")
        self.dp = dp
        self.y, self.x, self.c = dp // 4, (dp // 2) % 2, dp % 2
        self.yn, self.xn, self.cn = 1 - self.y, 1 - self.x, 1 - self.c
        self.over_x = (self.dp_of(self.y, self.xn, self.c), self.z)
        self.over_y = (self.dp_of(self.yn, self.x, self.c), self.z)
        self.core = (self.dp_of(self.y, self.x, self.cn), self.z)
        self.block = dp * 4 + self.z

    def dp_of(self, y, x, c):
        return y * 4 + x * 2 + c

    def seq(self, z):
        return (self.dp, z)

    def far(self, d):
        return lax.rem(self.z + d, NS)

    def greet(self):
        bar = pltpu.get_barrier_semaphore()
        peers = [self.seq(self.far(d)) for d in (1, 2, 3)]
        peers += [self.over_x, self.over_y, self.core]
        for peer in peers:
            pl.semaphore_signal(bar, inc=1, device_id=peer, device_id_type=MESH)
        pl.semaphore_wait(bar, len(peers))


def rcopy(src, dst, ssem, rsem, dev):
    return pltpu.make_async_remote_copy(
        src_ref=src, dst_ref=dst, send_sem=ssem, recv_sem=rsem, device_id=dev, device_id_type=MESH
    )


def take(ref, sem):
    pltpu.make_async_copy(ref, ref, sem).wait()


def window_start(w, part):
    return lax.rem(7 * w + SHIFT_S + part, SIDE)


def send_windows(me, src, dst, ssem, rsem, lsem):
    slot = lax.rem(me.z + 2, NS)
    for d in range(NS):
        w = me.far(d)
        wy, wx = w // 2, lax.rem(w, 2)
        for c in range(CL):
            for y7, ny in PARTS:
                for x7, nx in PARTS:
                    a = src.at[c, pl.ds(window_start(wy, y7), ny), pl.ds(window_start(wx, x7), nx)]
                    b = dst.at[c, slot, pl.ds(y7, ny), pl.ds(x7, nx)]
                    if d == 0:
                        pltpu.make_async_copy(a, b, lsem).start()
                    else:
                        rcopy(a, b, ssem.at[d - 1], rsem.at[d - 1], me.seq(w)).start()


def take_windows(me, dst, ssem, rsem, lsem):
    for d in range(NS):
        slot = lax.rem(me.z + NS - d + 2, NS)
        if d == 0:
            take(dst.at[:, slot], lsem)
        else:
            take(dst.at[:, slot], rsem.at[d - 1])
            take(dst.at[:, slot], ssem.at[d - 1])


def send_home(me, src, dst, ssem, rsem, lsem):
    wy, wx = me.z // 2, lax.rem(me.z, 2)
    for d in range(NS):
        t = me.far(d)
        slot = lax.rem(t + 2, NS)
        for c in range(CL):
            for y7, ny in PARTS:
                for x7, nx in PARTS:
                    a = src.at[c, slot, pl.ds(y7, ny), pl.ds(x7, nx)]
                    b = dst.at[c, pl.ds(window_start(wy, y7), ny), pl.ds(window_start(wx, x7), nx)]
                    if d == 0:
                        pltpu.make_async_copy(a, b, lsem).start()
                    else:
                        rcopy(a, b, ssem.at[d - 1], rsem.at[d - 1], me.seq(t)).start()


def take_home(me, src, ssem, rsem, lsem):
    take(src.at[:, 0], lsem)
    for d in (1, 2, 3):
        take(src.at[:, 0], rsem.at[d - 1])
        take(src.at[:, 0], ssem.at[d - 1])


class Gather:
    def __init__(self, me, k, shard, full, ssem, rsem, lsem):
        self.me, self.shard, self.full = me, shard, full
        self.r = SHARD[k]
        self.ssem, self.rsem, self.lsem = ssem.at[k], rsem.at[k], lsem.at[k]

    def rows(self, dp, first=0, count=NS):
        return self.full.at[pl.ds(pl.multiple_of((dp * NS + first) * self.r, self.r), count * self.r)]

    def push(self, ref, slot, dev, count_slot=None):
        rcopy(ref, ref, self.ssem.at[slot if count_slot is None else count_slot], self.rsem.at[slot], dev).start()

    def start(self):
        me = self.me
        own = self.rows(me.dp, me.z, 1)
        pltpu.make_async_copy(self.shard, own, self.lsem).start()
        for d in (1, 2, 3):
            rcopy(self.shard, own, self.ssem.at[d - 1], self.rsem.at[d - 1], me.seq(me.far(d))).start()

    def plane(self):
        me = self.me
        take(self.rows(me.dp, me.z, 1), self.lsem)
        for d in (1, 2, 3):
            take(self.rows(me.dp, me.far(NS - d), 1), self.rsem.at[d - 1])
        mine = self.rows(me.dp)
        self.push(mine, 3, me.over_x)
        self.push(mine, 4, me.over_y)
        self.push(mine, 5, me.core)

    def diagonal(self):
        me = self.me
        dx, dy = me.over_x[0], me.over_y[0]
        take(self.rows(dx), self.rsem.at[3])
        self.push(self.rows(dx, 0, 2), 6, me.over_y)
        self.push(self.rows(dx), 8, me.core)
        take(self.rows(dy), self.rsem.at[4])
        self.push(self.rows(dy, 2, 2), 7, me.over_x)
        self.push(self.rows(dy), 9, me.core)

    def last(self):
        me = self.me
        dd = me.dp_of(me.yn, me.xn, me.c)
        take(self.rows(dd, 0, 2), self.rsem.at[6])
        take(self.rows(dd, 2, 2), self.rsem.at[7])
        self.push(self.rows(dd), 10, me.core)

    def finish(self):
        me = self.me
        for slot, (y, x) in ((5, (me.y, me.x)), (8, (me.y, me.xn)), (9, (me.yn, me.x)), (10, (me.yn, me.xn))):
            take(self.rows(me.dp_of(y, x, me.cn)), self.rsem.at[slot])
        one, two, four = self.rows(0, 0, 1), self.rows(0, 0, 2), self.rows(0)
        for slot in range(11):
            take(one if slot < 3 else two if slot in (6, 7) else four, self.ssem.at[slot])


class Vectors:
    def __init__(self, me, full, ssem, rsem):
        self.me, self.full, self.ssem, self.rsem = me, full, ssem, rsem

    def rows(self, dp, first=0, count=NS):
        return self.full.at[pl.ds(dp * NS + first, count)]

    def push(self, ref, slot, dev):
        rcopy(ref, ref, self.ssem.at[slot], self.rsem.at[slot], dev).start()

    def start(self):
        me = self.me
        for d in (1, 2, 3):
            self.push(self.rows(me.dp, me.z, 1), d - 1, me.seq(me.far(d)))

    def plane(self):
        me = self.me
        for d in (1, 2, 3):
            take(self.rows(me.dp, me.far(NS - d), 1), self.rsem.at[d - 1])
        for slot, dev in ((3, me.over_x), (4, me.over_y), (5, me.core)):
            self.push(self.rows(me.dp), slot, dev)

    def diagonal(self):
        me = self.me
        dx, dy = me.over_x[0], me.over_y[0]
        take(self.rows(dx), self.rsem.at[3])
        self.push(self.rows(dx), 6, me.over_y)
        self.push(self.rows(dx), 8, me.core)
        take(self.rows(dy), self.rsem.at[4])
        self.push(self.rows(dy), 9, me.core)

    def last(self):
        me = self.me
        dd = me.dp_of(me.yn, me.xn, me.c)
        take(self.rows(dd), self.rsem.at[6])
        self.push(self.rows(dd), 10, me.core)

    def finish(self):
        me = self.me
        for slot, (y, x) in ((5, (me.y, me.x)), (8, (me.y, me.xn)), (9, (me.yn, me.x)), (10, (me.yn, me.xn))):
            take(self.rows(me.dp_of(y, x, me.cn)), self.rsem.at[slot])
        for slot in (0, 1, 2, 3, 4, 5, 6, 8, 9, 10):
            take(self.rows(0, 0, 1) if slot < 3 else self.rows(0), self.ssem.at[slot])


def pack_vectors(me, sv, g1, b1, qv, pb, g2, b2, b3, b4):
    row = jnp.zeros((1, 256), f32)
    sv[pl.ds(me.block, 1), 0] = row
    pieces = (g1[...], b1[...], qv[0:1, :], qv[1:2, :], pb[...], g2[...], b2[...], b4[...])
    for k, piece in enumerate(pieces):
        sv[pl.ds(me.block, 1), 0, 16 * k : 16 * k + 16] = piece.astype(f32)
    sv[pl.ds(me.block, 1), 0, 128:192] = b3[...].astype(f32)


def spread_vectors(sv, vec):
    v = sv[...].reshape(32, 256).astype(bf)
    lane = lax.broadcasted_iota(i32, (256, C), 1)
    row = lax.broadcasted_iota(i32, (256, C), 0)
    blk = lax.broadcasted_iota(i32, (32, C), 0)
    col = lax.broadcasted_iota(i32, (32, C), 1)
    for k in range(12):
        if k < 8:
            pick, own = row == 16 * k + (lane & 15), blk == (col >> 4)
        else:
            pick, own = row == 128 + (lane & 63), blk == (col >> 6) + 8 * (k - 8)
        y = nn(v, jnp.where(pick, 1.0, 0.0).astype(bf))
        vec[k : k + 1, :] = jnp.sum(jnp.where(own, y, 0.0), axis=0, keepdims=True)


def one_hot(lo, i):
    d = jnp.broadcast_to(lo[pl.ds(i, 1), :], (16, KP)).astype(bf)
    d = d - lax.broadcasted_iota(i32, (16, KP), 0).astype(f32).astype(bf)
    one, zero = jnp.asarray(1, bf), jnp.asarray(0, bf)
    return jnp.concatenate([jnp.where(d == jnp.asarray(16 * c, bf), one, zero) for c in range(16)], axis=0)


def order_index(me, idx, lab, perm, hi, lo, colb, lrow):
    p = perm[...]
    iv = idx[...]
    for dst, part in ((hi, iv >> 8), (lo, iv & 255)):
        rows = nn(p[0:RP, :], part.astype(f32).astype(bf)).astype(bf)
        dst[...] = nt(rows, p)
    own = lab[pl.ds(me.z, 1), :].astype(f32)
    own = jnp.broadcast_to(own, (8, WT)).astype(bf)
    lane = lax.broadcasted_iota(i32, (8, KP), 1)
    lrow[...] = jnp.where(lane < WT, nt(own, p), -1.0)
    colb[...] = jnp.broadcast_to(nt(p[0:RP, :], own)[:, 0:1], (RP, 128))


def table_rows(tbl, tab):
    whole = jnp.concatenate([tbl[s] for s in range(NS)], axis=0)
    for a in range(TA):
        tab[a * 16 : (a + 1) * 16, :] = whole[:, a * TB : (a + 1) * TB].astype(bf)


def gather_rows(first, count, tab, hi, lo, colb, lrow, bias):
    unroll = 8

    def body(t, _):
        for u in range(unroll):
            i = first + t * unroll + u
            y = nn(tab[...], one_hot(lo, i))
            high = jnp.broadcast_to(hi[pl.ds(i, 1), :], (16, KP))
            acc = jnp.zeros((16, KP), f32)
            for a in range(TA):
                acc = jnp.where(high == a, y[a * 16 : (a + 1) * 16], acc)
            acc = acc * LOG2E
            own = colb[pl.ds(i, 1), :]
            r0 = pl.multiple_of(i * 16, 16)
            for j in range(4):
                keep = lrow[0:1, j * 128 : (j + 1) * 128] == own
                bias[j, pl.ds(r0, 16), :] = jnp.where(keep, acc[:, j * 128 : (j + 1) * 128], MASKED)
        return 0

    lax.fori_loop(0, count // unroll, body, 0)


def scatter_rows(first, count, g, hi, lo, total):
    unroll = 8
    zero = jnp.asarray(0, bf)

    def body(t, _):
        ls, rs = [], []
        for u in range(unroll):
            i = first + t * unroll + u
            rs.append(one_hot(lo, i))
            high = jnp.broadcast_to(hi[pl.ds(i, 1), :], (16, KP)).astype(bf)
            r0 = pl.multiple_of(i * 16, 16)
            own = jnp.concatenate([g[j, pl.ds(r0, 16), :] for j in range(4)], axis=1).astype(bf)
            ls.append(
                jnp.concatenate([jnp.where(high == jnp.asarray(a, bf), own, zero) for a in range(TA)], axis=0)
            )
        total[...] += nt(jnp.concatenate(ls, axis=1), jnp.concatenate(rs, axis=1))
        return 0

    lax.fori_loop(0, count // unroll, body, 0)


def front_kernel(
    clips, cot, sq, sp, s1, s2, g1, b1, qv, pb, g2, b2, b3, b4, table, lab, idx, perm,
    xw, dyw, wq, wp, w1, w2, vec, bias, hi, lo,
    sv, tbl, tab, colb, lrow,
    xs, xr, xl, ds_, dr, dl, ws, wr, wl, vs, vr, ts, tr,
):
    me = Place()
    me.greet()
    pack_vectors(me, sv, g1, b1, qv, pb, g2, b2, b3, b4)
    tbl[pl.ds(me.z, 1), :, 2432:2560] = jnp.zeros((1, 4, 128), f32)
    tbl[pl.ds(me.z, 1), :, 0:TBL] = table[...].astype(f32)[None]
    weights = [
        Gather(me, k, shard, full, ws, wr, wl)
        for k, (shard, full) in enumerate(((sq, wq), (sp, wp), (s1, w1), (s2, w2)))
    ]
    vectors = Vectors(me, sv, vs, vr)
    for d in (1, 2, 3):
        own = tbl.at[me.z]
        rcopy(own, own, ts.at[d - 1], tr.at[d - 1], me.seq(me.far(d))).start()
    vectors.start()
    weights[0].start()
    send_windows(me, clips, xw, xs, xr, xl)
    for k in (1, 2, 3):
        weights[k].start()
    send_windows(me, cot, dyw, ds_, dr, dl)
    order_index(me, idx, lab, perm, hi, lo, colb, lrow)
    for d in (1, 2, 3):
        take(tbl.at[0], tr.at[d - 1])
    table_rows(tbl, tab)

    def rows(k):
        gather_rows(k * 40, 40, tab, hi, lo, colb, lrow, bias)

    rows(0)
    vectors.plane()
    weights[0].plane()
    rows(1)
    vectors.diagonal()
    weights[0].diagonal()
    rows(2)
    vectors.last()
    weights[0].last()
    weights[1].plane()
    rows(3)
    weights[1].diagonal()
    weights[2].plane()
    rows(4)
    weights[1].last()
    rows(5)
    weights[2].diagonal()
    weights[3].plane()
    rows(6)
    rows(7)
    weights[2].last()
    weights[3].diagonal()
    rows(8)
    vectors.finish()
    spread_vectors(sv, vec)
    rows(9)
    weights[3].last()
    for k in range(4):
        weights[k].finish()
    take_windows(me, xw, xs, xr, xl)
    take_windows(me, dyw, ds_, dr, dl)
    for d in (1, 2, 3):
        take(tbl.at[0], ts.at[d - 1])


def load_tokens(src, clip, dst, p):
    for s in range(NS):
        v = src[clip, s].astype(f32).reshape(98, C)
        dst[p * RP + s * 98 : p * RP + (s + 1) * 98, :] = v.astype(dst.dtype)
    dst[p * RP + WT : (p + 1) * RP, :] = jnp.zeros((RP - WT, C), dst.dtype)


def store_tokens(src, clip, dst, slot):
    for s in range(NS):
        v = src[clip, s * 98 : (s + 1) * 98, :]
        dst[slot, s] = v.reshape(49, 2, C).astype(bf).reshape(7, 7, 2, C)


def qkv_phase(x, vec, wq, n1, q, k, v):
    for p in range(CL):
        k[p, RP:KP, :] = jnp.zeros((KP - RP, C), bf)
        v[p, RP:KP, :] = jnp.zeros((KP - RP, C), bf)

    def body(p, _):
        r0 = pl.multiple_of(p * RP, RP)
        n, _r = norm_parts(x[pl.ds(r0, RP), :].astype(f32))
        y = (n * vec[0:1, :] + vec[1:2, :]).astype(bf)
        n1[pl.ds(r0, RP), :] = y
        q[pl.ds(r0, RP), :] = ((nn(y, wq[:, 0:C]) + vec[2:3, :]) * (SCALE * LOG2E)).astype(bf)
        k[p, 0:RP, :] = nn(y, wq[:, C : 2 * C]).astype(bf)
        v[p, 0:RP, :] = (nn(y, wq[:, 2 * C : 3 * C]) + vec[3:4, :]).astype(bf)
        return 0

    lax.fori_loop(0, CL, body, 0)


def attention_forward(q, k, v, bias, e, att, inv):
    lane = lax.broadcasted_iota(i32, (1, 128), 1) // HD

    def body(quad, _):
        l0 = pl.multiple_of(quad * 128, 128)
        for p in range(CL):
            qq = q[p * RP : (p + 1) * RP, pl.ds(l0, 128)]
            kk = k[p, :, pl.ds(l0, 128)]
            vv = v[p, :, pl.ds(l0, 128)]
            acc = jnp.zeros((RP, 128), f32)
            ainv = acc
            for hq in range(4):
                h = quad * 4 + hq
                s = nt(qq, jnp.where(lane == hq, kk, jnp.zeros_like(kk)))
                s = s + jnp.concatenate([bias[j, pl.ds(h, RP, stride=16), :] for j in range(4)], axis=1)
                w = jnp.exp2(s - jnp.max(s, axis=1, keepdims=True)).astype(bf)
                e[p, h] = w
                o = nn(w, jnp.where(lane == hq, vv, jnp.ones_like(vv)))
                one = 1.0 / pltpu.roll(o, HD, 1)
                acc = jnp.where(lane == hq, o * one, acc)
                ainv = jnp.where(lane == hq, one, ainv)
            att[p * RP : (p + 1) * RP, pl.ds(l0, 128)] = acc.astype(bf)
            inv[p * RP : (p + 1) * RP, pl.ds(l0, 128)] = ainv
        return 0

    lax.fori_loop(0, 4, body, 0)


def feed_forward(x, dy, att, vec, wp, w1, w2, nm, mid, acc, out, gvec):
    for p in range(CL):
        r = slice(p * RP, (p + 1) * RP)
        m = x[r, :].astype(f32) + nn(att[r, :], wp[...]) + vec[4:5, :]
        mid[r, :] = m
        n, _ = norm_parts(m)
        nm[r, :] = (n * vec[5:6, :] + vec[6:7, :]).astype(bf)
        out[p] = m + vec[7:8, :]
    acc[...] = jnp.zeros_like(acc)
    gvec[7:8, :] = jnp.sum(dy[...].astype(f32), axis=0, keepdims=True)
    nmt = nm[...].T
    dyv = dy[...]

    def body(c, _):
        c0 = pl.multiple_of(c * C, C)
        hid = nn(nm[...], w1[:, pl.ds(c0, C)]) + vec[pl.ds(8 + c, 1), :]
        density = jnp.exp2(hid * hid * (-0.5 * LOG2E)) * (1 / math.sqrt(2 * math.pi))
        phi = 0.5 * (1.0 + lax.erf(hid * (1 / math.sqrt(2.0))))
        act = (hid * phi).astype(bf)
        slope = phi + hid * density
        y = nn(act, w2[pl.ds(c0, C), :])
        for p in range(CL):
            out[p] += y[p * RP : (p + 1) * RP]
        dh = (nt(dyv, w2[pl.ds(c0, C), :]) * slope).astype(bf)
        gvec[pl.ds(8 + c, 1), :] = jnp.sum(dh.astype(f32), axis=0, keepdims=True)
        acc[...] += nt(dh, w1[:, pl.ds(c0, C)])
        w2[pl.ds(c0, C), :] = tn(act, dyv).astype(bf)
        w1[:, pl.ds(c0, C)] = nn(nmt, dh).astype(bf)
        return 0

    lax.fori_loop(0, 4, body, 0)


def middle_backward(dy, att, vec, wp, mid, acc, inv, gvec, do, dot):
    s4 = s5 = s6 = jnp.zeros((1, C), f32)
    parts = []
    for p in range(CL):
        r = slice(p * RP, (p + 1) * RP)
        n, rr = norm_parts(mid[r, :])
        gmn = acc[r, :]
        s5 += jnp.sum(gmn * n, axis=0, keepdims=True)
        s6 += jnp.sum(gmn, axis=0, keepdims=True)
        g = gmn * vec[5:6, :]
        gm = dy[r, :].astype(f32) + rr * (
            g - jnp.mean(g, axis=-1, keepdims=True) - n * jnp.mean(g * n, axis=-1, keepdims=True)
        )
        mid[r, :] = gm
        gb = gm.astype(bf)
        s4 += jnp.sum(gb.astype(f32), axis=0, keepdims=True)
        parts.append(gb)
        low = (nt(gb, wp[...]) * inv[r, :]).astype(bf)
        do[r, :] = low
        acc[r, :] = low.astype(f32) * att[r, :].astype(f32)
        dot[p] = low.T
    gvec[4:5, :] = s4
    gvec[5:6, :] = s5
    gvec[6:7, :] = s6
    wp[...] = tn(att[...], jnp.concatenate(parts, axis=0)).astype(bf)


def attention_backward(q, k, v, e, do, dot, prod, qt, g, dq, dkt, dvt):
    lane = lax.broadcasted_iota(i32, (1, 128), 1) // HD
    for p in range(CL):
        qt[p] = q[p * RP : (p + 1) * RP, :].T

    def body(quad, _):
        l0 = pl.multiple_of(quad * 128, 128)
        dqs = [jnp.zeros((RP, 128), f32) for _ in range(CL)]
        for hq in range(4):
            h = quad * 4 + hq
            f0 = pl.multiple_of(h * HD, HD)
            both = None
            for p in range(CL):
                r = slice(p * RP, (p + 1) * RP)
                kk = k[p, :, pl.ds(l0, 128)]
                vv = v[p, :, pl.ds(l0, 128)]
                dp = nt(do[r, pl.ds(l0, 128)], jnp.where(lane == hq, vv, jnp.zeros_like(vv)))
                inner = jnp.sum(jnp.where(lane == hq, prod[r, pl.ds(l0, 128)], 0.0), axis=1, keepdims=True)
                w = e[p, h]
                ds = w.astype(f32) * (dp - inner)
                both = ds if both is None else both + ds
                low = ds.astype(bf)
                dqs[p] = dqs[p] + nn(low, jnp.where(lane == hq, kk, jnp.zeros_like(kk)))
                dkt[p, pl.ds(f0, HD), :] = (nn(qt[p, pl.ds(f0, HD), :], low) * LN2).astype(bf)
                dvt[p, pl.ds(f0, HD), :] = nn(dot[p, pl.ds(f0, HD), :], w).astype(bf)
            for j in range(4):
                g[j, pl.ds(h, RP, stride=16), :] = both[:, j * 128 : (j + 1) * 128]
        for p in range(CL):
            dq[p * RP : (p + 1) * RP, pl.ds(l0, 128)] = (dqs[p] * SCALE).astype(bf)
        return 0

    lax.fori_loop(0, 4, body, 0)


def input_backward(x, n1, vec, wq, dq, dkt, dvt, dk, dv, mid, dx, gvec):
    s0 = s1 = jnp.zeros((1, C), f32)
    for p in range(CL):
        r = slice(p * RP, (p + 1) * RP)
        dk[r, :] = dkt[p].T[0:RP, :]
        dv[r, :] = dvt[p].T[0:RP, :]
    gvec[2:3, :] = jnp.sum(dq[...].astype(f32), axis=0, keepdims=True)
    gvec[3:4, :] = jnp.sum(dv[...].astype(f32), axis=0, keepdims=True)
    for p in range(CL):
        r = slice(p * RP, (p + 1) * RP)
        gn = nt(dq[r, :], wq[:, 0:C]) + nt(dk[r, :], wq[:, C : 2 * C]) + nt(dv[r, :], wq[:, 2 * C : 3 * C])
        n, rr = norm_parts(x[r, :].astype(f32))
        s0 += jnp.sum(gn * n, axis=0, keepdims=True)
        s1 += jnp.sum(gn, axis=0, keepdims=True)
        g = gn * vec[0:1, :]
        dx[p] = mid[r, :] + rr * (
            g - jnp.mean(g, axis=-1, keepdims=True) - n * jnp.mean(g * n, axis=-1, keepdims=True)
        )
    gvec[0:1, :] = s0
    gvec[1:2, :] = s1
    n1t = n1[...].T
    wq[:, 0:C] = nn(n1t, dq[...]).astype(bf)
    wq[:, C : 2 * C] = nn(n1t, dk[...]).astype(bf)
    wq[:, 2 * C : 3 * C] = nn(n1t, dv[...]).astype(bf)


def main_kernel(
    order, xw_in, dyw_in, wq_in, wp_in, w1_in, w2_in, vec, bias_in,
    outw_out, dxw_out, gq_out, gp_out, g1_out, g2_out, gvec, g_out,
    bg, e, wq, wp, w1, w2, xw, dyw, x, dy, n1, q, k, v, att, inv, nm, mid, acc, out, do, qt, dot, dkt, dvt, sem,
):
    ins = [
        pltpu.make_async_copy(a, b, sem.at[n])
        for n, (a, b) in enumerate(
            ((xw_in, xw), (wq_in, wq), (bias_in, bg), (dyw_in, dyw), (wp_in, wp), (w1_in, w1), (w2_in, w2))
        )
    ]
    for copy in ins:
        copy.start()
    gvec[...] = jnp.zeros_like(gvec)
    ins[0].wait()
    for p in range(CL):
        load_tokens(xw, p, x, p)
    ins[1].wait()
    qkv_phase(x, vec, wq, n1, q, k, v)
    ins[2].wait()
    attention_forward(q, k, v, bg, e, att, inv)
    for copy in ins[3:]:
        copy.wait()
    for p in range(CL):
        load_tokens(dyw, order[0, p], dy, p)
    feed_forward(x, dy, att, vec, wp, w1, w2, nm, mid, acc, out, gvec)
    for p in range(CL):
        store_tokens(out, order[0, p], xw, p)
    outs = [
        pltpu.make_async_copy(a, b, sem.at[7 + n])
        for n, (a, b) in enumerate(
            ((xw, outw_out), (w1, g1_out), (w2, g2_out), (wp, gp_out), (bg, g_out), (wq, gq_out), (dyw, dxw_out))
        )
    ]
    for copy in outs[0:3]:
        copy.start()
    middle_backward(dy, att, vec, wp, mid, acc, inv, gvec, do, dot)
    outs[3].start()
    attention_backward(q, k, v, e, do, dot, acc, qt, bg, nm, dkt, dvt)
    outs[4].start()
    input_backward(x, n1, vec, wq, nm, dkt, dvt, att, do, mid, out, gvec)
    outs[5].start()
    for p in range(CL):
        store_tokens(out, p, dyw, p)
    outs[6].start()
    for copy in outs:
        copy.wait()


class Reduce:
    def __init__(self, me, k, grad, out, sems, rc, s1, rx, ry, t, ra, s2, rz):
        self.me, self.k, self.grad, self.out = me, k, grad, out
        self.u = 4 * SHARD[k]
        self.h = self.u // 2
        self.ssem, self.rsem = sems[0].at[k], sems[1].at[k]
        self.rc, self.s1, self.rx, self.ry, self.t, self.ra, self.s2, self.rz = rc, s1, rx, ry, t, ra, s2, rz

    def at(self, ref, n, unit, first=0, count=None):
        return ref.at[pl.ds(pl.multiple_of(n * unit + first, 16), unit if count is None else count)]

    def val(self, ref, n, unit, first=0, count=None):
        return ref[pl.ds(pl.multiple_of(n * unit + first, 16), unit if count is None else count), :].astype(f32)

    def cores(self):
        me, u = self.me, self.u
        for g in range(4):
            rcopy(
                self.at(self.grad, g * 2 + me.cn, u), self.at(self.rc, g, u),
                self.ssem.at[g], self.rsem.at[g], me.core,
            ).start()

    def plane(self):
        me, u, h = self.me, self.u, self.h
        for g in range(4):
            take(self.at(self.rc, g, u), self.rsem.at[g])
            total = self.val(self.grad, g * 2 + me.c, u) + self.val(self.rc, g, u)
            self.s1[g * u : (g + 1) * u, :] = total.astype(bf)
        for n in range(2):
            rcopy(
                self.at(self.s1, n * 2 + me.xn, u, 0, h), self.at(self.rx, n, h),
                self.ssem.at[4 + n], self.rsem.at[4 + n], me.over_x,
            ).start()
            rcopy(
                self.at(self.s1, me.yn * 2 + n, u, h, h), self.at(self.ry, n, h),
                self.ssem.at[6 + n], self.rsem.at[6 + n], me.over_y,
            ).start()

    def diagonal(self):
        me, u, h = self.me, self.u, self.h
        for n in range(2):
            take(self.at(self.rx, n, h), self.rsem.at[4 + n])
            total = self.val(self.s1, n * 2 + me.x, u, 0, h) + self.val(self.rx, n, h)
            self.t[n * h : (n + 1) * h, :] = total.astype(bf)
            take(self.at(self.ry, n, h), self.rsem.at[6 + n])
            total = self.val(self.s1, me.y * 2 + n, u, h, h) + self.val(self.ry, n, h)
            self.t[(2 + n) * h : (3 + n) * h, :] = total.astype(bf)
        rcopy(
            self.at(self.t, me.yn, h), self.at(self.ra, 0, h), self.ssem.at[8], self.rsem.at[8], me.over_y
        ).start()
        rcopy(
            self.at(self.t, 2 + me.xn, h), self.at(self.ra, 1, h), self.ssem.at[9], self.rsem.at[9], me.over_x
        ).start()

    def line(self):
        me, h, r = self.me, self.h, SHARD[self.k]
        for n, own in enumerate((me.y, 2 + me.x)):
            take(self.at(self.ra, n, h), self.rsem.at[8 + n])
            total = self.val(self.t, own, h) + self.val(self.ra, n, h)
            self.s2[n * h : (n + 1) * h, :] = total.astype(bf)
        for d in (1, 2, 3):
            z = me.far(d)
            rcopy(
                self.at(self.s2, z, r), self.at(self.rz, d - 1, r),
                self.ssem.at[9 + d], self.rsem.at[9 + d], me.seq(z),
            ).start()

    def finish(self):
        me, r, u, h = self.me, SHARD[self.k], self.u, self.h
        total = self.val(self.s2, me.z, r)
        for d in (1, 2, 3):
            take(self.at(self.rz, d - 1, r), self.rsem.at[9 + d])
            total = total + self.val(self.rz, d - 1, r)
        self.out[...] = total
        for slot in range(13):
            count = u if slot < 4 else h if slot < 10 else r
            take(self.at(self.grad, 0, count), self.ssem.at[slot])


def tail_kernel(
    outw, dxw, gq, gp, g1, g2, gvec, g, hi, lo,
    out_t, dx_t, oq, op, o1, o2, og1, ob1, oqv, opb, og2, ob2, ob3, ob4, otab,
    *scr,
):
    grads, outs = (gq, gp, g1, g2), (oq, op, o1, o2)
    bufs = [scr[8 * k : 8 * (k + 1)] for k in range(4)]
    total, mine, tz, tx, vz, vx, ss, rs, os_, or_, ol, xs, xr, xl, zs, zr, es, er = scr[32:]
    me = Place()
    me.greet()
    send_home(me, outw, out_t, os_, or_, ol)
    send_home(me, dxw, dx_t, xs, xr, xl)
    reds = [Reduce(me, k, grads[k], outs[k], (ss, rs), *bufs[k]) for k in range(4)]
    total[...] = jnp.zeros_like(total)

    def rows(n):
        scatter_rows(n * 40, 40, g, hi, lo, total)

    for k in (2, 3, 1, 0):
        reds[k].cores()
    for d in (1, 2, 3):
        rcopy(gvec, vz.at[d - 1], zs.at[d - 1], zr.at[d - 1], me.seq(me.far(d))).start()
    rows(0)
    reds[2].plane()
    rows(1)
    reds[3].plane()
    rows(2)
    reds[1].plane()
    reds[0].plane()
    rows(3)
    reds[2].diagonal()
    rows(4)
    rows(5)
    reds[3].diagonal()
    reds[2].line()
    rows(6)
    rows(7)
    reds[1].diagonal()
    reds[0].diagonal()
    reds[3].line()
    rows(8)
    rows(9)
    reds[1].line()
    reds[0].line()
    for a in range(TA):
        for s in range(NS):
            mine[s, :, a * TB : (a + 1) * TB] = total[a * 16 + 4 * s : a * 16 + 4 * s + 4, :]
    for d in (1, 2, 3):
        rcopy(
            mine.at[me.far(d)], tz.at[d - 1], zs.at[2 + d], zr.at[2 + d], me.seq(me.far(d))
        ).start()
    table = mine[pl.ds(me.z, 1)].reshape(4, TA * TB)
    vecs = gvec[...]
    for d in (1, 2, 3):
        take(vz.at[d - 1], zr.at[d - 1])
        vecs = vecs + vz[d - 1]
    for d in (1, 2, 3):
        take(tz.at[d - 1], zr.at[2 + d])
        table = table + tz[d - 1]
    for n, dev in enumerate((me.core, me.over_x, me.over_y)):
        tx[2 * n] = table
        vx[2 * n] = vecs
        rcopy(tx.at[2 * n], tx.at[2 * n + 1], es.at[2 * n], er.at[2 * n], dev).start()
        rcopy(vx.at[2 * n], vx.at[2 * n + 1], es.at[2 * n + 1], er.at[2 * n + 1], dev).start()
        take(tx.at[2 * n + 1], er.at[2 * n])
        take(vx.at[2 * n + 1], er.at[2 * n + 1])
        table = table + tx[2 * n + 1]
        vecs = vecs + vx[2 * n + 1]
    otab[...] = table
    vx[6] = vecs
    part = pltpu.roll(vecs[0:8, :], C - me.block * 16, 1)
    for row, ref in ((0, og1), (1, ob1), (4, opb), (5, og2), (6, ob2), (7, ob4)):
        ref[...] = part[row : row + 1, 0:16]
    oqv[...] = part[2:4, 0:16]
    wide = vx[6, pl.ds(8 + me.block // 8, 1), :]
    wide = jnp.broadcast_to(wide, (8, C))
    ob3[...] = pltpu.roll(wide, C - lax.rem(me.block, 8) * 64, 1)[0:1, 0:64]
    for k in (2, 3, 1, 0):
        reds[k].finish()
    for n in range(3):
        take(tx.at[0], es.at[2 * n])
        take(vx.at[0], es.at[2 * n + 1])
        take(vz.at[0], zs.at[n])
        take(tz.at[0], zs.at[3 + n])
    take_home(me, outw, os_, or_, ol)
    take_home(me, dxw, xs, xr, xl)


def call(kernel, outs, ins, out_spaces, in_spaces, scratch, remote=None, args=()):
    def spec(space):
        return pl.BlockSpec(memory_space=space)

    params = dict(vmem_limit_bytes=62 * 1024 * 1024)
    if remote is not None:
        params.update(collective_id=remote, has_side_effects=True)
    return pl.pallas_call(
        kernel,
        out_shape=[jax.ShapeDtypeStruct(s, d) for s, d in outs],
        in_specs=[spec(s) for s in in_spaces],
        out_specs=[spec(s) for s in out_spaces],
        scratch_shapes=scratch,
        compiler_params=pltpu.CompilerParams(**params),
    )(*args)


def windowed(
    clips, out_grad, clip_order, region_label, rel_index, norm1_gain, norm1_bias, qkv_weight, qv_bias,
    bias_table, proj_weight, proj_bias, norm2_gain, norm2_bias, fc1_weight, fc1_bias, fc2_weight, fc2_bias,
):
    any_, vm = pl.ANY, VM
    at = np.arange(WT)
    canonical = (2 * (at // 98) + at % 2) * 49 + (at % 98) // 2
    perm = np.zeros((KP, WT), np.float32)
    perm[at, canonical] = 1
    perm = jnp.asarray(perm, bf)
    field = lambda a: jnp.transpose(a, (0, 2, 3, 1, 4))
    row = lambda a: a.reshape(1, -1)
    win = (CL, NS, 7, 7, 2, C)
    whole = ((C, 1536), (C, C), (C, 2048), (2048, C))
    bias_shape = (4, RP * 16, 128)
    xw, dyw, wq, wp, w1, w2, vec, bias, hi, lo = call(
        front_kernel,
        [(win, bf), (win, bf), *((s, bf) for s in whole), ((16, C), f32), (bias_shape, f32), ((RP, KP), f32), ((RP, KP), f32)],
        None,
        [any_] * 6 + [vm] * 4,
        [any_] * 6 + [vm] * 12,
        [
            VM((32, 1, 256), f32), VM((NS, 4, TA * TB), f32), VM((160, TB), bf), VM((RP, 128), f32), VM((8, KP), f32),
            DMA((3,)), DMA((3,)), DMA, DMA((3,)), DMA((3,)), DMA,
            DMA((4, 11)), DMA((4, 11)), DMA((4,)), DMA((11,)), DMA((11,)), DMA((3,)), DMA((3,)),
        ],
        0,
        (
            field(clips), field(out_grad), qkv_weight, proj_weight, fc1_weight, fc2_weight,
            row(norm1_gain), row(norm1_bias), qv_bias, row(proj_bias), row(norm2_gain), row(norm2_bias),
            row(fc1_bias), row(fc2_bias), bias_table, region_label, rel_index, perm,
        ),
    )
    rows = (RT, C)
    outw, dxw, gq, gp, g1, g2, gvec, g = call(
        main_kernel,
        [(win, bf), (win, bf), *((s, bf) for s in whole), ((16, C), f32), (bias_shape, f32)],
        None,
        [any_] * 6 + [vm, any_],
        [pltpu.SMEM] + [any_] * 6 + [vm, any_],
        [
            VM(bias_shape, f32), VM((CL, NHEAD, RP, KP), bf), *(VM(s, bf) for s in whole), VM(win, bf), VM(win, bf),
            VM(rows, bf), VM(rows, bf), VM(rows, bf), VM(rows, bf), VM((CL, KP, C), bf), VM((CL, KP, C), bf),
            VM(rows, bf), VM(rows, f32), VM(rows, bf), VM(rows, f32), VM(rows, f32), VM((CL, RP, C), f32), VM(rows, bf),
            VM((CL, C, RP), bf), VM((CL, C, RP), bf), VM((CL, C, KP), bf), VM((CL, C, KP), bf), DMA((14,)),
        ],
        None,
        (clip_order, xw, dyw, wq, wp, w1, w2, vec, bias),
    )
    scratch = []
    for r, w in zip(SHARD, WIDTH):
        u = 4 * r
        for n in (4 * u, 4 * u, u, u, 2 * u, u, u, 3 * r):
            scratch.append(VM((n, w), bf))
    field_shape = (CL, SIDE, SIDE, 2, C)
    out_t, dx_t, oq, op, o1, o2, og1, ob1, oqv, opb, og2, ob2, ob3, ob4, otab = call(
        tail_kernel,
        [
            (field_shape, bf), (field_shape, bf), *(((r, w), f32) for r, w in zip(SHARD, WIDTH)),
            ((1, 16), f32), ((1, 16), f32), ((2, 16), f32), ((1, 16), f32), ((1, 16), f32), ((1, 16), f32), ((1, 64), f32),
            ((1, 16), f32), ((4, TA * TB), f32),
        ],
        None,
        [any_] * 2 + [vm] * 13,
        [any_] * 2 + [vm] * 8,
        scratch + [
            VM((160, TB), f32), VM((NS, 4, TA * TB), f32), VM((3, 4, TA * TB), f32), VM((6, 4, TA * TB), f32),
            VM((3, 16, C), f32), VM((7, 16, C), f32),
            DMA((4, 13)), DMA((4, 13)), DMA((3,)), DMA((3,)), DMA, DMA((3,)), DMA((3,)), DMA, DMA((6,)), DMA((6,)),
            DMA((6,)), DMA((6,)),
        ],
        1,
        (outw, dxw, gq, gp, g1, g2, gvec, g, hi, lo),
    )
    back = lambda a: jnp.transpose(a, (0, 3, 1, 2, 4))
    flat = lambda a: a.reshape(-1)
    return (
        back(out_t), back(dx_t), flat(og1), flat(ob1), oq, oqv, otab[:, :TBL], op, flat(opb), flat(og2), flat(ob2),
        o1, flat(ob3), o2, flat(ob4),
    )


def solution(mesh):
    in_specs = (
        P("dp", "seq", None, None, None),
        P("dp", "seq", None, None, None),
        P("dp", None),
        P(),
        P(),
        P(("dp", "seq")),
        P(("dp", "seq")),
        P(("dp", "seq"), None),
        P(None, ("dp", "seq")),
        P("seq", None),
        P(("dp", "seq"), None),
        P(("dp", "seq")),
        P(("dp", "seq")),
        P(("dp", "seq")),
        P(("dp", "seq"), None),
        P(("dp", "seq")),
        P(("dp", "seq"), None),
        P(("dp", "seq")),
    )
    out_specs = (
        P("dp", "seq", None, None, None),
        P("dp", "seq", None, None, None),
        P(("dp", "seq")),
        P(("dp", "seq")),
        P(("dp", "seq"), None),
        P(None, ("dp", "seq")),
        P("seq", None),
        P(("dp", "seq"), None),
        P(("dp", "seq")),
        P(("dp", "seq")),
        P(("dp", "seq")),
        P(("dp", "seq"), None),
        P(("dp", "seq")),
        P(("dp", "seq"), None),
        P(("dp", "seq")),
    )
    local = windowed if mesh.shape["dp"] == 8 and mesh.shape["seq"] == NS else shards
    return jax.shard_map(local, mesh=mesh, in_specs=in_specs, out_specs=out_specs, check_vma=False)
```

```python
import functools
import math

import jax
import jax.numpy as jnp
import numpy as np
from jax import lax
from jax.experimental import pallas as pl
from jax.experimental.pallas import tpu as pltpu
from jax.sharding import PartitionSpec as P

HD = 32
WIN_T = 8
WIN_S = 7
SHIFT_T = 4
SHIFT_S = 3
FR = 8
SIDE = 14
MICRO = 2
NWIN = 4
WT = 392
TBL = 2535


eps_norm = 1e-05


def layer_norm(values, norm_gain, norm_shift):
    average = jnp.mean(values, axis=-1, keepdims=True)
    centred = values - average
    variance = jnp.mean(centred * centred, axis=-1, keepdims=True)
    return centred * lax.rsqrt(variance + eps_norm) * norm_gain + norm_shift


def gelu_exact(values):
    return jax.nn.gelu(values, approximate=False)


def matmul(left_side, right_side):
    return jnp.dot(left_side, right_side, preferred_element_type=jnp.float32)


def window_split(field):
    rolled = jnp.roll(field, (-SHIFT_T, -SHIFT_S, -SHIFT_S), (0, 1, 2))
    blocks = rolled.reshape(FR // WIN_T, WIN_T, SIDE // WIN_S, WIN_S, SIDE // WIN_S, WIN_S, -1)
    return blocks.transpose(0, 2, 4, 1, 3, 5, 6).reshape(NWIN, WT, -1)


def window_merge(windows):
    blocks = windows.reshape(FR // WIN_T, SIDE // WIN_S, SIDE // WIN_S, WIN_T, WIN_S, WIN_S, -1)
    field = blocks.transpose(0, 3, 1, 4, 2, 5, 6).reshape(FR, SIDE, SIDE, -1)
    return jnp.roll(field, (SHIFT_T, SHIFT_S, SHIFT_S), (0, 1, 2))


def to_heads(field_rows):
    feature_count = field_rows.shape[-1]
    windows = window_split(field_rows.reshape(FR, SIDE, SIDE, feature_count))
    return windows.reshape(NWIN, WT, feature_count // HD, HD)


def from_heads(windows):
    feature_count = windows.shape[-1] * windows.shape[-2]
    merged = window_merge(windows.reshape(NWIN, WT, feature_count))
    return merged.reshape(-1, feature_count)


def window_scores(query_win, key_win, rel_bias, keep_mask):
    scores = jnp.einsum("wihd,wjhd->whij", query_win, key_win, preferred_element_type=jnp.float32)
    scores = scores * HD ** (-0.5) + rel_bias[None]
    return jnp.where(keep_mask[:, None], scores, -1e30)


def attend_clip(query_rows, key_rows, value_rows, rel_bias, keep_mask):
    scores = window_scores(to_heads(query_rows), to_heads(key_rows), rel_bias, keep_mask)
    row_max = jnp.max(scores, axis=-1, keepdims=True)
    exponent = jnp.exp(scores - row_max)
    row_total = jnp.sum(exponent, axis=-1, keepdims=True)
    probabilities = (exponent / row_total).astype(jnp.bfloat16)
    attended = jnp.einsum(
        "whij,wjhd->wihd", probabilities, to_heads(value_rows), preferred_element_type=jnp.float32
    ).astype(jnp.bfloat16)
    return (from_heads(attended), (row_max + jnp.log(row_total))[..., 0])


def attend_back(query_rows, key_rows, value_rows, grad_rows, log_total, rel_bias, keep_mask):
    query_win = to_heads(query_rows)
    key_win = to_heads(key_rows)
    value_win = to_heads(value_rows)
    grad_win = to_heads(grad_rows)
    scores = window_scores(query_win, key_win, rel_bias, keep_mask)
    probabilities = jnp.exp(scores - log_total[..., None])
    grad_probs = jnp.einsum(
        "wihd,wjhd->whij", grad_win, value_win, preferred_element_type=jnp.float32
    )
    row_inner = jnp.sum(probabilities * grad_probs, axis=-1, keepdims=True)
    grad_scores = (probabilities * (grad_probs - row_inner)).astype(jnp.bfloat16)
    score_scale = HD ** (-0.5)
    grad_query = (
        jnp.einsum("whij,wjhd->wihd", grad_scores, key_win, preferred_element_type=jnp.float32)
        * score_scale
    )
    grad_key = (
        jnp.einsum("whij,wihd->wjhd", grad_scores, query_win, preferred_element_type=jnp.float32)
        * score_scale
    )
    grad_value = jnp.einsum(
        "whij,wihd->wjhd",
        probabilities.astype(jnp.bfloat16),
        grad_win,
        preferred_element_type=jnp.float32,
    )
    bias_term = jnp.sum(grad_scores.astype(jnp.float32), axis=0)
    return (
        from_heads(grad_query).astype(jnp.bfloat16),
        from_heads(grad_key).astype(jnp.bfloat16),
        from_heads(grad_value).astype(jnp.bfloat16),
        bias_term,
    )


def layer_pass(source, cot_block, full_weights, rel_bias, keep_mask):
    (
        norm_in_gain,
        norm_in_shift,
        qkv_w,
        qv_b,
        proj_w,
        proj_b,
        norm_mid_gain,
        norm_mid_shift,
        fc1_w,
        fc1_b,
        fc2_w,
        fc2_b,
    ) = full_weights
    clip_count = source.shape[0]
    model_width = source.shape[-1]
    shaped = (clip_count, -1, model_width)
    token_rows = source.reshape(-1, model_width).astype(jnp.float32)
    normed, norm_in_back = jax.vjp(
        layer_norm, token_rows, norm_in_gain.astype(jnp.float32), norm_in_shift.astype(jnp.float32)
    )
    normed_low = normed.astype(jnp.bfloat16)
    projected = matmul(normed_low, qkv_w)
    qv_float = qv_b.astype(jnp.float32)
    query_rows = (projected[:, :model_width] + qv_float[0]).astype(jnp.bfloat16)
    key_rows = projected[:, model_width : 2 * model_width].astype(jnp.bfloat16)
    value_rows = (projected[:, 2 * model_width :] + qv_float[1]).astype(jnp.bfloat16)
    parts = (
        lax.all_to_all(query_rows.reshape(shaped), "seq", split_axis=2, concat_axis=1, tiled=True),
        lax.all_to_all(key_rows.reshape(shaped), "seq", split_axis=2, concat_axis=1, tiled=True),
        lax.all_to_all(value_rows.reshape(shaped), "seq", split_axis=2, concat_axis=1, tiled=True),
    )
    merged_heads, log_total = lax.map(
        lambda clip_parts: attend_clip(*clip_parts, rel_bias, keep_mask), parts
    )
    attended_heads, log_total, query_heads, key_heads, value_heads = (
        merged_heads,
        log_total,
        parts[0],
        parts[1],
        parts[2],
    )
    attended = lax.all_to_all(
        attended_heads, "seq", split_axis=1, concat_axis=2, tiled=True
    ).reshape(-1, model_width)
    branch = matmul(attended, proj_w) + proj_b.astype(jnp.float32)
    middle = token_rows + branch
    normed_mid, norm_mid_back = jax.vjp(
        layer_norm, middle, norm_mid_gain.astype(jnp.float32), norm_mid_shift.astype(jnp.float32)
    )
    normed_mid_low = normed_mid.astype(jnp.bfloat16)
    hidden = matmul(normed_mid_low, fc1_w) + fc1_b.astype(jnp.float32)
    active, gelu_back = jax.vjp(gelu_exact, hidden)
    active_low = active.astype(jnp.bfloat16)
    result = matmul(active_low, fc2_w) + fc2_b.astype(jnp.float32)
    output = (middle + result).astype(jnp.bfloat16).reshape(source.shape)
    grad_low = cot_block.reshape(-1, model_width)
    grad_float = grad_low.astype(jnp.float32)
    grad_fc2_w = matmul(active_low.T, grad_low)
    grad_fc2_b = jnp.sum(grad_float, axis=0)
    grad_active = matmul(grad_low, fc2_w.T)
    grad_hidden = gelu_back(grad_active)[0].astype(jnp.bfloat16)
    grad_fc1_w = matmul(normed_mid_low.T, grad_hidden)
    grad_fc1_b = jnp.sum(grad_hidden.astype(jnp.float32), axis=0)
    grad_normed_mid = matmul(grad_hidden, fc1_w.T)
    grad_mid_part, grad_mid_gain, grad_mid_shift = norm_mid_back(grad_normed_mid)
    grad_middle = grad_float + grad_mid_part
    grad_branch = grad_middle.astype(jnp.bfloat16)
    grad_proj_w = matmul(attended.T, grad_branch)
    grad_proj_b = jnp.sum(grad_branch.astype(jnp.float32), axis=0)
    grad_attended = matmul(grad_branch, proj_w.T).astype(jnp.bfloat16)
    grad_heads = lax.all_to_all(
        grad_attended.reshape(shaped), "seq", split_axis=2, concat_axis=1, tiled=True
    )
    grad_query, grad_key, grad_value, bias_terms = lax.map(
        lambda clip_parts: attend_back(*clip_parts, rel_bias, keep_mask),
        (query_heads, key_heads, value_heads, grad_heads, log_total),
    )
    grad_query, grad_key, grad_value = (
        lax.all_to_all(grad_query, "seq", split_axis=1, concat_axis=2, tiled=True),
        lax.all_to_all(grad_key, "seq", split_axis=1, concat_axis=2, tiled=True),
        lax.all_to_all(grad_value, "seq", split_axis=1, concat_axis=2, tiled=True),
    )
    grad_query = grad_query.reshape(-1, model_width)
    grad_value = grad_value.reshape(-1, model_width)
    grad_projected = jnp.concatenate(
        [grad_query, grad_key.reshape(-1, model_width), grad_value], axis=1
    )
    grad_qkv_w = matmul(normed_low.T, grad_projected)
    grad_qv_b = jnp.stack(
        [
            jnp.sum(grad_query.astype(jnp.float32), axis=0),
            jnp.sum(grad_value.astype(jnp.float32), axis=0),
        ]
    )
    grad_normed = matmul(grad_projected, qkv_w.T)
    grad_rows_part, grad_in_gain, grad_in_shift = norm_in_back(grad_normed)
    grad_source = (grad_middle + grad_rows_part).astype(jnp.bfloat16).reshape(source.shape)
    grad_terms = (
        grad_in_gain,
        grad_in_shift,
        grad_qkv_w,
        grad_qv_b,
        grad_proj_w,
        grad_proj_b,
        grad_mid_gain,
        grad_mid_shift,
        grad_fc1_w,
        grad_fc1_b,
        grad_fc2_w,
        grad_fc2_b,
    )
    return (output, grad_source, grad_terms, jnp.sum(bias_terms, axis=0))


def shards(
    clips,
    out_grad,
    clip_order,
    region_label,
    rel_index,
    norm1_gain,
    norm1_bias,
    qkv_weight,
    qv_bias,
    bias_table,
    proj_weight,
    proj_bias,
    norm2_gain,
    norm2_bias,
    fc1_weight,
    fc1_bias,
    fc2_weight,
    fc2_bias,
):
    clip_count = clips.shape[0] // MICRO
    slot_order = clip_order[0]
    keep_mask = region_label[:, :, None] == region_label[:, None, :]
    rel_bias = jnp.take(bias_table.astype(jnp.float32), rel_index, axis=1)
    shard_set = (
        norm1_gain,
        norm1_bias,
        qkv_weight,
        qv_bias,
        proj_weight,
        proj_bias,
        norm2_gain,
        norm2_bias,
        fc1_weight,
        fc1_bias,
        fc2_weight,
        fc2_bias,
    )
    grad_sums = tuple((jnp.zeros(weight_shard.shape, jnp.float32) for weight_shard in shard_set))
    bias_sum = jnp.zeros(rel_bias.shape, jnp.float32)
    outputs = []
    source_grads = []
    for micro_index in range(MICRO):
        picked_slots = lax.dynamic_slice_in_dim(slot_order, micro_index * clip_count, clip_count)
        source = jnp.take(clips, picked_slots, axis=0)
        cot_block = out_grad[micro_index * clip_count : (micro_index + 1) * clip_count]
        full_weights = (
            lax.all_gather(norm1_gain, ("dp", "seq"), axis=0, tiled=True),
            lax.all_gather(norm1_bias, ("dp", "seq"), axis=0, tiled=True),
            lax.all_gather(qkv_weight, ("dp", "seq"), axis=0, tiled=True),
            lax.all_gather(qv_bias, ("dp", "seq"), axis=1, tiled=True),
            lax.all_gather(proj_weight, ("dp", "seq"), axis=0, tiled=True),
            lax.all_gather(proj_bias, ("dp", "seq"), axis=0, tiled=True),
            lax.all_gather(norm2_gain, ("dp", "seq"), axis=0, tiled=True),
            lax.all_gather(norm2_bias, ("dp", "seq"), axis=0, tiled=True),
            lax.all_gather(fc1_weight, ("dp", "seq"), axis=0, tiled=True),
            lax.all_gather(fc1_bias, ("dp", "seq"), axis=0, tiled=True),
            lax.all_gather(fc2_weight, ("dp", "seq"), axis=0, tiled=True),
            lax.all_gather(fc2_bias, ("dp", "seq"), axis=0, tiled=True),
        )
        output, grad_source, grad_terms, bias_term = layer_pass(
            source, cot_block, full_weights, rel_bias, keep_mask
        )
        grad_terms = (
            lax.psum_scatter(grad_terms[0], ("dp", "seq"), scatter_dimension=0, tiled=True),
            lax.psum_scatter(grad_terms[1], ("dp", "seq"), scatter_dimension=0, tiled=True),
            lax.psum_scatter(grad_terms[2], ("dp", "seq"), scatter_dimension=0, tiled=True),
            lax.psum_scatter(grad_terms[3], ("dp", "seq"), scatter_dimension=1, tiled=True),
            lax.psum_scatter(grad_terms[4], ("dp", "seq"), scatter_dimension=0, tiled=True),
            lax.psum_scatter(grad_terms[5], ("dp", "seq"), scatter_dimension=0, tiled=True),
            lax.psum_scatter(grad_terms[6], ("dp", "seq"), scatter_dimension=0, tiled=True),
            lax.psum_scatter(grad_terms[7], ("dp", "seq"), scatter_dimension=0, tiled=True),
            lax.psum_scatter(grad_terms[8], ("dp", "seq"), scatter_dimension=0, tiled=True),
            lax.psum_scatter(grad_terms[9], ("dp", "seq"), scatter_dimension=0, tiled=True),
            lax.psum_scatter(grad_terms[10], ("dp", "seq"), scatter_dimension=0, tiled=True),
            lax.psum_scatter(grad_terms[11], ("dp", "seq"), scatter_dimension=0, tiled=True),
        )
        grad_sums = tuple((previous + fresh for previous, fresh in zip(grad_sums, grad_terms)))
        bias_sum = bias_sum + bias_term
        outputs.append(output)
        source_grads.append(grad_source)
    flat_terms = bias_sum.reshape(bias_sum.shape[0], -1).T
    table_terms = jax.ops.segment_sum(flat_terms, rel_index.reshape(-1), num_segments=TBL).T
    table_grad = lax.psum(table_terms, "dp")
    output_all = jnp.concatenate(outputs, axis=0)
    clips_grad = jnp.zeros_like(clips).at[slot_order].set(jnp.concatenate(source_grads, axis=0))
    return (
        output_all,
        clips_grad,
        grad_sums[0],
        grad_sums[1],
        grad_sums[2],
        grad_sums[3],
        table_grad,
        grad_sums[4],
        grad_sums[5],
        grad_sums[6],
        grad_sums[7],
        grad_sums[8],
        grad_sums[9],
        grad_sums[10],
        grad_sums[11],
    )


EPS = 1e-5
LOG2E = math.log2(math.e)
LN2 = math.log(2.0)
SCALE = HD**-0.5
MASKED = -1e30
bf = jnp.bfloat16
f32 = jnp.float32
i32 = jnp.int32
MESH = pl.DeviceIdType.MESH
VM = pltpu.VMEM
DMA = pltpu.SemaphoreType.DMA

CL = 2
NS = 4
RP = 400
RT = CL * RP
KP = 512
C = 512
NHEAD = 16
TA = 10
TB = 256
SHARD = (16, 16, 16, 64)
WIDTH = (1536, 512, 2048, 512)
PARTS = ((0, 4), (4, 3))


def nn(a, b):
    return jnp.dot(a, b, preferred_element_type=f32)


def nt(a, b):
    return lax.dot_general(a, b, (((1,), (1,)), ((), ())), preferred_element_type=f32)


def tn(a, b):
    return lax.dot_general(a, b, (((0,), (0,)), ((), ())), preferred_element_type=f32)


def norm_parts(v):
    mu = jnp.mean(v, axis=-1, keepdims=True)
    c = v - mu
    r = lax.rsqrt(jnp.mean(c * c, axis=-1, keepdims=True) + EPS)
    return c * r, r


class Place:
    def __init__(self):
        dp, self.z = lax.axis_index("dp"), lax.axis_index("seq")
        self.dp = dp
        self.y, self.x, self.c = dp // 4, (dp // 2) % 2, dp % 2
        self.yn, self.xn, self.cn = 1 - self.y, 1 - self.x, 1 - self.c
        self.over_x = (self.dp_of(self.y, self.xn, self.c), self.z)
        self.over_y = (self.dp_of(self.yn, self.x, self.c), self.z)
        self.core = (self.dp_of(self.y, self.x, self.cn), self.z)
        self.block = dp * 4 + self.z

    def dp_of(self, y, x, c):
        return y * 4 + x * 2 + c

    def seq(self, z):
        return (self.dp, z)

    def far(self, d):
        return lax.rem(self.z + d, NS)

    def greet(self):
        bar = pltpu.get_barrier_semaphore()
        peers = [self.seq(self.far(d)) for d in (1, 2, 3)]
        peers += [self.over_x, self.over_y, self.core]
        for peer in peers:
            pl.semaphore_signal(bar, inc=1, device_id=peer, device_id_type=MESH)
        pl.semaphore_wait(bar, len(peers))


def rcopy(src, dst, ssem, rsem, dev):
    return pltpu.make_async_remote_copy(
        src_ref=src, dst_ref=dst, send_sem=ssem, recv_sem=rsem, device_id=dev, device_id_type=MESH
    )


def take(ref, sem):
    pltpu.make_async_copy(ref, ref, sem).wait()


def window_start(w, part):
    return lax.rem(7 * w + SHIFT_S + part, SIDE)


def send_windows(me, src, dst, ssem, rsem, lsem):
    slot = lax.rem(me.z + 2, NS)
    for d in range(NS):
        w = me.far(d)
        wy, wx = w // 2, lax.rem(w, 2)
        for c in range(CL):
            for y7, ny in PARTS:
                for x7, nx in PARTS:
                    a = src.at[c, pl.ds(window_start(wy, y7), ny), pl.ds(window_start(wx, x7), nx)]
                    b = dst.at[c, slot, pl.ds(y7, ny), pl.ds(x7, nx)]
                    if d == 0:
                        pltpu.make_async_copy(a, b, lsem).start()
                    else:
                        rcopy(a, b, ssem.at[d - 1], rsem.at[d - 1], me.seq(w)).start()


def take_windows(me, dst, ssem, rsem, lsem):
    for d in range(NS):
        slot = lax.rem(me.z + NS - d + 2, NS)
        if d == 0:
            take(dst.at[:, slot], lsem)
        else:
            take(dst.at[:, slot], rsem.at[d - 1])
            take(dst.at[:, slot], ssem.at[d - 1])


def send_home(me, src, dst, ssem, rsem, lsem):
    wy, wx = me.z // 2, lax.rem(me.z, 2)
    for d in range(NS):
        t = me.far(d)
        slot = lax.rem(t + 2, NS)
        for c in range(CL):
            for y7, ny in PARTS:
                for x7, nx in PARTS:
                    a = src.at[c, slot, pl.ds(y7, ny), pl.ds(x7, nx)]
                    b = dst.at[c, pl.ds(window_start(wy, y7), ny), pl.ds(window_start(wx, x7), nx)]
                    if d == 0:
                        pltpu.make_async_copy(a, b, lsem).start()
                    else:
                        rcopy(a, b, ssem.at[d - 1], rsem.at[d - 1], me.seq(t)).start()


def take_home(me, src, ssem, rsem, lsem):
    take(src.at[:, 0], lsem)
    for d in (1, 2, 3):
        take(src.at[:, 0], rsem.at[d - 1])
        take(src.at[:, 0], ssem.at[d - 1])


class Gather:
    def __init__(self, me, k, shard, full, zsem, ssem, rsem):
        self.me, self.shard, self.full, self.r = me, shard, full, SHARD[k]
        self.zsem, self.ssem, self.rsem = zsem.at[k], ssem.at[k], rsem.at[k]

    def rows(self, dp, first=0, count=NS):
        return self.full.at[pl.ds(pl.multiple_of((dp * NS + first) * self.r, self.r), count * self.r)]

    def push(self, ref, slot, dev, sem=None):
        rcopy(ref, ref, self.ssem if sem is None else sem, self.rsem.at[slot], dev).start()

    def spread(self, z):
        block = self.rows(self.me.dp, z, 1)
        self.push(block, 4 + z, self.me.over_x)
        self.push(block, 8 + z, self.me.over_y)
        self.push(block, 16 + z, self.me.core)

    def onward(self, n, act):
        z = self.me.z
        for ok, source, target in (((z >= n) & (z < NS - 1), z - n, z + 1), ((z + n < NS) & (z > 0), z + n, z - 1)):
            pl.when(ok)(functools.partial(act, self.rows(self.me.dp, source, 1), source, target))

    def along(self, n):
        self.onward(n, lambda block, source, target: self.push(block, source, self.me.seq(target), self.zsem))

    def start(self):
        me = self.me
        self.full[pl.ds(pl.multiple_of(me.block * self.r, self.r), self.r), :] = self.shard[...]
        self.along(0)
        self.spread(me.z)

    def step(self, n):
        z = self.me.z

        def came(source):
            take(self.rows(self.me.dp, source, 1), self.rsem.at[source])

        for ok, source in ((z >= n, z - n), (z + n < NS, z + n)):
            pl.when(ok)(functools.partial(came, source))
        self.along(n)
        for ok, source in ((z >= n, z - n), (z + n < NS, z + n)):
            pl.when(ok)(functools.partial(self.spread, source))

    def corner(self):
        me = self.me
        dx, dy = me.over_x[0], me.over_y[0]
        for z in range(NS):
            take(self.rows(dx, z, 1), self.rsem.at[4 + z])
            if z < 2:
                self.push(self.rows(dx, z, 1), 12 + z, me.over_y)
        self.push(self.rows(dx), 20, me.core)
        for z in range(NS):
            take(self.rows(dy, z, 1), self.rsem.at[8 + z])
            if z >= 2:
                self.push(self.rows(dy, z, 1), 12 + z, me.over_x)
        self.push(self.rows(dy), 21, me.core)

    def last(self):
        me = self.me
        dd = me.dp_of(me.yn, me.xn, me.c)
        for z in range(NS):
            take(self.rows(dd, z, 1), self.rsem.at[12 + z])
        self.push(self.rows(dd), 22, me.core)

    def finish(self):
        me = self.me
        for z in range(NS):
            take(self.rows(me.dp_of(me.y, me.x, me.cn), z, 1), self.rsem.at[16 + z])
        for slot, (y, x) in ((20, (me.y, me.xn)), (21, (me.yn, me.x)), (22, (me.yn, me.xn))):
            take(self.rows(me.dp_of(y, x, me.cn)), self.rsem.at[slot])
        for n in range(NS - 1):
            self.onward(n, lambda block, source, target: take(block, self.zsem))
        take(self.full.at[pl.ds(0, 28 * self.r)], self.ssem)


class Vectors:
    def __init__(self, me, full, ssem, rsem):
        self.me, self.full, self.ssem, self.rsem = me, full, ssem, rsem

    def rows(self, dp, first=0, count=NS):
        return self.full.at[pl.ds(dp * NS + first, count)]

    def push(self, ref, slot, dev):
        rcopy(ref, ref, self.ssem.at[slot], self.rsem.at[slot], dev).start()

    def start(self):
        me = self.me
        for d in (1, 2, 3):
            self.push(self.rows(me.dp, me.z, 1), d - 1, me.seq(me.far(d)))

    def plane(self):
        me = self.me
        for d in (1, 2, 3):
            take(self.rows(me.dp, me.far(NS - d), 1), self.rsem.at[d - 1])
        for slot, dev in ((3, me.over_x), (4, me.over_y), (5, me.core)):
            self.push(self.rows(me.dp), slot, dev)

    def diagonal(self):
        me = self.me
        dx, dy = me.over_x[0], me.over_y[0]
        take(self.rows(dx), self.rsem.at[3])
        self.push(self.rows(dx), 6, me.over_y)
        self.push(self.rows(dx), 8, me.core)
        take(self.rows(dy), self.rsem.at[4])
        self.push(self.rows(dy), 9, me.core)

    def last(self):
        me = self.me
        dd = me.dp_of(me.yn, me.xn, me.c)
        take(self.rows(dd), self.rsem.at[6])
        self.push(self.rows(dd), 10, me.core)

    def finish(self):
        me = self.me
        for slot, (y, x) in ((5, (me.y, me.x)), (8, (me.y, me.xn)), (9, (me.yn, me.x)), (10, (me.yn, me.xn))):
            take(self.rows(me.dp_of(y, x, me.cn)), self.rsem.at[slot])
        for slot in (0, 1, 2, 3, 4, 5, 6, 8, 9, 10):
            take(self.rows(0, 0, 1) if slot < 3 else self.rows(0), self.ssem.at[slot])


def pack_vectors(me, sv, g1, b1, qv, pb, g2, b2, b3, b4):
    row = jnp.zeros((1, 256), f32)
    sv[pl.ds(me.block, 1), 0] = row
    pieces = (g1[...], b1[...], qv[0:1, :], qv[1:2, :], pb[...], g2[...], b2[...], b4[...])
    for k, piece in enumerate(pieces):
        sv[pl.ds(me.block, 1), 0, 16 * k : 16 * k + 16] = piece.astype(f32)
    sv[pl.ds(me.block, 1), 0, 128:192] = b3[...].astype(f32)


def spread_vectors(sv, vec):
    v = sv[...].reshape(32, 256).astype(bf)
    lane = lax.broadcasted_iota(i32, (256, C), 1)
    row = lax.broadcasted_iota(i32, (256, C), 0)
    blk = lax.broadcasted_iota(i32, (32, C), 0)
    col = lax.broadcasted_iota(i32, (32, C), 1)
    for k in range(12):
        if k < 8:
            pick, own = row == 16 * k + (lane & 15), blk == (col >> 4)
        else:
            pick, own = row == 128 + (lane & 63), blk == (col >> 6) + 8 * (k - 8)
        y = nn(v, jnp.where(pick, 1.0, 0.0).astype(bf))
        vec[k : k + 1, :] = jnp.sum(jnp.where(own, y, 0.0), axis=0, keepdims=True)


def one_hot(lo, i):
    d = jnp.broadcast_to(lo[pl.ds(i, 1), :], (16, KP)).astype(bf)
    d = d - lax.broadcasted_iota(i32, (16, KP), 0).astype(f32).astype(bf)
    one, zero = jnp.asarray(1, bf), jnp.asarray(0, bf)
    return jnp.concatenate([jnp.where(d == jnp.asarray(16 * c, bf), one, zero) for c in range(16)], axis=0)


def order_index(me, idx, lab, perm, hi, lo, colb, lrow):
    p = perm[...]
    iv = idx[...]
    for dst, part in ((hi, iv >> 8), (lo, iv & 255)):
        rows = nn(p[0:RP, :], part.astype(f32).astype(bf)).astype(bf)
        dst[...] = nt(rows, p)
    own = lab[pl.ds(me.z, 1), :].astype(f32)
    own = jnp.broadcast_to(own, (8, WT)).astype(bf)
    lane = lax.broadcasted_iota(i32, (8, KP), 1)
    lrow[...] = jnp.where(lane < WT, nt(own, p), -1.0)
    colb[...] = jnp.broadcast_to(nt(p[0:RP, :], own)[:, 0:1], (RP, 128))


def table_rows(tbl, tab):
    whole = jnp.concatenate([tbl[s] for s in range(NS)], axis=0)
    for a in range(TA):
        tab[a * 16 : (a + 1) * 16, :] = whole[:, a * TB : (a + 1) * TB].astype(bf)


def gather_rows(first, count, tab, hi, lo, colb, lrow, bias):
    unroll = 8

    def body(t, _):
        for u in range(unroll):
            i = first + t * unroll + u
            y = nn(tab[...], one_hot(lo, i))
            high = jnp.broadcast_to(hi[pl.ds(i, 1), :], (16, KP))
            acc = jnp.zeros((16, KP), f32)
            for a in range(TA):
                acc = jnp.where(high == a, y[a * 16 : (a + 1) * 16], acc)
            acc = acc * LOG2E
            own = colb[pl.ds(i, 1), :]
            r0 = pl.multiple_of(i * 16, 16)
            for j in range(4):
                keep = lrow[0:1, j * 128 : (j + 1) * 128] == own
                bias[j, pl.ds(r0, 16), :] = jnp.where(keep, acc[:, j * 128 : (j + 1) * 128], MASKED)
        return 0

    lax.fori_loop(0, count // unroll, body, 0)


def scatter_rows(first, count, g, other, hi, lo, total):
    unroll = 8
    zero = jnp.asarray(0, bf)

    def body(t, _):
        ls, rs = [], []
        for u in range(unroll):
            n = t * unroll + u
            i = first + n
            rs.append(one_hot(lo, i))
            high = jnp.broadcast_to(hi[pl.ds(i, 1), :], (16, KP)).astype(bf)
            r0 = pl.multiple_of(i * 16, 16)
            own = jnp.concatenate([g[j, pl.ds(r0, 16), :] for j in range(4)], axis=1)
            own = (own + other[pl.ds(pl.multiple_of(n * 16, 16), 16), :].astype(f32)).astype(bf)
            ls.append(
                jnp.concatenate([jnp.where(high == jnp.asarray(a, bf), own, zero) for a in range(TA)], axis=0)
            )
        total[...] += nt(jnp.concatenate(ls, axis=1), jnp.concatenate(rs, axis=1))
        return 0

    lax.fori_loop(0, count // unroll, body, 0)


def load_tokens(src, clip, dst, p):
    for s in range(NS):
        v = src[clip, s].astype(f32).reshape(98, C)
        dst[p * RP + s * 98 : p * RP + (s + 1) * 98, :] = v.astype(dst.dtype)
    dst[p * RP + WT : (p + 1) * RP, :] = jnp.zeros((RP - WT, C), dst.dtype)


def store_tokens(src, clip, dst, slot):
    for s in range(NS):
        v = src[clip, s * 98 : (s + 1) * 98, :]
        dst[slot, s] = v.reshape(49, 2, C).astype(bf).reshape(7, 7, 2, C)


def qkv_phase(x, vec, wq, n1, q, k, v):
    for p in range(CL):
        k[p, RP:KP, :] = jnp.zeros((KP - RP, C), bf)
        v[p, RP:KP, :] = jnp.zeros((KP - RP, C), bf)

    def body(p, _):
        r0 = pl.multiple_of(p * RP, RP)
        n, _r = norm_parts(x[pl.ds(r0, RP), :].astype(f32))
        y = (n * vec[0:1, :] + vec[1:2, :]).astype(bf)
        n1[pl.ds(r0, RP), :] = y
        q[pl.ds(r0, RP), :] = ((nn(y, wq[:, 0:C]) + vec[2:3, :]) * (SCALE * LOG2E)).astype(bf)
        k[p, 0:RP, :] = nn(y, wq[:, C : 2 * C]).astype(bf)
        v[p, 0:RP, :] = (nn(y, wq[:, 2 * C : 3 * C]) + vec[3:4, :]).astype(bf)
        return 0

    lax.fori_loop(0, CL, body, 0)


def attention_forward(q, k, v, bias, e, att, inv, poll):
    lane = lax.broadcasted_iota(i32, (1, 128), 1) // HD

    def body(t, _):
        quad, p = t // CL, lax.rem(t, CL)
        l0 = pl.multiple_of(quad * 128, 128)
        r = pl.ds(pl.multiple_of(p * RP, RP), RP)
        qq = q[r, pl.ds(l0, 128)]
        kk = k[p, :, pl.ds(l0, 128)]
        vv = v[p, :, pl.ds(l0, 128)]
        acc = jnp.zeros((RP, 128), f32)
        ainv = acc
        for hq in range(4):
            h = quad * 4 + hq
            s = nt(qq, jnp.where(lane == hq, kk, jnp.zeros_like(kk)))
            s = s + jnp.concatenate([bias[j, pl.ds(h, RP, stride=16), :] for j in range(4)], axis=1)
            w = jnp.exp2(s - jnp.max(s, axis=1, keepdims=True)).astype(bf)
            e[p, h] = w
            o = nn(w, jnp.where(lane == hq, vv, jnp.ones_like(vv)))
            one = 1.0 / pltpu.roll(o, HD, 1)
            acc = jnp.where(lane == hq, o * one, acc)
            ainv = jnp.where(lane == hq, one, ainv)
        att[r, pl.ds(l0, 128)] = acc.astype(bf)
        inv[r, pl.ds(l0, 128)] = ainv
        poll(t)
        return 0

    lax.fori_loop(0, 4 * CL, body, 0)


def feed_forward(x, dy, att, vec, wp, w1, w2, nm, mid, acc, out, gvec):
    for p in range(CL):
        r = slice(p * RP, (p + 1) * RP)
        m = x[r, :].astype(f32) + nn(att[r, :], wp[...]) + vec[4:5, :]
        mid[r, :] = m
        n, _ = norm_parts(m)
        nm[r, :] = (n * vec[5:6, :] + vec[6:7, :]).astype(bf)
        out[p] = m + vec[7:8, :]
    acc[...] = jnp.zeros_like(acc)
    gvec[7:8, :] = jnp.sum(dy[...].astype(f32), axis=0, keepdims=True)

    def body(c, _):
        c0 = pl.multiple_of(c * C, C)
        g1 = g2 = gb = None
        for p in range(CL):
            r = slice(p * RP, (p + 1) * RP)
            hid = nn(nm[r, :], w1[:, pl.ds(c0, C)]) + vec[pl.ds(8 + c, 1), :]
            density = jnp.exp2(hid * hid * (-0.5 * LOG2E)) * (1 / math.sqrt(2 * math.pi))
            phi = 0.5 * (1.0 + lax.erf(hid * (1 / math.sqrt(2.0))))
            act = (hid * phi).astype(bf)
            slope = phi + hid * density
            out[p] += nn(act, w2[pl.ds(c0, C), :])
            dh = (nt(dy[r, :], w2[pl.ds(c0, C), :]) * slope).astype(bf)
            acc[r, :] += nt(dh, w1[:, pl.ds(c0, C)])
            a2, a1, ab = tn(act, dy[r, :]), tn(nm[r, :], dh), jnp.sum(dh.astype(f32), axis=0, keepdims=True)
            g2, g1, gb = (a2, a1, ab) if p == 0 else (g2 + a2, g1 + a1, gb + ab)
        gvec[pl.ds(8 + c, 1), :] = gb
        w2[pl.ds(c0, C), :] = g2.astype(bf)
        w1[:, pl.ds(c0, C)] = g1.astype(bf)
        return 0

    lax.fori_loop(0, 4, body, 0)


def middle_backward(dy, att, vec, wp, mid, acc, inv, gvec, do):
    s4 = s5 = s6 = jnp.zeros((1, C), f32)
    parts = []
    for p in range(CL):
        r = slice(p * RP, (p + 1) * RP)
        n, rr = norm_parts(mid[r, :])
        gmn = acc[r, :]
        s5 += jnp.sum(gmn * n, axis=0, keepdims=True)
        s6 += jnp.sum(gmn, axis=0, keepdims=True)
        g = gmn * vec[5:6, :]
        gm = dy[r, :].astype(f32) + rr * (
            g - jnp.mean(g, axis=-1, keepdims=True) - n * jnp.mean(g * n, axis=-1, keepdims=True)
        )
        mid[r, :] = gm
        gb = gm.astype(bf)
        s4 += jnp.sum(gb.astype(f32), axis=0, keepdims=True)
        parts.append(gb)
        low = (nt(gb, wp[...]) * inv[r, :]).astype(bf)
        do[r, :] = low
        acc[r, :] = low.astype(f32) * att[r, :].astype(f32)
    gvec[4:5, :] = s4
    gvec[5:6, :] = s5
    gvec[6:7, :] = s6
    wp[...] = tn(att[...], jnp.concatenate(parts, axis=0)).astype(bf)


def attention_backward(q, k, v, e, do, prod, g, dq, dk, dv, poll):
    lane = lax.broadcasted_iota(i32, (1, 128), 1) // HD

    def body(quad, _):
        l0 = pl.multiple_of(quad * 128, 128)
        dqs = [jnp.zeros((RP, 128), f32) for _ in range(CL)]
        dks, dvs = [[], []], [[], []]
        qts = [q[p * RP : (p + 1) * RP, pl.ds(l0, 128)].T for p in range(CL)]
        dots = [do[p * RP : (p + 1) * RP, pl.ds(l0, 128)].T for p in range(CL)]
        for hq in range(4):
            h = quad * 4 + hq
            f = slice(hq * HD, (hq + 1) * HD)
            both = None
            for p in range(CL):
                r = slice(p * RP, (p + 1) * RP)
                kk = k[p, :, pl.ds(l0, 128)]
                vv = v[p, :, pl.ds(l0, 128)]
                dp = nt(do[r, pl.ds(l0, 128)], jnp.where(lane == hq, vv, jnp.zeros_like(vv)))
                inner = jnp.sum(jnp.where(lane == hq, prod[r, pl.ds(l0, 128)], 0.0), axis=1, keepdims=True)
                w = e[p, h]
                ds = w.astype(f32) * (dp - inner)
                both = ds if both is None else both + ds
                low = ds.astype(bf)
                dqs[p] = dqs[p] + nn(low, jnp.where(lane == hq, kk, jnp.zeros_like(kk)))
                dks[p].append((nn(qts[p][f], low) * LN2).astype(bf))
                dvs[p].append(nn(dots[p][f], w).astype(bf))
            for j in range(4):
                g[j, pl.ds(h, RP, stride=16), :] = both[:, j * 128 : (j + 1) * 128]
            if hq == 1:
                poll(quad, 0)
        for p in range(CL):
            r = slice(p * RP, (p + 1) * RP)
            dq[r, pl.ds(l0, 128)] = (dqs[p] * SCALE).astype(bf)
            dk[r, pl.ds(l0, 128)] = jnp.concatenate(dks[p], axis=0).T[0:RP]
            dv[p, 0:RP, pl.ds(l0, 128)] = jnp.concatenate(dvs[p], axis=0).T[0:RP]
        poll(quad, 1)
        return 0

    lax.fori_loop(0, 4, body, 0)


def input_backward(x, n1, vec, wq, dq, dk, dv, mid, dx, gvec):
    s0 = s1 = s3 = jnp.zeros((1, C), f32)
    gvec[2:3, :] = jnp.sum(dq[...].astype(f32), axis=0, keepdims=True)
    for p in range(CL):
        r = slice(p * RP, (p + 1) * RP)
        dvp = dv[p, 0:RP, :]
        s3 += jnp.sum(dvp.astype(f32), axis=0, keepdims=True)
        gn = nt(dq[r, :], wq[:, 0:C]) + nt(dk[r, :], wq[:, C : 2 * C]) + nt(dvp, wq[:, 2 * C : 3 * C])
        n, rr = norm_parts(x[r, :].astype(f32))
        s0 += jnp.sum(gn * n, axis=0, keepdims=True)
        s1 += jnp.sum(gn, axis=0, keepdims=True)
        g = gn * vec[0:1, :]
        dx[p] = mid[r, :] + rr * (
            g - jnp.mean(g, axis=-1, keepdims=True) - n * jnp.mean(g * n, axis=-1, keepdims=True)
        )
    gvec[0:1, :] = s0
    gvec[1:2, :] = s1
    gvec[3:4, :] = s3
    n1t = n1[...].T
    wq[:, 0:C] = nn(n1t, dq[...]).astype(bf)
    wq[:, C : 2 * C] = nn(n1t, dk[...]).astype(bf)
    dva = jnp.concatenate([dv[p, 0:RP, :] for p in range(CL)], axis=0)
    wq[:, 2 * C : 3 * C] = nn(n1t, dva).astype(bf)


class Reduce:
    def __init__(self, me, k, grad, out, ssem, rsem, rc, rx, ry, ra, rz):
        self.me, self.r, self.grad, self.out = me, SHARD[k], grad, out
        self.u = 4 * self.r
        self.h = self.u // 2
        self.ssem, self.rsem = ssem.at[k], rsem.at[k]
        self.rc, self.rx, self.ry, self.ra, self.rz = rc, rx, ry, ra, rz

    def own(self, y, x, c, first=0, count=None):
        return pl.ds(pl.multiple_of(self.me.dp_of(y, x, c) * self.u + first, self.r), self.u if count is None else count)

    def send(self, rows, dst, slot, dev):
        rcopy(self.grad.at[rows], dst, self.ssem.at[slot], self.rsem.at[slot], dev).start()

    def add(self, rows, part, slot):
        take(part, self.rsem.at[slot])
        self.grad[rows, :] = (self.grad[rows, :].astype(f32) + part[...].astype(f32)).astype(bf)

    def cores(self):
        me = self.me
        for g in range(4):
            self.send(self.own(g // 2, g % 2, me.cn), self.rc.at[g], g, me.core)

    def plane(self):
        me, h = self.me, self.h
        for g in range(4):
            self.add(self.own(g // 2, g % 2, me.c), self.rc.at[g], g)
        for n in range(2):
            self.send(self.own(n, me.xn, me.c, 0, h), self.rx.at[n], 4 + n, me.over_x)
            self.send(self.own(me.yn, n, me.c, h, h), self.ry.at[n], 6 + n, me.over_y)

    def corner(self):
        me, h = self.me, self.h
        for n in range(2):
            self.add(self.own(n, me.x, me.c, 0, h), self.rx.at[n], 4 + n)
            self.add(self.own(me.y, n, me.c, h, h), self.ry.at[n], 6 + n)
        self.send(self.own(me.yn, me.x, me.c, 0, h), self.ra.at[0], 8, me.over_y)
        self.send(self.own(me.y, me.xn, me.c, h, h), self.ra.at[1], 9, me.over_x)

    def line(self):
        me, h, r = self.me, self.h, self.r
        for n in range(2):
            self.add(self.own(me.y, me.x, me.c, n * h, h), self.ra.at[n], 8 + n)
        for d in (1, 2, 3):
            z = me.far(d)
            self.send(self.own(me.y, me.x, me.c, z * r, r), self.rz.at[d - 1], 9 + d, me.seq(z))

    def finish(self):
        me, r, u, h = self.me, self.r, self.u, self.h
        total = self.grad[self.own(me.y, me.x, me.c, me.z * r, r), :].astype(f32)
        for d in (1, 2, 3):
            take(self.rz.at[d - 1], self.rsem.at[9 + d])
            total = total + self.rz[d - 1].astype(f32)
        self.out[...] = total
        for slot in range(13):
            count = u if slot < 4 else h if slot < 10 else r
            take(self.grad.at[pl.ds(0, count)], self.ssem.at[slot])


SEG = 40
SEGS = RP // 2 // SEG


def block_kernel(
    order, clips, cot, sq, sp, s1, s2, g1, b1, qv, pb, g2, b2, b3, b4, table, lab, idx, perm,
    out_t, dx_t, oq, op, o1, o2, og1, ob1, oqv, opb, og2, ob2, ob3, ob4, otab,
    bg, e, wq, wp, w1, w2, xw, dyw, x, dy, n1, q, k, v, att, inv, nm, mid, acc, out, do,
    hi, lo, sv, tbl, tab, colb, lrow, vec, gvec, total, tz, tx, vz, vx,
    *rest,
):
    parts = [rest[5 * n : 5 * n + 5] for n in range(4)]
    (xs, xr, xl, ds_, dr, dl, os_, or_, ol, hs, hr, hl, wz, ws, wr, vs, vr, ts, tr, bs, br, free, es, er,
     rs, rr, zs, zr, as_, ar) = rest[20:]
    me = Place()
    me.greet()
    pack_vectors(me, sv, g1, b1, qv, pb, g2, b2, b3, b4)
    tbl[pl.ds(me.z, 1), :, 2432:2560] = jnp.zeros((1, 4, 128), f32)
    tbl[pl.ds(me.z, 1), :, 0:TBL] = table[...].astype(f32)[None]
    weights = [
        Gather(me, n, shard, full, wz, ws, wr)
        for n, (shard, full) in enumerate(((sq, wq), (sp, wp), (s1, w1), (s2, w2)))
    ]
    later = [weights[1], weights[2], weights[3]]
    vectors = Vectors(me, sv, vs, vr)
    for d in (1, 2, 3):
        own = tbl.at[me.z]
        rcopy(own, own, ts.at[d - 1], tr.at[d - 1], me.seq(me.far(d))).start()
    vectors.start()
    weights[0].start()
    send_windows(me, clips, xw, xs, xr, xl)
    order_index(me, idx, lab, perm, hi, lo, colb, lrow)
    weights[0].step(1)
    for d in (1, 2, 3):
        take(tbl.at[0], tr.at[d - 1])
        take(tbl.at[0], ts.at[d - 1])
    table_rows(tbl, tab)

    def bias_rows(n, half):
        return bg.at[:, pl.ds(pl.multiple_of((half * SEGS + n) * SEG * 16, 16), SEG * 16)]

    def rows(n):
        gather_rows((me.c * SEGS + n) * SEG, SEG, tab, hi, lo, colb, lrow, bg)
        part = bias_rows(n, me.c)
        rcopy(part, part, bs.at[n], br.at[n], me.core).start()

    weights[0].step(2)
    vectors.plane()
    rows(0)
    weights[0].step(3)
    rows(1)
    vectors.diagonal()
    weights[0].corner()
    rows(2)
    vectors.last()
    weights[0].last()
    rows(3)
    vectors.finish()
    spread_vectors(sv, vec)
    for w in later:
        w.start()
    rows(4)
    weights[0].finish()
    take_windows(me, xw, xs, xr, xl)
    send_windows(me, cot, dyw, ds_, dr, dl)
    for p in range(CL):
        load_tokens(xw, p, x, p)
    for w in later:
        w.step(1)
    qkv_phase(x, vec, wq, n1, q, k, v)
    for n in range(SEGS):
        take(bias_rows(n, me.cn), br.at[n])
        take(bias_rows(n, me.c), bs.at[n])

    def forward_poll(t):
        steps = {0: lambda w: w.step(2), 1: lambda w: w.step(3), 3: lambda w: w.corner(), 5: lambda w: w.last()}
        for at, step in steps.items():

            def go(step=step):
                for w in later:
                    step(w)

            pl.when(t == at)(go)

    attention_forward(q, k, v, bg, e, att, inv, forward_poll)
    gvec[...] = jnp.zeros_like(gvec)
    for w in later:
        w.finish()
    take_windows(me, dyw, ds_, dr, dl)
    for p in range(CL):
        load_tokens(dyw, order[0, p], dy, p)
    feed_forward(x, dy, att, vec, wp, w1, w2, nm, mid, acc, out, gvec)
    reds = [
        Reduce(me, n, grad, total_out, rs, rr, *parts[n])
        for n, (grad, total_out) in enumerate(((wq, oq), (wp, op), (w1, o1), (w2, o2)))
    ]
    reds[2].cores()
    reds[3].cores()
    for p in range(CL):
        store_tokens(out, order[0, p], xw, p)
    send_home(me, xw, out_t, os_, or_, ol)
    middle_backward(dy, att, vec, wp, mid, acc, inv, gvec, do)
    reds[1].cores()
    reds[2].plane()

    def backward_poll(quad, half):
        def go1():
            reds[3].plane()
            reds[1].plane()

        def go2():
            reds[2].corner()

        if half == 0:
            pl.when(quad == 1)(go1)
        else:
            pl.when(quad == 3)(go2)

    attention_backward(q, k, v, e, do, acc, bg, nm, att, v, backward_poll)
    pl.semaphore_signal(free, inc=1, device_id=me.core, device_id_type=MESH)
    input_backward(x, n1, vec, wq, nm, att, v, mid, out, gvec)
    reds[0].cores()
    for p in range(CL):
        store_tokens(out, p, dyw, p)
    send_home(me, dyw, dx_t, hs, hr, hl)
    for d in (1, 2, 3):
        rcopy(gvec, vz.at[d - 1], zs.at[d - 1], zr.at[d - 1], me.seq(me.far(d))).start()
    other, halves = SEG * 16, ((0, 384), (1, 256))
    for n in range(SEGS):
        r0 = pl.multiple_of((me.cn * SEGS + n) * other, 16)
        lowered = jnp.concatenate([bg[j, pl.ds(r0, other), :] for j in range(4)], axis=1).astype(bf)
        e[1, 2 * n, 0:384, :] = lowered[0:384]
        e[1, 2 * n + 1, 0:256, :] = lowered[384:640]
        if n == 0:
            pl.semaphore_wait(free, 1)
        for m, count in halves:
            rcopy(
                e.at[1, 2 * n + m, pl.ds(0, count)], e.at[0, 2 * n + m, pl.ds(0, count)],
                es.at[2 * n + m], er.at[2 * n + m], me.core,
            ).start()
    total[...] = jnp.zeros_like(total)

    def scatter(n):
        for m, count in halves:
            take(e.at[0, 2 * n + m, pl.ds(0, count)], er.at[2 * n + m])
        first = (me.c * SEGS + n) * SEG
        scatter_rows(first, 24, bg, e.at[0, 2 * n], hi, lo, total)
        scatter_rows(first + 24, 16, bg, e.at[0, 2 * n + 1], hi, lo, total)

    scatter(0)
    reds[0].plane()
    reds[3].corner()
    reds[1].corner()
    scatter(1)
    reds[2].line()
    scatter(2)
    reds[0].corner()
    reds[3].line()
    reds[1].line()
    vecs = gvec[...]
    for d in (1, 2, 3):
        take(vz.at[d - 1], zr.at[d - 1])
        vecs = vecs + vz[d - 1]
    scatter(3)
    reds[0].line()
    scatter(4)
    for a in range(TA):
        for s in range(NS):
            tbl[s, :, a * TB : (a + 1) * TB] = total[a * 16 + 4 * s : a * 16 + 4 * s + 4, :]
    for d in (1, 2, 3):
        rcopy(tbl.at[me.far(d)], tz.at[d - 1], zs.at[2 + d], zr.at[2 + d], me.seq(me.far(d))).start()
    table = tbl[pl.ds(me.z, 1)].reshape(4, TA * TB)
    for n in (2, 3, 1):
        reds[n].finish()
    for d in (1, 2, 3):
        take(tz.at[d - 1], zr.at[2 + d])
        table = table + tz[d - 1]
    for n, dev in enumerate((me.core, me.over_x, me.over_y)):
        tx[2 * n] = table
        vx[2 * n] = vecs
        rcopy(tx.at[2 * n], tx.at[2 * n + 1], as_.at[2 * n], ar.at[2 * n], dev).start()
        rcopy(vx.at[2 * n], vx.at[2 * n + 1], as_.at[2 * n + 1], ar.at[2 * n + 1], dev).start()
        take(tx.at[2 * n + 1], ar.at[2 * n])
        take(vx.at[2 * n + 1], ar.at[2 * n + 1])
        table = table + tx[2 * n + 1]
        vecs = vecs + vx[2 * n + 1]
    otab[...] = table
    vx[6] = vecs
    part = pltpu.roll(vecs[0:8, :], C - me.block * 16, 1)
    for row, ref in ((0, og1), (1, ob1), (4, opb), (5, og2), (6, ob2), (7, ob4)):
        ref[...] = part[row : row + 1, 0:16]
    oqv[...] = part[2:4, 0:16]
    wide = jnp.broadcast_to(vx[6, pl.ds(8 + me.block // 8, 1), :], (8, C))
    ob3[...] = pltpu.roll(wide, C - lax.rem(me.block, 8) * 64, 1)[0:1, 0:64]
    reds[0].finish()
    for n in range(SEGS):
        for m, count in halves:
            take(e.at[1, 2 * n + m, pl.ds(0, count)], es.at[2 * n + m])
    for n in range(3):
        take(tx.at[0], as_.at[2 * n])
        take(vx.at[0], as_.at[2 * n + 1])
        take(vz.at[0], zs.at[n])
        take(tz.at[0], zs.at[3 + n])
    take_home(me, xw, os_, or_, ol)
    take_home(me, dyw, hs, hr, hl)


def publish_kernel(*refs):
    n = len(refs) // 2
    for source, target in zip(refs[:n], refs[n:]):
        target[...] = source[...]


def windowed(
    clips, out_grad, clip_order, region_label, rel_index, norm1_gain, norm1_bias, qkv_weight, qv_bias,
    bias_table, proj_weight, proj_bias, norm2_gain, norm2_bias, fc1_weight, fc1_bias, fc2_weight, fc2_bias,
):
    at = np.arange(WT)
    canonical = (2 * (at // 98) + at % 2) * 49 + (at % 98) // 2
    perm = np.zeros((KP, WT), np.float32)
    perm[at, canonical] = 1
    perm = jnp.asarray(perm, bf)
    field = lambda a: jnp.transpose(a, (0, 2, 3, 1, 4))
    row = lambda a: a.reshape(1, -1)
    spec = lambda space: pl.BlockSpec(memory_space=space)
    win = (CL, NS, 7, 7, 2, C)
    whole = ((C, 1536), (C, C), (C, 2048), (2048, C))
    rows = (RT, C)
    keys = (CL, KP, C)
    tab = (4, TA * TB)
    reduce_scratch = []
    for r, w in zip(SHARD, WIDTH):
        u, h = 4 * r, 2 * r
        reduce_scratch += [VM((n, m, w), bf) for n, m in ((4, u), (2, h), (2, h), (2, h), (3, r))]
    field_shape = (CL, SIDE, SIDE, 2, C)
    outs = [
        (field_shape, bf), (field_shape, bf), *(((r, w), f32) for r, w in zip(SHARD, WIDTH)),
        ((1, 16), f32), ((1, 16), f32), ((2, 16), f32), ((1, 16), f32), ((1, 16), f32), ((1, 16), f32), ((1, 64), f32),
        ((1, 16), f32), (tab, f32),
    ]
    outs = [jax.ShapeDtypeStruct(s, d) for s, d in outs]
    results = pl.pallas_call(
        block_kernel,
        out_shape=outs,
        in_specs=[spec(pltpu.SMEM)] + [spec(pl.ANY)] * 2 + [spec(VM)] * 16,
        out_specs=[spec(pl.ANY)] * 2 + [spec(VM)] * 13,
        scratch_shapes=[
            VM((4, RP * 16, 128), f32), VM((CL, NHEAD, RP, KP), bf), *(VM(s, bf) for s in whole), VM(win, bf), VM(win, bf),
            VM(rows, bf), VM(rows, bf), VM(rows, bf), VM(rows, bf), VM(keys, bf), VM(keys, bf),
            VM(rows, bf), VM(rows, f32), VM(rows, bf), VM(rows, f32), VM(rows, f32), VM((CL, RP, C), f32), VM(rows, bf),
            VM((RP, KP), f32), VM((RP, KP), f32), VM((32, 1, 256), f32), VM((NS, *tab), f32), VM((TA * 16, TB), bf),
            VM((RP, 128), f32), VM((8, KP), f32), VM((16, C), f32), VM((16, C), f32), VM((TA * 16, TB), f32),
            VM((3, *tab), f32), VM((6, *tab), f32), VM((3, 16, C), f32), VM((7, 16, C), f32),
            *reduce_scratch,
            *(DMA((3,)), DMA((3,)), DMA) * 4,
            DMA((4,)), DMA((4,)), DMA((4, 23)), DMA((11,)), DMA((11,)), DMA((3,)), DMA((3,)),
            DMA((SEGS,)), DMA((SEGS,)), pltpu.SemaphoreType.REGULAR, DMA((2 * SEGS,)), DMA((2 * SEGS,)),
            DMA((4, 13)), DMA((4, 13)), DMA((6,)), DMA((6,)), DMA((6,)), DMA((6,)),
        ],
        compiler_params=pltpu.CompilerParams(
            collective_id=0, has_side_effects=True, vmem_limit_bytes=64 * 1024 * 1024 - 64 * 1024
        ),
    )(
        clip_order, field(clips), field(out_grad), qkv_weight, proj_weight, fc1_weight, fc2_weight,
        row(norm1_gain), row(norm1_bias), qv_bias, row(proj_bias), row(norm2_gain), row(norm2_bias),
        row(fc1_bias), row(fc2_bias), bias_table, region_label, rel_index, perm,
    )
    out_t, dx_t, oq, op, o1, o2, og1, ob1, oqv, opb, og2, ob2, ob3, ob4, otab = pl.pallas_call(
        publish_kernel,
        out_shape=outs,
        in_specs=[spec(VM)] * 15,
        out_specs=[spec(VM)] * 15,
    )(*results)
    back = lambda a: jnp.transpose(a, (0, 3, 1, 2, 4))
    flat = lambda a: a.reshape(-1)
    return (
        back(out_t), back(dx_t), flat(og1), flat(ob1), oq, oqv, otab[:, :TBL], op, flat(opb), flat(og2), flat(ob2),
        o1, flat(ob3), o2, flat(ob4),
    )


def solution(mesh):
    in_specs = (
        P("dp", "seq", None, None, None),
        P("dp", "seq", None, None, None),
        P("dp", None),
        P(),
        P(),
        P(("dp", "seq")),
        P(("dp", "seq")),
        P(("dp", "seq"), None),
        P(None, ("dp", "seq")),
        P("seq", None),
        P(("dp", "seq"), None),
        P(("dp", "seq")),
        P(("dp", "seq")),
        P(("dp", "seq")),
        P(("dp", "seq"), None),
        P(("dp", "seq")),
        P(("dp", "seq"), None),
        P(("dp", "seq")),
    )
    out_specs = (
        P("dp", "seq", None, None, None),
        P("dp", "seq", None, None, None),
        P(("dp", "seq")),
        P(("dp", "seq")),
        P(("dp", "seq"), None),
        P(None, ("dp", "seq")),
        P("seq", None),
        P(("dp", "seq"), None),
        P(("dp", "seq")),
        P(("dp", "seq")),
        P(("dp", "seq")),
        P(("dp", "seq"), None),
        P(("dp", "seq")),
        P(("dp", "seq"), None),
        P(("dp", "seq")),
    )
    local = windowed if mesh.shape["dp"] == 8 and mesh.shape["seq"] == NS else shards
    return jax.shard_map(local, mesh=mesh, in_specs=in_specs, out_specs=out_specs, check_vma=False)
```

```python
import functools
import math

import jax
import jax.numpy as jnp
import numpy as np
from jax import lax
from jax.experimental import pallas as pl
from jax.experimental.pallas import tpu as pltpu
from jax.sharding import PartitionSpec as P

HD = 32
WIN_T = 8
WIN_S = 7
SHIFT_T = 4
SHIFT_S = 3
FR = 8
SIDE = 14
MICRO = 2
NWIN = 4
WT = 392
TBL = 2535


eps_norm = 1e-05


def layer_norm(values, norm_gain, norm_shift):
    average = jnp.mean(values, axis=-1, keepdims=True)
    centred = values - average
    variance = jnp.mean(centred * centred, axis=-1, keepdims=True)
    return centred * lax.rsqrt(variance + eps_norm) * norm_gain + norm_shift


def gelu_exact(values):
    return jax.nn.gelu(values, approximate=False)


def matmul(left_side, right_side):
    return jnp.dot(left_side, right_side, preferred_element_type=jnp.float32)


def window_split(field):
    rolled = jnp.roll(field, (-SHIFT_T, -SHIFT_S, -SHIFT_S), (0, 1, 2))
    blocks = rolled.reshape(FR // WIN_T, WIN_T, SIDE // WIN_S, WIN_S, SIDE // WIN_S, WIN_S, -1)
    return blocks.transpose(0, 2, 4, 1, 3, 5, 6).reshape(NWIN, WT, -1)


def window_merge(windows):
    blocks = windows.reshape(FR // WIN_T, SIDE // WIN_S, SIDE // WIN_S, WIN_T, WIN_S, WIN_S, -1)
    field = blocks.transpose(0, 3, 1, 4, 2, 5, 6).reshape(FR, SIDE, SIDE, -1)
    return jnp.roll(field, (SHIFT_T, SHIFT_S, SHIFT_S), (0, 1, 2))


def to_heads(field_rows):
    feature_count = field_rows.shape[-1]
    windows = window_split(field_rows.reshape(FR, SIDE, SIDE, feature_count))
    return windows.reshape(NWIN, WT, feature_count // HD, HD)


def from_heads(windows):
    feature_count = windows.shape[-1] * windows.shape[-2]
    merged = window_merge(windows.reshape(NWIN, WT, feature_count))
    return merged.reshape(-1, feature_count)


def window_scores(query_win, key_win, rel_bias, keep_mask):
    scores = jnp.einsum("wihd,wjhd->whij", query_win, key_win, preferred_element_type=jnp.float32)
    scores = scores * HD ** (-0.5) + rel_bias[None]
    return jnp.where(keep_mask[:, None], scores, -1e30)


def attend_clip(query_rows, key_rows, value_rows, rel_bias, keep_mask):
    scores = window_scores(to_heads(query_rows), to_heads(key_rows), rel_bias, keep_mask)
    row_max = jnp.max(scores, axis=-1, keepdims=True)
    exponent = jnp.exp(scores - row_max)
    row_total = jnp.sum(exponent, axis=-1, keepdims=True)
    probabilities = (exponent / row_total).astype(jnp.bfloat16)
    attended = jnp.einsum(
        "whij,wjhd->wihd", probabilities, to_heads(value_rows), preferred_element_type=jnp.float32
    ).astype(jnp.bfloat16)
    return (from_heads(attended), (row_max + jnp.log(row_total))[..., 0])


def attend_back(query_rows, key_rows, value_rows, grad_rows, log_total, rel_bias, keep_mask):
    query_win = to_heads(query_rows)
    key_win = to_heads(key_rows)
    value_win = to_heads(value_rows)
    grad_win = to_heads(grad_rows)
    scores = window_scores(query_win, key_win, rel_bias, keep_mask)
    probabilities = jnp.exp(scores - log_total[..., None])
    grad_probs = jnp.einsum(
        "wihd,wjhd->whij", grad_win, value_win, preferred_element_type=jnp.float32
    )
    row_inner = jnp.sum(probabilities * grad_probs, axis=-1, keepdims=True)
    grad_scores = (probabilities * (grad_probs - row_inner)).astype(jnp.bfloat16)
    score_scale = HD ** (-0.5)
    grad_query = (
        jnp.einsum("whij,wjhd->wihd", grad_scores, key_win, preferred_element_type=jnp.float32)
        * score_scale
    )
    grad_key = (
        jnp.einsum("whij,wihd->wjhd", grad_scores, query_win, preferred_element_type=jnp.float32)
        * score_scale
    )
    grad_value = jnp.einsum(
        "whij,wihd->wjhd",
        probabilities.astype(jnp.bfloat16),
        grad_win,
        preferred_element_type=jnp.float32,
    )
    bias_term = jnp.sum(grad_scores.astype(jnp.float32), axis=0)
    return (
        from_heads(grad_query).astype(jnp.bfloat16),
        from_heads(grad_key).astype(jnp.bfloat16),
        from_heads(grad_value).astype(jnp.bfloat16),
        bias_term,
    )


def layer_pass(source, cot_block, full_weights, rel_bias, keep_mask):
    (
        norm_in_gain,
        norm_in_shift,
        qkv_w,
        qv_b,
        proj_w,
        proj_b,
        norm_mid_gain,
        norm_mid_shift,
        fc1_w,
        fc1_b,
        fc2_w,
        fc2_b,
    ) = full_weights
    clip_count = source.shape[0]
    model_width = source.shape[-1]
    shaped = (clip_count, -1, model_width)
    token_rows = source.reshape(-1, model_width).astype(jnp.float32)
    normed, norm_in_back = jax.vjp(
        layer_norm, token_rows, norm_in_gain.astype(jnp.float32), norm_in_shift.astype(jnp.float32)
    )
    normed_low = normed.astype(jnp.bfloat16)
    projected = matmul(normed_low, qkv_w)
    qv_float = qv_b.astype(jnp.float32)
    query_rows = (projected[:, :model_width] + qv_float[0]).astype(jnp.bfloat16)
    key_rows = projected[:, model_width : 2 * model_width].astype(jnp.bfloat16)
    value_rows = (projected[:, 2 * model_width :] + qv_float[1]).astype(jnp.bfloat16)
    parts = (
        lax.all_to_all(query_rows.reshape(shaped), "seq", split_axis=2, concat_axis=1, tiled=True),
        lax.all_to_all(key_rows.reshape(shaped), "seq", split_axis=2, concat_axis=1, tiled=True),
        lax.all_to_all(value_rows.reshape(shaped), "seq", split_axis=2, concat_axis=1, tiled=True),
    )
    merged_heads, log_total = lax.map(
        lambda clip_parts: attend_clip(*clip_parts, rel_bias, keep_mask), parts
    )
    attended_heads, log_total, query_heads, key_heads, value_heads = (
        merged_heads,
        log_total,
        parts[0],
        parts[1],
        parts[2],
    )
    attended = lax.all_to_all(
        attended_heads, "seq", split_axis=1, concat_axis=2, tiled=True
    ).reshape(-1, model_width)
    branch = matmul(attended, proj_w) + proj_b.astype(jnp.float32)
    middle = token_rows + branch
    normed_mid, norm_mid_back = jax.vjp(
        layer_norm, middle, norm_mid_gain.astype(jnp.float32), norm_mid_shift.astype(jnp.float32)
    )
    normed_mid_low = normed_mid.astype(jnp.bfloat16)
    hidden = matmul(normed_mid_low, fc1_w) + fc1_b.astype(jnp.float32)
    active, gelu_back = jax.vjp(gelu_exact, hidden)
    active_low = active.astype(jnp.bfloat16)
    result = matmul(active_low, fc2_w) + fc2_b.astype(jnp.float32)
    output = (middle + result).astype(jnp.bfloat16).reshape(source.shape)
    grad_low = cot_block.reshape(-1, model_width)
    grad_float = grad_low.astype(jnp.float32)
    grad_fc2_w = matmul(active_low.T, grad_low)
    grad_fc2_b = jnp.sum(grad_float, axis=0)
    grad_active = matmul(grad_low, fc2_w.T)
    grad_hidden = gelu_back(grad_active)[0].astype(jnp.bfloat16)
    grad_fc1_w = matmul(normed_mid_low.T, grad_hidden)
    grad_fc1_b = jnp.sum(grad_hidden.astype(jnp.float32), axis=0)
    grad_normed_mid = matmul(grad_hidden, fc1_w.T)
    grad_mid_part, grad_mid_gain, grad_mid_shift = norm_mid_back(grad_normed_mid)
    grad_middle = grad_float + grad_mid_part
    grad_branch = grad_middle.astype(jnp.bfloat16)
    grad_proj_w = matmul(attended.T, grad_branch)
    grad_proj_b = jnp.sum(grad_branch.astype(jnp.float32), axis=0)
    grad_attended = matmul(grad_branch, proj_w.T).astype(jnp.bfloat16)
    grad_heads = lax.all_to_all(
        grad_attended.reshape(shaped), "seq", split_axis=2, concat_axis=1, tiled=True
    )
    grad_query, grad_key, grad_value, bias_terms = lax.map(
        lambda clip_parts: attend_back(*clip_parts, rel_bias, keep_mask),
        (query_heads, key_heads, value_heads, grad_heads, log_total),
    )
    grad_query, grad_key, grad_value = (
        lax.all_to_all(grad_query, "seq", split_axis=1, concat_axis=2, tiled=True),
        lax.all_to_all(grad_key, "seq", split_axis=1, concat_axis=2, tiled=True),
        lax.all_to_all(grad_value, "seq", split_axis=1, concat_axis=2, tiled=True),
    )
    grad_query = grad_query.reshape(-1, model_width)
    grad_value = grad_value.reshape(-1, model_width)
    grad_projected = jnp.concatenate(
        [grad_query, grad_key.reshape(-1, model_width), grad_value], axis=1
    )
    grad_qkv_w = matmul(normed_low.T, grad_projected)
    grad_qv_b = jnp.stack(
        [
            jnp.sum(grad_query.astype(jnp.float32), axis=0),
            jnp.sum(grad_value.astype(jnp.float32), axis=0),
        ]
    )
    grad_normed = matmul(grad_projected, qkv_w.T)
    grad_rows_part, grad_in_gain, grad_in_shift = norm_in_back(grad_normed)
    grad_source = (grad_middle + grad_rows_part).astype(jnp.bfloat16).reshape(source.shape)
    grad_terms = (
        grad_in_gain,
        grad_in_shift,
        grad_qkv_w,
        grad_qv_b,
        grad_proj_w,
        grad_proj_b,
        grad_mid_gain,
        grad_mid_shift,
        grad_fc1_w,
        grad_fc1_b,
        grad_fc2_w,
        grad_fc2_b,
    )
    return (output, grad_source, grad_terms, jnp.sum(bias_terms, axis=0))


def shards(
    clips,
    out_grad,
    clip_order,
    region_label,
    rel_index,
    norm1_gain,
    norm1_bias,
    qkv_weight,
    qv_bias,
    bias_table,
    proj_weight,
    proj_bias,
    norm2_gain,
    norm2_bias,
    fc1_weight,
    fc1_bias,
    fc2_weight,
    fc2_bias,
):
    clip_count = clips.shape[0] // MICRO
    slot_order = clip_order[0]
    keep_mask = region_label[:, :, None] == region_label[:, None, :]
    rel_bias = jnp.take(bias_table.astype(jnp.float32), rel_index, axis=1)
    shard_set = (
        norm1_gain,
        norm1_bias,
        qkv_weight,
        qv_bias,
        proj_weight,
        proj_bias,
        norm2_gain,
        norm2_bias,
        fc1_weight,
        fc1_bias,
        fc2_weight,
        fc2_bias,
    )
    grad_sums = tuple((jnp.zeros(weight_shard.shape, jnp.float32) for weight_shard in shard_set))
    bias_sum = jnp.zeros(rel_bias.shape, jnp.float32)
    outputs = []
    source_grads = []
    for micro_index in range(MICRO):
        picked_slots = lax.dynamic_slice_in_dim(slot_order, micro_index * clip_count, clip_count)
        source = jnp.take(clips, picked_slots, axis=0)
        cot_block = out_grad[micro_index * clip_count : (micro_index + 1) * clip_count]
        full_weights = (
            lax.all_gather(norm1_gain, ("dp", "seq"), axis=0, tiled=True),
            lax.all_gather(norm1_bias, ("dp", "seq"), axis=0, tiled=True),
            lax.all_gather(qkv_weight, ("dp", "seq"), axis=0, tiled=True),
            lax.all_gather(qv_bias, ("dp", "seq"), axis=1, tiled=True),
            lax.all_gather(proj_weight, ("dp", "seq"), axis=0, tiled=True),
            lax.all_gather(proj_bias, ("dp", "seq"), axis=0, tiled=True),
            lax.all_gather(norm2_gain, ("dp", "seq"), axis=0, tiled=True),
            lax.all_gather(norm2_bias, ("dp", "seq"), axis=0, tiled=True),
            lax.all_gather(fc1_weight, ("dp", "seq"), axis=0, tiled=True),
            lax.all_gather(fc1_bias, ("dp", "seq"), axis=0, tiled=True),
            lax.all_gather(fc2_weight, ("dp", "seq"), axis=0, tiled=True),
            lax.all_gather(fc2_bias, ("dp", "seq"), axis=0, tiled=True),
        )
        output, grad_source, grad_terms, bias_term = layer_pass(
            source, cot_block, full_weights, rel_bias, keep_mask
        )
        grad_terms = (
            lax.psum_scatter(grad_terms[0], ("dp", "seq"), scatter_dimension=0, tiled=True),
            lax.psum_scatter(grad_terms[1], ("dp", "seq"), scatter_dimension=0, tiled=True),
            lax.psum_scatter(grad_terms[2], ("dp", "seq"), scatter_dimension=0, tiled=True),
            lax.psum_scatter(grad_terms[3], ("dp", "seq"), scatter_dimension=1, tiled=True),
            lax.psum_scatter(grad_terms[4], ("dp", "seq"), scatter_dimension=0, tiled=True),
            lax.psum_scatter(grad_terms[5], ("dp", "seq"), scatter_dimension=0, tiled=True),
            lax.psum_scatter(grad_terms[6], ("dp", "seq"), scatter_dimension=0, tiled=True),
            lax.psum_scatter(grad_terms[7], ("dp", "seq"), scatter_dimension=0, tiled=True),
            lax.psum_scatter(grad_terms[8], ("dp", "seq"), scatter_dimension=0, tiled=True),
            lax.psum_scatter(grad_terms[9], ("dp", "seq"), scatter_dimension=0, tiled=True),
            lax.psum_scatter(grad_terms[10], ("dp", "seq"), scatter_dimension=0, tiled=True),
            lax.psum_scatter(grad_terms[11], ("dp", "seq"), scatter_dimension=0, tiled=True),
        )
        grad_sums = tuple((previous + fresh for previous, fresh in zip(grad_sums, grad_terms)))
        bias_sum = bias_sum + bias_term
        outputs.append(output)
        source_grads.append(grad_source)
    flat_terms = bias_sum.reshape(bias_sum.shape[0], -1).T
    table_terms = jax.ops.segment_sum(flat_terms, rel_index.reshape(-1), num_segments=TBL).T
    table_grad = lax.psum(table_terms, "dp")
    output_all = jnp.concatenate(outputs, axis=0)
    clips_grad = jnp.zeros_like(clips).at[slot_order].set(jnp.concatenate(source_grads, axis=0))
    return (
        output_all,
        clips_grad,
        grad_sums[0],
        grad_sums[1],
        grad_sums[2],
        grad_sums[3],
        table_grad,
        grad_sums[4],
        grad_sums[5],
        grad_sums[6],
        grad_sums[7],
        grad_sums[8],
        grad_sums[9],
        grad_sums[10],
        grad_sums[11],
    )


EPS = 1e-5
LOG2E = math.log2(math.e)
LN2 = math.log(2.0)
SCALE = HD**-0.5
MASKED = -1e30
bf = jnp.bfloat16
f32 = jnp.float32
i32 = jnp.int32
MESH = pl.DeviceIdType.MESH
VM = pltpu.VMEM
DMA = pltpu.SemaphoreType.DMA

CL = 2
NS = 4
RP = 400
RT = CL * RP
KP = 512
C = 512
NHEAD = 16
TA = 10
HR = 17
TB = 256
SHARD = (16, 16, 16, 64)
WIDTH = (1536, 512, 2048, 512)
PARTS = ((0, 4), (4, 3))


def nn(a, b):
    return jnp.dot(a, b, preferred_element_type=f32)


def nt(a, b):
    return lax.dot_general(a, b, (((1,), (1,)), ((), ())), preferred_element_type=f32)


def tn(a, b):
    return lax.dot_general(a, b, (((0,), (0,)), ((), ())), preferred_element_type=f32)


def norm_parts(v):
    mu = jnp.mean(v, axis=-1, keepdims=True)
    c = v - mu
    r = lax.rsqrt(jnp.mean(c * c, axis=-1, keepdims=True) + EPS)
    return c * r, r


class Place:
    def __init__(self):
        dp, self.z = lax.axis_index("dp"), lax.axis_index("seq")
        self.dp = dp
        self.y, self.x, self.c = dp // 4, (dp // 2) % 2, dp % 2
        self.yn, self.xn, self.cn = 1 - self.y, 1 - self.x, 1 - self.c
        self.over_x = (self.dp_of(self.y, self.xn, self.c), self.z)
        self.over_y = (self.dp_of(self.yn, self.x, self.c), self.z)
        self.core = (self.dp_of(self.y, self.x, self.cn), self.z)
        self.corner = (self.dp_of(self.yn, self.xn, self.c), self.z)
        self.block = dp * 4 + self.z
        self.z1 = self.z + 1 - 2 * lax.rem(self.z, 2)
        self.z2 = lax.rem(self.z + 2, NS)
        self.z3 = NS - 1 - self.z

    def dp_of(self, y, x, c):
        return y * 4 + x * 2 + c

    def seq(self, z):
        return (self.dp, z)

    def far(self, d):
        return lax.rem(self.z + d, NS)

    def greet(self):
        bar = pltpu.get_barrier_semaphore()
        self.peers = [self.seq(self.far(d)) for d in (1, 2, 3)]
        self.peers += [self.over_x, self.over_y, self.corner, self.core]
        for peer in self.peers:
            pl.semaphore_signal(bar, inc=1, device_id=peer, device_id_type=MESH)

    def met(self):
        pl.semaphore_wait(pltpu.get_barrier_semaphore(), len(self.peers))


def rcopy(src, dst, ssem, rsem, dev):
    return pltpu.make_async_remote_copy(
        src_ref=src, dst_ref=dst, send_sem=ssem, recv_sem=rsem, device_id=dev, device_id_type=MESH
    )


def take(ref, sem):
    pltpu.make_async_copy(ref, ref, sem).wait()


def window_start(w, part):
    return lax.rem(7 * w + SHIFT_S + part, SIDE)


def send_windows(me, c, src, dst, ssem, rsem, lsem):
    slot = lax.rem(me.z + 2, NS)
    for d in range(NS):
        w = me.far(d)
        wy, wx = w // 2, lax.rem(w, 2)
        for y7, ny in PARTS:
            for x7, nx in PARTS:
                a = src.at[c, pl.ds(window_start(wy, y7), ny), pl.ds(window_start(wx, x7), nx)]
                b = dst.at[c, slot, pl.ds(y7, ny), pl.ds(x7, nx)]
                if d == 0:
                    pltpu.make_async_copy(a, b, lsem.at[c]).start()
                else:
                    rcopy(a, b, ssem.at[c, d - 1], rsem.at[c, d - 1], me.seq(w)).start()


def take_windows(me, c, dst, ssem, rsem, lsem):
    for d in range(NS):
        part = dst.at[c, lax.rem(me.z + NS - d + 2, NS)]
        if d == 0:
            take(part, lsem.at[c])
        else:
            take(part, rsem.at[c, d - 1])
            take(part, ssem.at[c, d - 1])


def send_home(me, src, dst, ssem, rsem, lsem):
    wy, wx = me.z // 2, lax.rem(me.z, 2)
    for d in range(NS):
        t = me.far(d)
        slot = lax.rem(t + 2, NS)
        for c in range(CL):
            for y7, ny in PARTS:
                for x7, nx in PARTS:
                    a = src.at[c, slot, pl.ds(y7, ny), pl.ds(x7, nx)]
                    b = dst.at[c, pl.ds(window_start(wy, y7), ny), pl.ds(window_start(wx, x7), nx)]
                    if d == 0:
                        pltpu.make_async_copy(a, b, lsem).start()
                    else:
                        rcopy(a, b, ssem.at[d - 1], rsem.at[d - 1], me.seq(t)).start()


def take_home(me, src, ssem, rsem, lsem):
    take(src.at[:, 0], lsem)
    for d in (1, 2, 3):
        take(src.at[:, 0], rsem.at[d - 1])
        take(src.at[:, 0], ssem.at[d - 1])


class Gather:
    def __init__(self, me, k, shard, full, zsem, ssem, rsem):
        self.me, self.shard, self.full, self.r = me, shard, full, SHARD[k]
        self.zsem, self.ssem, self.rsem = zsem.at[k], ssem.at[k], rsem.at[k]

    def rows(self, dp, first=0, count=NS):
        return self.full.at[pl.ds(pl.multiple_of((dp * NS + first) * self.r, self.r), count * self.r)]

    def push(self, ref, slot, dev, sem=None):
        rcopy(ref, ref, self.ssem if sem is None else sem, self.rsem.at[slot], dev).start()

    def spread(self, z):
        block = self.rows(self.me.dp, z, 1)
        self.push(block, 4 + z, self.me.over_x)
        self.push(block, 8 + z, self.me.over_y)
        self.push(block, 16 + z, self.me.core)

    def fill(self):
        self.full[pl.ds(pl.multiple_of(self.me.block * self.r, self.r), self.r), :] = self.shard[...]

    def start(self):
        me = self.me
        self.spread(me.z)
        for z in (me.z2, me.z1):
            self.push(self.rows(me.dp, me.z, 1), me.z, me.seq(z), self.zsem)

    def came(self, z):
        take(self.rows(self.me.dp, z, 1), self.rsem.at[z])

    def step1(self):
        me = self.me
        self.came(me.z2)
        self.push(self.rows(me.dp, me.z2, 1), me.z2, me.seq(me.z1), self.zsem)
        self.spread(me.z2)

    def step2(self):
        for z in (self.me.z1, self.me.z3):
            self.came(z)
            self.spread(z)

    def corner(self):
        me = self.me
        dx, dy = me.over_x[0], me.over_y[0]
        for z in range(NS):
            take(self.rows(dx, z, 1), self.rsem.at[4 + z])
            if z < 2:
                self.push(self.rows(dx, z, 1), 12 + z, me.over_y)
        self.push(self.rows(dx), 20, me.core)
        for z in range(NS):
            take(self.rows(dy, z, 1), self.rsem.at[8 + z])
            if z >= 2:
                self.push(self.rows(dy, z, 1), 12 + z, me.over_x)
        self.push(self.rows(dy), 21, me.core)

    def last(self):
        me = self.me
        dd = me.dp_of(me.yn, me.xn, me.c)
        for z in range(NS):
            take(self.rows(dd, z, 1), self.rsem.at[12 + z])
        self.push(self.rows(dd), 22, me.core)

    def finish(self):
        me = self.me
        for z in range(NS):
            take(self.rows(me.dp_of(me.y, me.x, me.cn), z, 1), self.rsem.at[16 + z])
        for slot, (y, x) in ((20, (me.y, me.xn)), (21, (me.yn, me.x)), (22, (me.yn, me.xn))):
            take(self.rows(me.dp_of(y, x, me.cn)), self.rsem.at[slot])
        take(self.full.at[pl.ds(0, 3 * self.r)], self.zsem)
        take(self.full.at[pl.ds(0, 28 * self.r)], self.ssem)


class DirectGather(Gather):
    def spread(self, z):
        super().spread(z)
        self.push(self.rows(self.me.dp, z, 1), 12 + z, self.me.corner)

    def groups(self):
        me = self.me
        for n, device in enumerate((me.over_x, me.over_y, me.corner)):
            for z in range(NS):
                take(self.rows(device[0], z, 1), self.rsem.at[(4, 8, 12)[n] + z])
            self.push(self.rows(device[0]), 20 + n, me.core)


class Vectors:
    def __init__(self, me, full, ssem, rsem):
        self.me, self.full, self.ssem, self.rsem = me, full, ssem, rsem

    def rows(self, dp, first=0, count=NS):
        return self.full.at[pl.ds(dp * NS + first, count)]

    def push(self, ref, slot, dev):
        rcopy(ref, ref, self.ssem.at[slot], self.rsem.at[slot], dev).start()

    def start(self):
        me = self.me
        for d in (1, 2, 3):
            self.push(self.rows(me.dp, me.z, 1), d - 1, me.seq(me.far(d)))

    def plane(self):
        me = self.me
        for d in (1, 2, 3):
            take(self.rows(me.dp, me.far(NS - d), 1), self.rsem.at[d - 1])
        for slot, dev in ((3, me.over_x), (4, me.over_y), (5, me.core)):
            self.push(self.rows(me.dp), slot, dev)

    def diagonal(self):
        me = self.me
        dx, dy = me.over_x[0], me.over_y[0]
        take(self.rows(dx), self.rsem.at[3])
        self.push(self.rows(dx), 6, me.over_y)
        self.push(self.rows(dx), 8, me.core)
        take(self.rows(dy), self.rsem.at[4])
        self.push(self.rows(dy), 9, me.core)

    def last(self):
        me = self.me
        dd = me.dp_of(me.yn, me.xn, me.c)
        take(self.rows(dd), self.rsem.at[6])
        self.push(self.rows(dd), 10, me.core)

    def finish(self):
        me = self.me
        for slot, (y, x) in ((5, (me.y, me.x)), (8, (me.y, me.xn)), (9, (me.yn, me.x)), (10, (me.yn, me.xn))):
            take(self.rows(me.dp_of(y, x, me.cn)), self.rsem.at[slot])
        for slot in (0, 1, 2, 3, 4, 5, 6, 8, 9, 10):
            take(self.rows(0, 0, 1) if slot < 3 else self.rows(0), self.ssem.at[slot])


def pack_vectors(me, sv, g1, b1, qv, pb, g2, b2, b3, b4):
    row = jnp.zeros((1, 256), f32)
    sv[pl.ds(me.block, 1), 0] = row
    pieces = (g1[...], b1[...], qv[0:1, :], qv[1:2, :], pb[...], g2[...], b2[...], b4[...])
    for k, piece in enumerate(pieces):
        sv[pl.ds(me.block, 1), 0, 16 * k : 16 * k + 16] = piece.astype(f32)
    sv[pl.ds(me.block, 1), 0, 128:192] = b3[...].astype(f32)


def spread_vectors(sv, vec):
    v = sv[...].reshape(32, 256).astype(bf)
    lane = lax.broadcasted_iota(i32, (256, C), 1)
    row = lax.broadcasted_iota(i32, (256, C), 0)
    blk = lax.broadcasted_iota(i32, (32, C), 0)
    col = lax.broadcasted_iota(i32, (32, C), 1)
    for k in range(12):
        if k < 8:
            pick, own = row == 16 * k + (lane & 15), blk == (col >> 4)
        else:
            pick, own = row == 128 + (lane & 63), blk == (col >> 6) + 8 * (k - 8)
        y = nn(v, jnp.where(pick, 1.0, 0.0).astype(bf))
        vec[k : k + 1, :] = jnp.sum(jnp.where(own, y, 0.0), axis=0, keepdims=True)


def one_hot(lo, i):
    d = jnp.broadcast_to(lo[pl.ds(i, 1), :], (16, KP)).astype(bf)
    d = d - lax.broadcasted_iota(i32, (16, KP), 0).astype(f32).astype(bf)
    one, zero = jnp.asarray(1, bf), jnp.asarray(0, bf)
    return jnp.concatenate([jnp.where(d == jnp.asarray(16 * c, bf), one, zero) for c in range(16)], axis=0)


def order_index(me, idx, lab, perm, hi, lo, colb, lrow):
    p = perm[...]
    iv = idx[...]
    for dst, part in ((hi, iv >> 8), (lo, iv & 255)):
        rows = nn(p[0:RP, :], part.astype(f32).astype(bf)).astype(bf)
        dst[...] = nt(rows, p)
    own = lab[pl.ds(me.z, 1), :].astype(f32)
    own = jnp.broadcast_to(own, (8, WT)).astype(bf)
    lane = lax.broadcasted_iota(i32, (8, KP), 1)
    lrow[...] = jnp.where(lane < WT, nt(own, p), -1.0)
    colb[...] = jnp.broadcast_to(nt(p[0:RP, :], own)[:, 0:1], (RP, 128))


def table_rows(tbl, tab):
    whole = jnp.concatenate([tbl[s].astype(f32) for s in range(NS)], axis=0)
    for a in range(TA):
        tab[a * 16 : (a + 1) * 16, :] = whole[:, a * TB : (a + 1) * TB].astype(bf)


def gather_rows(first, count, tab, hi, lo, colb, lrow, bias):
    unroll = 20

    def body(t, _):
        for u in range(unroll):
            i = first + t * unroll + u
            y = nn(tab[...], one_hot(lo, i))
            high = jnp.broadcast_to(hi[pl.ds(i, 1), :], (16, KP))
            acc = jnp.zeros((16, KP), f32)
            for a in range(TA):
                acc = jnp.where(high == a, y[a * 16 : (a + 1) * 16], acc)
            acc = acc * LOG2E
            own = colb[pl.ds(i, 1), :]
            r0 = i * HR
            for j in range(4):
                keep = lrow[0:1, j * 128 : (j + 1) * 128] == own
                bias[j, pl.ds(r0, 16), :] = jnp.where(keep, acc[:, j * 128 : (j + 1) * 128], MASKED)
        return 0

    lax.fori_loop(0, count // unroll, body, 0)


def scatter_rows(first, count, g, other, hi, lo, total):
    unroll = 10
    zero = jnp.asarray(0, bf)

    def body(t, _):
        ls, rs = [], []
        for u in range(unroll):
            n = t * unroll + u
            i = first + n
            rs.append(one_hot(lo, i))
            high = jnp.broadcast_to(hi[pl.ds(i, 1), :], (16, KP)).astype(bf)
            own = jnp.concatenate([g[j, pl.ds(i * HR, 16), :] for j in range(4)], axis=1)
            own = (own + other[pl.ds(pl.multiple_of(n * 16, 16), 16), :].astype(f32)).astype(bf)
            ls.append(jnp.concatenate([jnp.where(high == jnp.asarray(a, bf), own, zero) for a in range(TA)], axis=0))
        total[...] += nt(jnp.concatenate(rs, axis=1), jnp.concatenate(ls, axis=1))
        return 0

    lax.fori_loop(0, count // unroll, body, 0)


def load_tokens(src, clip, dst, p):
    for s in range(NS):
        v = src[clip, s].astype(f32).reshape(98, C)
        dst[p * RP + s * 98 : p * RP + (s + 1) * 98, :] = v.astype(dst.dtype)
    dst[p * RP + WT : (p + 1) * RP, :] = jnp.zeros((RP - WT, C), dst.dtype)


def store_tokens(src, clip, dst, slot):
    for s in range(NS):
        v = src[clip, s * 98 : (s + 1) * 98, :]
        dst[slot, s] = v.reshape(49, 2, C).astype(bf).reshape(7, 7, 2, C)


def qkv_phase(p, x, vec, wq, n1, q, k, v):
    r = slice(p * RP, (p + 1) * RP)
    k[p, RP:KP, :] = jnp.zeros((KP - RP, C), bf)
    v[p, RP:KP, :] = jnp.zeros((KP - RP, C), bf)
    n, _ = norm_parts(x[r, :].astype(f32))
    y = (n * vec[0:1, :] + vec[1:2, :]).astype(bf)
    n1[r, :] = y
    q[r, :] = ((nn(y, wq[:, 0:C]) + vec[2:3, :]) * (SCALE * LOG2E)).astype(bf)
    k[p, 0:RP, :] = nn(y, wq[:, C : 2 * C]).astype(bf)
    v[p, 0:RP, :] = (nn(y, wq[:, 2 * C : 3 * C]) + vec[3:4, :]).astype(bf)


def attention_forward(p, q, k, v, bias, e, att, inv, poll):
    lane = lax.broadcasted_iota(i32, (1, 128), 1) // HD

    def body(quad, _):
        l0 = pl.multiple_of(quad * 128, 128)
        r = slice(p * RP, (p + 1) * RP)
        qq = q[r, pl.ds(l0, 128)]
        kk = k[p, :, pl.ds(l0, 128)]
        vv = v[p, :, pl.ds(l0, 128)]
        acc = sums = jnp.zeros((RP, 128), f32)
        for hq in range(4):
            h = quad * 4 + hq
            s = nt(qq, jnp.where(lane == hq, kk, jnp.zeros_like(kk)))
            s = s + jnp.concatenate([bias[j, pl.ds(h, RP, stride=HR), :] for j in range(4)], axis=1)
            w = jnp.exp2(s - jnp.max(s, axis=1, keepdims=True)).astype(bf)
            e[p, h] = w
            o = nn(w, jnp.where(lane == hq, vv, jnp.ones_like(vv)))
            acc = jnp.where(lane == hq, o, acc)
            sums = jnp.where(lane == (hq + 1) % 4, o, sums)
        ainv = 1.0 / pltpu.roll(sums, 128 - HD, 1)
        att[r, pl.ds(l0, 128)] = (acc * ainv).astype(bf)
        inv[r, pl.ds(l0, 128)] = ainv
        poll(quad)
        return 0

    lax.fori_loop(0, 4, body, 0)


def feed_forward(x, att, vec, wp, w1, w2, nm, mid, out, keep):
    for p in range(CL):
        r = slice(p * RP, (p + 1) * RP)
        m = x[r, :].astype(f32) + nn(att[r, :], wp[...]) + vec[4:5, :]
        mid[r, :] = m
        n, _ = norm_parts(m)
        nm[r, :] = (n * vec[5:6, :] + vec[6:7, :]).astype(bf)
        out[p] = m + vec[7:8, :]

    def body(c, _):
        c0 = pl.multiple_of(c * C, C)
        for p in range(CL):
            r = slice(p * RP, (p + 1) * RP)
            hid = nn(nm[r, :], w1[:, pl.ds(c0, C)]) + vec[pl.ds(8 + c, 1), :]
            density = jnp.exp2(hid * hid * (-0.5 * LOG2E)) * (1 / math.sqrt(2 * math.pi))
            phi = 0.5 * (1.0 + lax.erf(hid * (1 / math.sqrt(2.0))))
            act = (hid * phi).astype(bf)
            slope = phi + hid * density
            out[p] += nn(act, w2[pl.ds(c0, C), :])
            for j in range(4):
                t = slice(j * 128, (j + 1) * 128)
                keep[c, j * RT + p * RP : j * RT + (p + 1) * RP, :] = slope[:, t]
                keep[c, (4 + j) * RT + p * RP : (4 + j) * RT + (p + 1) * RP, :] = act[:, t].astype(f32)
        return 0

    lax.fori_loop(0, 4, body, 0)


def feed_backward(dy, w1, w2, nm, acc, gvec, keep, poll):
    acc[...] = jnp.zeros_like(acc)
    gvec[7:8, :] = jnp.sum(dy[...].astype(f32), axis=0, keepdims=True)

    def body(c, _):
        c0 = pl.multiple_of(c * C, C)
        g1 = g2 = gb = None
        for p in range(CL):
            r = slice(p * RP, (p + 1) * RP)

            def kept(n):
                return jnp.concatenate(
                    [keep[c, (n + j) * RT + p * RP : (n + j) * RT + (p + 1) * RP, :] for j in range(4)], axis=1
                )

            dh = (nt(dy[r, :], w2[pl.ds(c0, C), :]) * kept(0)).astype(bf)
            acc[p] += nt(dh, w1[:, pl.ds(c0, C)])
            act = kept(4).astype(bf)
            a2, a1, ab = tn(act, dy[r, :]), tn(nm[r, :], dh), jnp.sum(dh.astype(f32), axis=0, keepdims=True)
            g2, g1, gb = (a2, a1, ab) if p == 0 else (g2 + a2, g1 + a1, gb + ab)
        gvec[pl.ds(8 + c, 1), :] = gb
        w2[pl.ds(c0, C), :] = g2.astype(bf)
        w1[:, pl.ds(c0, C)] = g1.astype(bf)
        poll(c)
        return 0

    lax.fori_loop(0, 4, body, 0)


def middle_backward(dy, att, vec, wp, mid, acc, inv, gvec, do):
    s4 = s5 = s6 = jnp.zeros((1, C), f32)
    parts = []
    for p in range(CL):
        r = slice(p * RP, (p + 1) * RP)
        n, rr = norm_parts(mid[r, :])
        gmn = acc[p]
        s5 += jnp.sum(gmn * n, axis=0, keepdims=True)
        s6 += jnp.sum(gmn, axis=0, keepdims=True)
        g = gmn * vec[5:6, :]
        gm = dy[r, :].astype(f32) + rr * (
            g - jnp.mean(g, axis=-1, keepdims=True) - n * jnp.mean(g * n, axis=-1, keepdims=True)
        )
        mid[r, :] = gm
        gb = gm.astype(bf)
        s4 += jnp.sum(gb.astype(f32), axis=0, keepdims=True)
        parts.append(gb)
        low = (nt(gb, wp[...]) * inv[r, :]).astype(bf)
        do[r, :] = low
        acc[p] = low.astype(f32) * att[r, :].astype(f32)
    gvec[4:5, :] = s4
    gvec[5:6, :] = s5
    gvec[6:7, :] = s6
    wp[...] = tn(att[...], jnp.concatenate(parts, axis=0)).astype(bf)


def attention_backward(q, k, v, e, do, prod, g, dq, dk, dv, poll):
    lane = lax.broadcasted_iota(i32, (1, 128), 1) // HD

    def body(quad, _):
        l0 = pl.multiple_of(quad * 128, 128)
        dqs = [jnp.zeros((RP, 128), f32) for _ in range(CL)]
        dks, dvs = [[], []], [[], []]
        qts = [q[p * RP : (p + 1) * RP, pl.ds(l0, 128)].T for p in range(CL)]
        dots = [do[p * RP : (p + 1) * RP, pl.ds(l0, 128)].T for p in range(CL)]
        for hq in range(4):
            h = quad * 4 + hq
            f = slice(hq * HD, (hq + 1) * HD)
            both = None
            for p in range(CL):
                r = slice(p * RP, (p + 1) * RP)
                kk = k[p, :, pl.ds(l0, 128)]
                vv = v[p, :, pl.ds(l0, 128)]
                dp = nt(do[r, pl.ds(l0, 128)], jnp.where(lane == hq, vv, jnp.zeros_like(vv)))
                inner = jnp.sum(jnp.where(lane == hq, prod[p, :, pl.ds(l0, 128)], 0.0), axis=1, keepdims=True)
                w = e[p, h]
                ds = w.astype(f32) * (dp - inner)
                both = ds if both is None else both + ds
                low = ds.astype(bf)
                dqs[p] = dqs[p] + nn(low, jnp.where(lane == hq, kk, jnp.zeros_like(kk)))
                dks[p].append((nn(qts[p][f], low) * LN2).astype(bf))
                dvs[p].append(nn(dots[p][f], w).astype(bf))
            for j in range(4):
                g[j, pl.ds(h, RP, stride=HR), :] = both[:, j * 128 : (j + 1) * 128]
            if hq == 1:
                poll(quad, 0)
        for p in range(CL):
            r = slice(p * RP, (p + 1) * RP)
            dq[r, pl.ds(l0, 128)] = (dqs[p] * SCALE).astype(bf)
            dk[r, pl.ds(l0, 128)] = jnp.concatenate(dks[p], axis=0).T[0:RP]
            dv[p, 0:RP, pl.ds(l0, 128)] = jnp.concatenate(dvs[p], axis=0).T[0:RP]
        poll(quad, 1)
        return 0

    lax.fori_loop(0, 4, body, 0)


def input_backward(x, n1, vec, wq, dq, dk, dv, mid, dx, gvec):
    s0 = s1 = s3 = jnp.zeros((1, C), f32)
    gvec[2:3, :] = jnp.sum(dq[...].astype(f32), axis=0, keepdims=True)
    for p in range(CL):
        r = slice(p * RP, (p + 1) * RP)
        dvp = dv[p, 0:RP, :]
        s3 += jnp.sum(dvp.astype(f32), axis=0, keepdims=True)
        gn = nt(dq[r, :], wq[:, 0:C]) + nt(dk[r, :], wq[:, C : 2 * C]) + nt(dvp, wq[:, 2 * C : 3 * C])
        n, rr = norm_parts(x[r, :].astype(f32))
        s0 += jnp.sum(gn * n, axis=0, keepdims=True)
        s1 += jnp.sum(gn, axis=0, keepdims=True)
        g = gn * vec[0:1, :]
        dx[p] = mid[r, :] + rr * (
            g - jnp.mean(g, axis=-1, keepdims=True) - n * jnp.mean(g * n, axis=-1, keepdims=True)
        )
    gvec[0:1, :] = s0
    gvec[1:2, :] = s1
    gvec[3:4, :] = s3
    n1t = n1[...].T
    wq[:, 0:C] = nn(n1t, dq[...]).astype(bf)
    wq[:, C : 2 * C] = nn(n1t, dk[...]).astype(bf)
    dva = jnp.concatenate([dv[p, 0:RP, :] for p in range(CL)], axis=0)
    wq[:, 2 * C : 3 * C] = nn(n1t, dva).astype(bf)


class Reduce:
    def __init__(self, me, k, grad, out, ssem, rsem, rc, rx, ry, ra, rz):
        self.me, self.r, self.grad, self.out = me, SHARD[k], grad, out
        self.u = 4 * self.r
        self.h = self.u // 2
        self.ssem, self.rsem = ssem.at[k], rsem.at[k]
        self.rc, self.rx, self.ry, self.ra, self.rz = rc, rx, ry, ra, rz

    def own(self, y, x, c, first=0, count=None):
        return pl.ds(pl.multiple_of(self.me.dp_of(y, x, c) * self.u + first, self.r), self.u if count is None else count)

    def send(self, rows, dst, slot, dev):
        rcopy(self.grad.at[rows], dst, self.ssem.at[slot], self.rsem.at[slot], dev).start()

    def add(self, rows, part, slot):
        take(part, self.rsem.at[slot])
        self.grad[rows, :] = self.grad[rows, :] + part[...]

    def core_part(self, g):
        self.send(self.own(g // 2, g % 2, self.me.cn), self.rc.at[g], g, self.me.core)

    def cores(self):
        for g in range(4):
            self.core_part(g)

    def plane(self):
        me, h = self.me, self.h
        for g in range(4):
            self.add(self.own(g // 2, g % 2, me.c), self.rc.at[g], g)
        for n in range(2):
            self.send(self.own(n, me.xn, me.c, 0, h), self.rx.at[n], 4 + n, me.over_x)
            self.send(self.own(me.yn, n, me.c, h, h), self.ry.at[n], 6 + n, me.over_y)

    def plane_part(self, g):
        me, h = self.me, self.h
        y, x = g // 2, g % 2
        self.add(self.own(y, x, me.c), self.rc.at[g], g)

        def over_x():
            self.send(self.own(y, x, me.c, 0, h), self.rx.at[y], 4 + y, me.over_x)

        def over_y():
            self.send(self.own(y, x, me.c, h, h), self.ry.at[x], 6 + x, me.over_y)

        pl.when(x == me.xn)(over_x)
        pl.when(y == me.yn)(over_y)

    def corner(self):
        me, h = self.me, self.h
        for n in range(2):
            self.add(self.own(n, me.x, me.c, 0, h), self.rx.at[n], 4 + n)
            self.add(self.own(me.y, n, me.c, h, h), self.ry.at[n], 6 + n)
        self.send(self.own(me.yn, me.x, me.c, 0, h), self.ra.at[0], 8, me.over_y)
        self.send(self.own(me.y, me.xn, me.c, h, h), self.ra.at[1], 9, me.over_x)

    def line(self):
        me, h, r = self.me, self.h, self.r
        for n in range(2):
            self.add(self.own(me.y, me.x, me.c, n * h, h), self.ra.at[n], 8 + n)
        for n, z in enumerate((me.z1, me.z3)):
            self.send(self.own(me.y, me.x, me.c, z * r, r), self.rz.at[n], 10 + n, me.seq(me.z1))

    def across(self):
        me, r = self.me, self.r
        rows = self.own(me.y, me.x, me.c, me.z2 * r, r)
        self.add(rows, self.rz.at[1], 11)
        self.send(rows, self.rz.at[2], 12, me.seq(me.z2))

    def finish(self):
        me, r, u, h = self.me, self.r, self.u, self.h
        total = self.grad[self.own(me.y, me.x, me.c, me.z * r, r), :].astype(f32)
        for n, slot in ((0, 10), (2, 12)):
            take(self.rz.at[n], self.rsem.at[slot])
            total = total + self.rz[n].astype(f32)
        self.out[...] = total
        for slot in range(13):
            count = u if slot < 4 else h if slot < 10 else r
            take(self.grad.at[pl.ds(0, count)], self.ssem.at[slot])


SEG = 40
SEGS = RP // 2 // SEG


def block_kernel(
    order, clips, cot, sq, sp, s1, s2, g1, b1, qv, pb, g2, b2, b3, b4, table, lab, idx, perm,
    out_t, dx_t, oq, op, o1, o2, og1, ob1, oqv, opb, og2, ob2, ob3, ob4, otab,
    bg, e, wq, wp, w1, w2, xw, dyw, x, dy, n1, q, k, v, att, inv, nm, mid, out, do,
    hi, lo, sv, tbl, tblb, tab, colb, lrow, vec, gvec, total, tz, tx, vz, vx,
    *rest,
):
    parts = [rest[5 * n : 5 * n + 5] for n in range(4)]
    (xs, xr, xl, ds_, dr, dl, os_, or_, ol, hs, hr, hl, wz, ws, wr, vs, vr, ts, tr, bs, br, free, es, er,
     rs, rr, zs, zr, as_, ar) = rest[20:]
    me = Place()
    me.greet()
    weights = [
        kind(me, n, shard, full, wz, ws, wr)
        for n, (kind, shard, full) in enumerate(
            ((DirectGather, sq, wq), (Gather, sp, wp), (Gather, s1, w1), (Gather, s2, w2))
        )
    ]
    first, later = weights[0], weights[1:]
    for w in weights:
        w.fill()
    pack_vectors(me, sv, g1, b1, qv, pb, g2, b2, b3, b4)
    tblb[pl.ds(me.z, 1), :, 2432:2560] = jnp.zeros((1, 4, 128), bf)
    tblb[pl.ds(me.z, 1), :, 0:TBL] = table[...][None]
    vectors = Vectors(me, sv, vs, vr)
    order_index(me, idx, lab, perm, hi, lo, colb, lrow)
    me.met()
    for d in (1, 2, 3):
        own = tblb.at[me.z]
        rcopy(own, own, ts.at[d - 1], tr.at[d - 1], me.seq(me.far(d))).start()
    first.start()
    vectors.start()
    send_windows(me, 0, clips, xw, xs, xr, xl)
    for w in later:
        w.start()
    for d in (1, 2, 3):
        take(tblb.at[0], tr.at[d - 1])
        take(tblb.at[0], ts.at[d - 1])
    table_rows(tblb, tab)

    def bias_rows(n, half):
        return bg.at[:, pl.ds(pl.multiple_of((half * SEGS + n) * SEG * HR, 8), SEG * HR)]

    def rows(n):
        gather_rows((me.c * SEGS + n) * SEG, SEG, tab, hi, lo, colb, lrow, bg)
        part = bias_rows(n, me.c)
        rcopy(part, part, bs.at[n], br.at[n], me.core).start()

    rows(0)
    first.step1()
    first.step2()
    vectors.plane()
    rows(1)
    vectors.diagonal()
    rows(2)
    first.groups()
    vectors.last()
    rows(3)
    vectors.finish()
    spread_vectors(sv, vec)
    rows(4)
    first.finish()

    def first_poll(quad):
        def second():
            for w in later:
                w.step2()

        pl.when(quad == 2)(second)

    def second_poll(quad):
        def last():
            for w in later:
                w.last()

        pl.when(quad == 1)(last)

    for p, poll in enumerate((first_poll, second_poll)):
        if p == 1:
            for w in later:
                w.corner()
        take_windows(me, p, xw, xs, xr, xl)
        if p == 0:
            for w in later:
                w.step1()
            send_windows(me, 1, clips, xw, xs, xr, xl)
            for c in range(CL):
                send_windows(me, c, cot, dyw, ds_, dr, dl)
        load_tokens(xw, p, x, p)
        qkv_phase(p, x, vec, wq, n1, q, k, v)
        if p == 0:
            for n in range(SEGS):
                take(bias_rows(n, me.cn), br.at[n])
                take(bias_rows(n, me.c), bs.at[n])
        attention_forward(p, q, k, v, bg, e, att, inv, poll)
    gvec[...] = jnp.zeros_like(gvec)
    for w in later:
        w.finish()
    feed_forward(x, att, vec, wp, w1, w2, nm, mid, out, bg)
    for p in range(CL):
        store_tokens(out, order[0, p], xw, p)
    send_home(me, xw, out_t, os_, or_, ol)
    reds = [
        Reduce(me, n, grad, total_out, rs, rr, *parts[n])
        for n, (grad, total_out) in enumerate(((wq, oq), (wp, op), (w1, o1), (w2, o2)))
    ]
    for p in range(CL):
        take_windows(me, p, dyw, ds_, dr, dl)
    for p in range(CL):
        load_tokens(dyw, order[0, p], dy, p)

    def chunk_poll(c):
        reds[3].core_part(c)
        pl.when(c > 0)(lambda: reds[3].plane_part(c - 1))

    feed_backward(dy, w1, w2, nm, out, gvec, bg, chunk_poll)
    reds[2].cores()
    reds[3].plane_part(3)
    middle_backward(dy, att, vec, wp, mid, out, inv, gvec, do)
    reds[1].cores()
    reds[3].corner()
    reds[2].plane()

    def backward_poll(quad, half):
        def both(name):
            for n in (2, 1):
                getattr(reds[n], name)()

        steps = ((0, reds[1].plane), (2, reds[3].line), (4, reds[3].across))
        steps += ((5, lambda: both("corner")), (7, lambda: both("line")))
        for n, step in steps:
            if half == n % 2:
                pl.when(quad == n // 2)(step)

    attention_backward(q, k, v, e, do, out, bg, nm, att, v, backward_poll)
    pl.semaphore_signal(free, inc=1, device_id=me.core, device_id_type=MESH)
    input_backward(x, n1, vec, wq, nm, att, v, mid, out, gvec)
    reds[0].cores()
    for d in (1, 2, 3):
        rcopy(gvec, vz.at[d - 1], zs.at[d - 1], zr.at[d - 1], me.seq(me.far(d))).start()
    for n in (2, 1):
        reds[n].across()
    for p in range(CL):
        store_tokens(out, p, dyw, p)
    send_home(me, dyw, dx_t, hs, hr, hl)
    halves = ((0, SEG * 8), (1, SEG * 8))
    for n in range(SEGS):

        def lower(i, _, n=n):
            for m in range(2):
                for u in range(2):
                    at = m * SEG // 2 + u * SEG // 4 + i
                    r0 = ((me.cn * SEGS + n) * SEG + at) * HR
                    row = jnp.concatenate([bg[j, pl.ds(r0, 16), :] for j in range(4)], axis=1)
                    e[1, 2 * n + m, pl.ds(pl.multiple_of((u * SEG // 4 + i) * 16, 16), 16), :] = row.astype(bf)
            return 0

        lax.fori_loop(0, SEG // 4, lower, 0)
        if n == 0:
            pl.semaphore_wait(free, 1)
        for m, count in halves:
            rcopy(
                e.at[1, 2 * n + m, pl.ds(0, count)], e.at[0, 2 * n + m, pl.ds(0, count)],
                es.at[2 * n + m], er.at[2 * n + m], me.core,
            ).start()
    total[...] = jnp.zeros_like(total)

    def scatter(n):
        for m, count in halves:
            take(e.at[0, 2 * n + m, pl.ds(0, count)], er.at[2 * n + m])
        first = (me.c * SEGS + n) * SEG
        for m in range(2):
            scatter_rows(first + m * SEG // 2, SEG // 2, bg, e.at[0, 2 * n + m], hi, lo, total)

    scatter(0)
    reds[0].plane()
    scatter(1)
    scatter(2)
    reds[0].corner()
    scatter(3)
    reds[0].line()
    scatter(4)
    sums = total[...].T
    for a in range(TA):
        for s in range(NS):
            tbl[s, :, a * TB : (a + 1) * TB] = sums[a * 16 + 4 * s : a * 16 + 4 * s + 4, :]
    tblb[...] = tbl[...].astype(bf)
    for d in (1, 2, 3):
        rcopy(tblb.at[me.far(d)], tz.at[d - 1], zs.at[2 + d], zr.at[2 + d], me.seq(me.far(d))).start()
    reds[0].across()
    table = tbl[pl.ds(me.z, 1)].reshape(4, TA * TB)
    vecs = gvec[...]
    for d in (1, 2, 3):
        take(vz.at[d - 1], zr.at[d - 1])
        vecs = vecs + vz[d - 1]
    for n in (2, 3, 1):
        reds[n].finish()
    for d in (1, 2, 3):
        take(tz.at[d - 1], zr.at[2 + d])
        table = table + tz[d - 1].astype(f32)
    for n, dev in enumerate((me.core, me.over_x, me.over_y)):
        tx[2 * n] = table
        vx[2 * n] = vecs
        rcopy(tx.at[2 * n], tx.at[2 * n + 1], as_.at[2 * n], ar.at[2 * n], dev).start()
        rcopy(vx.at[2 * n], vx.at[2 * n + 1], as_.at[2 * n + 1], ar.at[2 * n + 1], dev).start()
        take(tx.at[2 * n + 1], ar.at[2 * n])
        take(vx.at[2 * n + 1], ar.at[2 * n + 1])
        table = table + tx[2 * n + 1]
        vecs = vecs + vx[2 * n + 1]
    otab[...] = table
    vx[6] = vecs
    part = pltpu.roll(vecs[0:8, :], C - me.block * 16, 1)
    for row, ref in ((0, og1), (1, ob1), (4, opb), (5, og2), (6, ob2), (7, ob4)):
        ref[...] = part[row : row + 1, 0:16]
    oqv[...] = part[2:4, 0:16]
    wide = jnp.broadcast_to(vx[6, pl.ds(8 + me.block // 8, 1), :], (8, C))
    ob3[...] = pltpu.roll(wide, C - lax.rem(me.block, 8) * 64, 1)[0:1, 0:64]
    reds[0].finish()
    for n in range(SEGS):
        for m, count in halves:
            take(e.at[1, 2 * n + m, pl.ds(0, count)], es.at[2 * n + m])
    for n in range(3):
        take(tx.at[0], as_.at[2 * n])
        take(vx.at[0], as_.at[2 * n + 1])
        take(vz.at[0], zs.at[n])
        take(tz.at[0], zs.at[3 + n])
    take_home(me, xw, os_, or_, ol)
    take_home(me, dyw, hs, hr, hl)


def publish_kernel(*refs):
    n = len(refs) // 2
    for source, target in zip(refs[:n], refs[n:]):
        target[...] = source[...]


def windowed(
    clips, out_grad, clip_order, region_label, rel_index, norm1_gain, norm1_bias, qkv_weight, qv_bias,
    bias_table, proj_weight, proj_bias, norm2_gain, norm2_bias, fc1_weight, fc1_bias, fc2_weight, fc2_bias,
):
    at = np.arange(WT)
    canonical = (2 * (at // 98) + at % 2) * 49 + (at % 98) // 2
    perm = np.zeros((KP, WT), np.float32)
    perm[at, canonical] = 1
    perm = jnp.asarray(perm, bf)
    field = lambda a: jnp.transpose(a, (0, 2, 3, 1, 4))
    row = lambda a: a.reshape(1, -1)
    spec = lambda space: pl.BlockSpec(memory_space=space)
    win = (CL, NS, 7, 7, 2, C)
    whole = ((C, 1536), (C, C), (C, 2048), (2048, C))
    rows = (RT, C)
    keys = (CL, KP, C)
    tab = (4, TA * TB)
    reduce_scratch = []
    for r, w in zip(SHARD, WIDTH):
        u, h = 4 * r, 2 * r
        reduce_scratch += [VM((n, m, w), bf) for n, m in ((4, u), (2, h), (2, h), (2, h), (3, r))]
    field_shape = (CL, SIDE, SIDE, 2, C)
    outs = [
        (field_shape, bf), (field_shape, bf), *(((r, w), f32) for r, w in zip(SHARD, WIDTH)),
        ((1, 16), f32), ((1, 16), f32), ((2, 16), f32), ((1, 16), f32), ((1, 16), f32), ((1, 16), f32), ((1, 64), f32),
        ((1, 16), f32), (tab, f32),
    ]
    outs = [jax.ShapeDtypeStruct(s, d) for s, d in outs]
    results = pl.pallas_call(
        block_kernel,
        out_shape=outs,
        in_specs=[spec(pltpu.SMEM)] + [spec(pl.ANY)] * 2 + [spec(VM)] * 16,
        out_specs=[spec(pl.ANY)] * 2 + [spec(VM)] * 13,
        scratch_shapes=[
            VM((4, RP * HR, 128), f32), VM((CL, NHEAD, RP, KP), bf), *(VM(s, bf) for s in whole), VM(win, bf), VM(win, bf),
            VM(rows, bf), VM(rows, bf), VM(rows, bf), VM(rows, bf), VM(keys, bf), VM(keys, bf),
            VM(rows, bf), VM(rows, f32), VM(rows, bf), VM(rows, f32), VM((CL, RP, C), f32), VM(rows, bf),
            VM((RP, KP), f32), VM((RP, KP), f32), VM((32, 1, 256), f32), VM((NS, *tab), f32), VM((NS, *tab), bf), VM((TA * 16, TB), bf),
            VM((RP, 128), f32), VM((8, KP), f32), VM((16, C), f32), VM((16, C), f32), VM((TB, TA * 16), f32),
            VM((3, *tab), bf), VM((6, *tab), f32), VM((3, 16, C), f32), VM((7, 16, C), f32),
            *reduce_scratch,
            *(DMA((2, 3)), DMA((2, 3)), DMA((2,))) * 2, *(DMA((3,)), DMA((3,)), DMA) * 2,
            DMA((4,)), DMA((4,)), DMA((4, 23)), DMA((11,)), DMA((11,)), DMA((3,)), DMA((3,)),
            DMA((SEGS,)), DMA((SEGS,)), pltpu.SemaphoreType.REGULAR, DMA((2 * SEGS,)), DMA((2 * SEGS,)),
            DMA((4, 13)), DMA((4, 13)), DMA((6,)), DMA((6,)), DMA((6,)), DMA((6,)),
        ],
        compiler_params=pltpu.CompilerParams(
            collective_id=0, has_side_effects=True, vmem_limit_bytes=64 * 1024 * 1024 - 64 * 1024
        ),
    )(
        clip_order, field(clips), field(out_grad), qkv_weight, proj_weight, fc1_weight, fc2_weight,
        row(norm1_gain), row(norm1_bias), qv_bias, row(proj_bias), row(norm2_gain), row(norm2_bias),
        row(fc1_bias), row(fc2_bias), bias_table, region_label, rel_index, perm,
    )
    out_t, dx_t, oq, op, o1, o2, og1, ob1, oqv, opb, og2, ob2, ob3, ob4, otab = pl.pallas_call(
        publish_kernel,
        out_shape=outs,
        in_specs=[spec(VM)] * 15,
        out_specs=[spec(VM)] * 15,
    )(*results)
    back = lambda a: jnp.transpose(a, (0, 3, 1, 2, 4))
    flat = lambda a: a.reshape(-1)
    return (
        back(out_t), back(dx_t), flat(og1), flat(ob1), oq, oqv, otab[:, :TBL], op, flat(opb), flat(og2), flat(ob2),
        o1, flat(ob3), o2, flat(ob4),
    )


def solution(mesh):
    in_specs = (
        P("dp", "seq", None, None, None),
        P("dp", "seq", None, None, None),
        P("dp", None),
        P(),
        P(),
        P(("dp", "seq")),
        P(("dp", "seq")),
        P(("dp", "seq"), None),
        P(None, ("dp", "seq")),
        P("seq", None),
        P(("dp", "seq"), None),
        P(("dp", "seq")),
        P(("dp", "seq")),
        P(("dp", "seq")),
        P(("dp", "seq"), None),
        P(("dp", "seq")),
        P(("dp", "seq"), None),
        P(("dp", "seq")),
    )
    out_specs = (
        P("dp", "seq", None, None, None),
        P("dp", "seq", None, None, None),
        P(("dp", "seq")),
        P(("dp", "seq")),
        P(("dp", "seq"), None),
        P(None, ("dp", "seq")),
        P("seq", None),
        P(("dp", "seq"), None),
        P(("dp", "seq")),
        P(("dp", "seq")),
        P(("dp", "seq")),
        P(("dp", "seq"), None),
        P(("dp", "seq")),
        P(("dp", "seq"), None),
        P(("dp", "seq")),
    )
    local = windowed if mesh.shape["dp"] == 8 and mesh.shape["seq"] == NS else shards
    return jax.shard_map(local, mesh=mesh, in_specs=in_specs, out_specs=out_specs, check_vma=False)
```

```python
import functools
import math

import jax
import jax.numpy as jnp
import numpy as np
from jax import lax
from jax.experimental import pallas as pl
from jax.experimental.pallas import tpu as pltpu
from jax.sharding import PartitionSpec as P

HD = 32
WIN_T = 8
WIN_S = 7
SHIFT_T = 4
SHIFT_S = 3
FR = 8
SIDE = 14
MICRO = 2
NWIN = 4
WT = 392
TBL = 2535


eps_norm = 1e-05


def layer_norm(values, norm_gain, norm_shift):
    average = jnp.mean(values, axis=-1, keepdims=True)
    centred = values - average
    variance = jnp.mean(centred * centred, axis=-1, keepdims=True)
    return centred * lax.rsqrt(variance + eps_norm) * norm_gain + norm_shift


def gelu_exact(values):
    return jax.nn.gelu(values, approximate=False)


def matmul(left_side, right_side):
    return jnp.dot(left_side, right_side, preferred_element_type=jnp.float32)


def window_split(field):
    rolled = jnp.roll(field, (-SHIFT_T, -SHIFT_S, -SHIFT_S), (0, 1, 2))
    blocks = rolled.reshape(FR // WIN_T, WIN_T, SIDE // WIN_S, WIN_S, SIDE // WIN_S, WIN_S, -1)
    return blocks.transpose(0, 2, 4, 1, 3, 5, 6).reshape(NWIN, WT, -1)


def window_merge(windows):
    blocks = windows.reshape(FR // WIN_T, SIDE // WIN_S, SIDE // WIN_S, WIN_T, WIN_S, WIN_S, -1)
    field = blocks.transpose(0, 3, 1, 4, 2, 5, 6).reshape(FR, SIDE, SIDE, -1)
    return jnp.roll(field, (SHIFT_T, SHIFT_S, SHIFT_S), (0, 1, 2))


def to_heads(field_rows):
    feature_count = field_rows.shape[-1]
    windows = window_split(field_rows.reshape(FR, SIDE, SIDE, feature_count))
    return windows.reshape(NWIN, WT, feature_count // HD, HD)


def from_heads(windows):
    feature_count = windows.shape[-1] * windows.shape[-2]
    merged = window_merge(windows.reshape(NWIN, WT, feature_count))
    return merged.reshape(-1, feature_count)


def window_scores(query_win, key_win, rel_bias, keep_mask):
    scores = jnp.einsum("wihd,wjhd->whij", query_win, key_win, preferred_element_type=jnp.float32)
    scores = scores * HD ** (-0.5) + rel_bias[None]
    return jnp.where(keep_mask[:, None], scores, -1e30)


def attend_clip(query_rows, key_rows, value_rows, rel_bias, keep_mask):
    scores = window_scores(to_heads(query_rows), to_heads(key_rows), rel_bias, keep_mask)
    row_max = jnp.max(scores, axis=-1, keepdims=True)
    exponent = jnp.exp(scores - row_max)
    row_total = jnp.sum(exponent, axis=-1, keepdims=True)
    probabilities = (exponent / row_total).astype(jnp.bfloat16)
    attended = jnp.einsum(
        "whij,wjhd->wihd", probabilities, to_heads(value_rows), preferred_element_type=jnp.float32
    ).astype(jnp.bfloat16)
    return (from_heads(attended), (row_max + jnp.log(row_total))[..., 0])


def attend_back(query_rows, key_rows, value_rows, grad_rows, log_total, rel_bias, keep_mask):
    query_win = to_heads(query_rows)
    key_win = to_heads(key_rows)
    value_win = to_heads(value_rows)
    grad_win = to_heads(grad_rows)
    scores = window_scores(query_win, key_win, rel_bias, keep_mask)
    probabilities = jnp.exp(scores - log_total[..., None])
    grad_probs = jnp.einsum(
        "wihd,wjhd->whij", grad_win, value_win, preferred_element_type=jnp.float32
    )
    row_inner = jnp.sum(probabilities * grad_probs, axis=-1, keepdims=True)
    grad_scores = (probabilities * (grad_probs - row_inner)).astype(jnp.bfloat16)
    score_scale = HD ** (-0.5)
    grad_query = (
        jnp.einsum("whij,wjhd->wihd", grad_scores, key_win, preferred_element_type=jnp.float32)
        * score_scale
    )
    grad_key = (
        jnp.einsum("whij,wihd->wjhd", grad_scores, query_win, preferred_element_type=jnp.float32)
        * score_scale
    )
    grad_value = jnp.einsum(
        "whij,wihd->wjhd",
        probabilities.astype(jnp.bfloat16),
        grad_win,
        preferred_element_type=jnp.float32,
    )
    bias_term = jnp.sum(grad_scores.astype(jnp.float32), axis=0)
    return (
        from_heads(grad_query).astype(jnp.bfloat16),
        from_heads(grad_key).astype(jnp.bfloat16),
        from_heads(grad_value).astype(jnp.bfloat16),
        bias_term,
    )


def layer_pass(source, cot_block, full_weights, rel_bias, keep_mask):
    (
        norm_in_gain,
        norm_in_shift,
        qkv_w,
        qv_b,
        proj_w,
        proj_b,
        norm_mid_gain,
        norm_mid_shift,
        fc1_w,
        fc1_b,
        fc2_w,
        fc2_b,
    ) = full_weights
    clip_count = source.shape[0]
    model_width = source.shape[-1]
    shaped = (clip_count, -1, model_width)
    token_rows = source.reshape(-1, model_width).astype(jnp.float32)
    normed, norm_in_back = jax.vjp(
        layer_norm, token_rows, norm_in_gain.astype(jnp.float32), norm_in_shift.astype(jnp.float32)
    )
    normed_low = normed.astype(jnp.bfloat16)
    projected = matmul(normed_low, qkv_w)
    qv_float = qv_b.astype(jnp.float32)
    query_rows = (projected[:, :model_width] + qv_float[0]).astype(jnp.bfloat16)
    key_rows = projected[:, model_width : 2 * model_width].astype(jnp.bfloat16)
    value_rows = (projected[:, 2 * model_width :] + qv_float[1]).astype(jnp.bfloat16)
    parts = (
        lax.all_to_all(query_rows.reshape(shaped), "seq", split_axis=2, concat_axis=1, tiled=True),
        lax.all_to_all(key_rows.reshape(shaped), "seq", split_axis=2, concat_axis=1, tiled=True),
        lax.all_to_all(value_rows.reshape(shaped), "seq", split_axis=2, concat_axis=1, tiled=True),
    )
    merged_heads, log_total = lax.map(
        lambda clip_parts: attend_clip(*clip_parts, rel_bias, keep_mask), parts
    )
    attended_heads, log_total, query_heads, key_heads, value_heads = (
        merged_heads,
        log_total,
        parts[0],
        parts[1],
        parts[2],
    )
    attended = lax.all_to_all(
        attended_heads, "seq", split_axis=1, concat_axis=2, tiled=True
    ).reshape(-1, model_width)
    branch = matmul(attended, proj_w) + proj_b.astype(jnp.float32)
    middle = token_rows + branch
    normed_mid, norm_mid_back = jax.vjp(
        layer_norm, middle, norm_mid_gain.astype(jnp.float32), norm_mid_shift.astype(jnp.float32)
    )
    normed_mid_low = normed_mid.astype(jnp.bfloat16)
    hidden = matmul(normed_mid_low, fc1_w) + fc1_b.astype(jnp.float32)
    active, gelu_back = jax.vjp(gelu_exact, hidden)
    active_low = active.astype(jnp.bfloat16)
    result = matmul(active_low, fc2_w) + fc2_b.astype(jnp.float32)
    output = (middle + result).astype(jnp.bfloat16).reshape(source.shape)
    grad_low = cot_block.reshape(-1, model_width)
    grad_float = grad_low.astype(jnp.float32)
    grad_fc2_w = matmul(active_low.T, grad_low)
    grad_fc2_b = jnp.sum(grad_float, axis=0)
    grad_active = matmul(grad_low, fc2_w.T)
    grad_hidden = gelu_back(grad_active)[0].astype(jnp.bfloat16)
    grad_fc1_w = matmul(normed_mid_low.T, grad_hidden)
    grad_fc1_b = jnp.sum(grad_hidden.astype(jnp.float32), axis=0)
    grad_normed_mid = matmul(grad_hidden, fc1_w.T)
    grad_mid_part, grad_mid_gain, grad_mid_shift = norm_mid_back(grad_normed_mid)
    grad_middle = grad_float + grad_mid_part
    grad_branch = grad_middle.astype(jnp.bfloat16)
    grad_proj_w = matmul(attended.T, grad_branch)
    grad_proj_b = jnp.sum(grad_branch.astype(jnp.float32), axis=0)
    grad_attended = matmul(grad_branch, proj_w.T).astype(jnp.bfloat16)
    grad_heads = lax.all_to_all(
        grad_attended.reshape(shaped), "seq", split_axis=2, concat_axis=1, tiled=True
    )
    grad_query, grad_key, grad_value, bias_terms = lax.map(
        lambda clip_parts: attend_back(*clip_parts, rel_bias, keep_mask),
        (query_heads, key_heads, value_heads, grad_heads, log_total),
    )
    grad_query, grad_key, grad_value = (
        lax.all_to_all(grad_query, "seq", split_axis=1, concat_axis=2, tiled=True),
        lax.all_to_all(grad_key, "seq", split_axis=1, concat_axis=2, tiled=True),
        lax.all_to_all(grad_value, "seq", split_axis=1, concat_axis=2, tiled=True),
    )
    grad_query = grad_query.reshape(-1, model_width)
    grad_value = grad_value.reshape(-1, model_width)
    grad_projected = jnp.concatenate(
        [grad_query, grad_key.reshape(-1, model_width), grad_value], axis=1
    )
    grad_qkv_w = matmul(normed_low.T, grad_projected)
    grad_qv_b = jnp.stack(
        [
            jnp.sum(grad_query.astype(jnp.float32), axis=0),
            jnp.sum(grad_value.astype(jnp.float32), axis=0),
        ]
    )
    grad_normed = matmul(grad_projected, qkv_w.T)
    grad_rows_part, grad_in_gain, grad_in_shift = norm_in_back(grad_normed)
    grad_source = (grad_middle + grad_rows_part).astype(jnp.bfloat16).reshape(source.shape)
    grad_terms = (
        grad_in_gain,
        grad_in_shift,
        grad_qkv_w,
        grad_qv_b,
        grad_proj_w,
        grad_proj_b,
        grad_mid_gain,
        grad_mid_shift,
        grad_fc1_w,
        grad_fc1_b,
        grad_fc2_w,
        grad_fc2_b,
    )
    return (output, grad_source, grad_terms, jnp.sum(bias_terms, axis=0))


def shards(
    clips,
    out_grad,
    clip_order,
    region_label,
    rel_index,
    norm1_gain,
    norm1_bias,
    qkv_weight,
    qv_bias,
    bias_table,
    proj_weight,
    proj_bias,
    norm2_gain,
    norm2_bias,
    fc1_weight,
    fc1_bias,
    fc2_weight,
    fc2_bias,
):
    clip_count = clips.shape[0] // MICRO
    slot_order = clip_order[0]
    keep_mask = region_label[:, :, None] == region_label[:, None, :]
    rel_bias = jnp.take(bias_table.astype(jnp.float32), rel_index, axis=1)
    shard_set = (
        norm1_gain,
        norm1_bias,
        qkv_weight,
        qv_bias,
        proj_weight,
        proj_bias,
        norm2_gain,
        norm2_bias,
        fc1_weight,
        fc1_bias,
        fc2_weight,
        fc2_bias,
    )
    grad_sums = tuple((jnp.zeros(weight_shard.shape, jnp.float32) for weight_shard in shard_set))
    bias_sum = jnp.zeros(rel_bias.shape, jnp.float32)
    outputs = []
    source_grads = []
    for micro_index in range(MICRO):
        picked_slots = lax.dynamic_slice_in_dim(slot_order, micro_index * clip_count, clip_count)
        source = jnp.take(clips, picked_slots, axis=0)
        cot_block = out_grad[micro_index * clip_count : (micro_index + 1) * clip_count]
        full_weights = (
            lax.all_gather(norm1_gain, ("dp", "seq"), axis=0, tiled=True),
            lax.all_gather(norm1_bias, ("dp", "seq"), axis=0, tiled=True),
            lax.all_gather(qkv_weight, ("dp", "seq"), axis=0, tiled=True),
            lax.all_gather(qv_bias, ("dp", "seq"), axis=1, tiled=True),
            lax.all_gather(proj_weight, ("dp", "seq"), axis=0, tiled=True),
            lax.all_gather(proj_bias, ("dp", "seq"), axis=0, tiled=True),
            lax.all_gather(norm2_gain, ("dp", "seq"), axis=0, tiled=True),
            lax.all_gather(norm2_bias, ("dp", "seq"), axis=0, tiled=True),
            lax.all_gather(fc1_weight, ("dp", "seq"), axis=0, tiled=True),
            lax.all_gather(fc1_bias, ("dp", "seq"), axis=0, tiled=True),
            lax.all_gather(fc2_weight, ("dp", "seq"), axis=0, tiled=True),
            lax.all_gather(fc2_bias, ("dp", "seq"), axis=0, tiled=True),
        )
        output, grad_source, grad_terms, bias_term = layer_pass(
            source, cot_block, full_weights, rel_bias, keep_mask
        )
        grad_terms = (
            lax.psum_scatter(grad_terms[0], ("dp", "seq"), scatter_dimension=0, tiled=True),
            lax.psum_scatter(grad_terms[1], ("dp", "seq"), scatter_dimension=0, tiled=True),
            lax.psum_scatter(grad_terms[2], ("dp", "seq"), scatter_dimension=0, tiled=True),
            lax.psum_scatter(grad_terms[3], ("dp", "seq"), scatter_dimension=1, tiled=True),
            lax.psum_scatter(grad_terms[4], ("dp", "seq"), scatter_dimension=0, tiled=True),
            lax.psum_scatter(grad_terms[5], ("dp", "seq"), scatter_dimension=0, tiled=True),
            lax.psum_scatter(grad_terms[6], ("dp", "seq"), scatter_dimension=0, tiled=True),
            lax.psum_scatter(grad_terms[7], ("dp", "seq"), scatter_dimension=0, tiled=True),
            lax.psum_scatter(grad_terms[8], ("dp", "seq"), scatter_dimension=0, tiled=True),
            lax.psum_scatter(grad_terms[9], ("dp", "seq"), scatter_dimension=0, tiled=True),
            lax.psum_scatter(grad_terms[10], ("dp", "seq"), scatter_dimension=0, tiled=True),
            lax.psum_scatter(grad_terms[11], ("dp", "seq"), scatter_dimension=0, tiled=True),
        )
        grad_sums = tuple((previous + fresh for previous, fresh in zip(grad_sums, grad_terms)))
        bias_sum = bias_sum + bias_term
        outputs.append(output)
        source_grads.append(grad_source)
    flat_terms = bias_sum.reshape(bias_sum.shape[0], -1).T
    table_terms = jax.ops.segment_sum(flat_terms, rel_index.reshape(-1), num_segments=TBL).T
    table_grad = lax.psum(table_terms, "dp")
    output_all = jnp.concatenate(outputs, axis=0)
    clips_grad = jnp.zeros_like(clips).at[slot_order].set(jnp.concatenate(source_grads, axis=0))
    return (
        output_all,
        clips_grad,
        grad_sums[0],
        grad_sums[1],
        grad_sums[2],
        grad_sums[3],
        table_grad,
        grad_sums[4],
        grad_sums[5],
        grad_sums[6],
        grad_sums[7],
        grad_sums[8],
        grad_sums[9],
        grad_sums[10],
        grad_sums[11],
    )


EPS = 1e-5
LOG2E = math.log2(math.e)
LN2 = math.log(2.0)
SCALE = HD**-0.5
MASKED = -1e30
bf = jnp.bfloat16
f32 = jnp.float32
i32 = jnp.int32
MESH = pl.DeviceIdType.MESH
VM = pltpu.VMEM
DMA = pltpu.SemaphoreType.DMA

CL = 2
NS = 4
RP = 400
RT = CL * RP
KP = 512
C = 512
NHEAD = 16
TA = 10
HR = 17
TB = 256
SHARD = (16, 16, 16, 64)
WIDTH = (1536, 512, 2048, 512)
PARTS = ((0, 4), (4, 3))


def nn(a, b):
    return jnp.dot(a, b, preferred_element_type=f32)


def nt(a, b):
    return lax.dot_general(a, b, (((1,), (1,)), ((), ())), preferred_element_type=f32)


def tn(a, b):
    return lax.dot_general(a, b, (((0,), (0,)), ((), ())), preferred_element_type=f32)


def norm_parts(v):
    mu = jnp.mean(v, axis=-1, keepdims=True)
    c = v - mu
    r = lax.rsqrt(jnp.mean(c * c, axis=-1, keepdims=True) + EPS)
    return c * r, r


class Place:
    def __init__(self):
        dp, self.z = lax.axis_index("dp"), lax.axis_index("seq")
        self.dp = dp
        self.y, self.x, self.c = dp // 4, (dp // 2) % 2, dp % 2
        self.yn, self.xn, self.cn = 1 - self.y, 1 - self.x, 1 - self.c
        self.over_x = (self.dp_of(self.y, self.xn, self.c), self.z)
        self.over_y = (self.dp_of(self.yn, self.x, self.c), self.z)
        self.core = (self.dp_of(self.y, self.x, self.cn), self.z)
        self.corner = (self.dp_of(self.yn, self.xn, self.c), self.z)
        self.block = dp * 4 + self.z
        self.z1 = self.z + 1 - 2 * lax.rem(self.z, 2)
        self.z2 = lax.rem(self.z + 2, NS)
        self.z3 = NS - 1 - self.z

    def dp_of(self, y, x, c):
        return y * 4 + x * 2 + c

    def seq(self, z):
        return (self.dp, z)

    def far(self, d):
        return lax.rem(self.z + d, NS)

    def greet(self):
        bar = pltpu.get_barrier_semaphore()
        self.peers = [self.seq(self.far(d)) for d in (1, 2, 3)]
        self.peers += [self.over_x, self.over_y, self.corner, self.core]
        for peer in self.peers:
            pl.semaphore_signal(bar, inc=1, device_id=peer, device_id_type=MESH)

    def met(self):
        pl.semaphore_wait(pltpu.get_barrier_semaphore(), len(self.peers))


def rcopy(src, dst, ssem, rsem, dev):
    return pltpu.make_async_remote_copy(
        src_ref=src, dst_ref=dst, send_sem=ssem, recv_sem=rsem, device_id=dev, device_id_type=MESH
    )


def take(ref, sem):
    pltpu.make_async_copy(ref, ref, sem).wait()


def window_start(w, part):
    return lax.rem(7 * w + SHIFT_S + part, SIDE)


def send_windows(me, c, src, dst, ssem, rsem, lsem):
    slot = lax.rem(me.z + 2, NS)
    for d in range(NS):
        w = me.far(d)
        wy, wx = w // 2, lax.rem(w, 2)
        for y7, ny in PARTS:
            for x7, nx in PARTS:
                a = src.at[c, pl.ds(window_start(wy, y7), ny), pl.ds(window_start(wx, x7), nx)]
                b = dst.at[c, slot, pl.ds(y7, ny), pl.ds(x7, nx)]
                if d == 0:
                    pltpu.make_async_copy(a, b, lsem.at[c]).start()
                else:
                    rcopy(a, b, ssem.at[c, d - 1], rsem.at[c, d - 1], me.seq(w)).start()


def take_windows(me, c, dst, ssem, rsem, lsem):
    for d in range(NS):
        part = dst.at[c, lax.rem(me.z + NS - d + 2, NS)]
        if d == 0:
            take(part, lsem.at[c])
        else:
            take(part, rsem.at[c, d - 1])
            take(part, ssem.at[c, d - 1])


def send_home(me, clips, src, dst, ssem, rsem, lsem):
    wy, wx = me.z // 2, lax.rem(me.z, 2)
    for d in range(NS):
        t = me.far(d)
        slot = lax.rem(t + 2, NS)
        for c in clips:
            for y7, ny in PARTS:
                for x7, nx in PARTS:
                    a = src.at[c, slot, pl.ds(y7, ny), pl.ds(x7, nx)]
                    b = dst.at[c, pl.ds(window_start(wy, y7), ny), pl.ds(window_start(wx, x7), nx)]
                    if d == 0:
                        pltpu.make_async_copy(a, b, lsem).start()
                    else:
                        rcopy(a, b, ssem.at[d - 1], rsem.at[d - 1], me.seq(t)).start()


def take_home(me, src, ssem, rsem, lsem):
    take(src.at[:, 0], lsem)
    for d in (1, 2, 3):
        take(src.at[:, 0], rsem.at[d - 1])
        take(src.at[:, 0], ssem.at[d - 1])


class Gather:
    def __init__(self, me, k, shard, full, zsem, ssem, rsem):
        self.me, self.shard, self.full, self.r = me, shard, full, SHARD[k]
        self.zsem, self.ssem, self.rsem = zsem.at[k], ssem.at[k], rsem.at[k]

    def rows(self, dp, first=0, count=NS):
        return self.full.at[pl.ds(pl.multiple_of((dp * NS + first) * self.r, self.r), count * self.r)]

    def push(self, ref, slot, dev, sem=None):
        rcopy(ref, ref, self.ssem if sem is None else sem, self.rsem.at[slot], dev).start()

    def spread(self, z):
        block = self.rows(self.me.dp, z, 1)
        self.push(block, 4 + z, self.me.over_x)
        self.push(block, 8 + z, self.me.over_y)
        self.push(block, 16 + z, self.me.core)

    def fill(self):
        self.full[pl.ds(pl.multiple_of(self.me.block * self.r, self.r), self.r), :] = self.shard[...]

    def start(self):
        me = self.me
        self.spread(me.z)
        for z in (me.z2, me.z1):
            self.push(self.rows(me.dp, me.z, 1), me.z, me.seq(z), self.zsem)

    def came(self, z):
        take(self.rows(self.me.dp, z, 1), self.rsem.at[z])

    def step1(self):
        me = self.me
        self.came(me.z2)
        self.push(self.rows(me.dp, me.z2, 1), me.z2, me.seq(me.z1), self.zsem)
        self.spread(me.z2)

    def step2(self):
        for z in (self.me.z1, self.me.z3):
            self.came(z)
            self.spread(z)

    def corner(self):
        me = self.me
        dx, dy = me.over_x[0], me.over_y[0]
        for z in range(NS):
            take(self.rows(dx, z, 1), self.rsem.at[4 + z])
            if z < 2:
                self.push(self.rows(dx, z, 1), 12 + z, me.over_y)
        self.push(self.rows(dx), 20, me.core)
        for z in range(NS):
            take(self.rows(dy, z, 1), self.rsem.at[8 + z])
            if z >= 2:
                self.push(self.rows(dy, z, 1), 12 + z, me.over_x)
        self.push(self.rows(dy), 21, me.core)

    def last(self):
        me = self.me
        dd = me.dp_of(me.yn, me.xn, me.c)
        for z in range(NS):
            take(self.rows(dd, z, 1), self.rsem.at[12 + z])
        self.push(self.rows(dd), 22, me.core)

    def finish(self):
        me = self.me
        for z in range(NS):
            take(self.rows(me.dp_of(me.y, me.x, me.cn), z, 1), self.rsem.at[16 + z])
        for slot, (y, x) in ((20, (me.y, me.xn)), (21, (me.yn, me.x)), (22, (me.yn, me.xn))):
            take(self.rows(me.dp_of(y, x, me.cn)), self.rsem.at[slot])
        take(self.full.at[pl.ds(0, 3 * self.r)], self.zsem)
        take(self.full.at[pl.ds(0, 28 * self.r)], self.ssem)


class DirectGather(Gather):
    def spread(self, z):
        super().spread(z)
        self.push(self.rows(self.me.dp, z, 1), 12 + z, self.me.corner)

    def start(self):
        me = self.me
        for d in (1, 2, 3):
            self.push(self.rows(me.dp, me.z, 1), me.z, me.seq(me.far(d)), self.zsem)
        self.spread(me.z)

    def step(self, d):
        z = self.me.far(NS - d)
        self.came(z)
        self.spread(z)

    def groups(self):
        me = self.me
        for n, device in enumerate((me.over_x, me.over_y, me.corner)):
            for z in range(NS):
                take(self.rows(device[0], z, 1), self.rsem.at[(4, 8, 12)[n] + z])
            self.push(self.rows(device[0]), 20 + n, me.core)


class Vectors:
    def __init__(self, me, full, ssem, rsem):
        self.me, self.full, self.ssem, self.rsem = me, full, ssem, rsem

    def rows(self, dp, first=0, count=NS):
        return self.full.at[pl.ds(dp * NS + first, count)]

    def push(self, ref, slot, dev):
        rcopy(ref, ref, self.ssem.at[slot], self.rsem.at[slot], dev).start()

    def start(self):
        me = self.me
        for d in (1, 2, 3):
            self.push(self.rows(me.dp, me.z, 1), d - 1, me.seq(me.far(d)))

    def plane(self):
        me = self.me
        for d in (1, 2, 3):
            take(self.rows(me.dp, me.far(NS - d), 1), self.rsem.at[d - 1])
        for slot, dev in ((3, me.over_x), (4, me.over_y), (5, me.core)):
            self.push(self.rows(me.dp), slot, dev)

    def diagonal(self):
        me = self.me
        dx, dy = me.over_x[0], me.over_y[0]
        take(self.rows(dx), self.rsem.at[3])
        self.push(self.rows(dx), 6, me.over_y)
        self.push(self.rows(dx), 8, me.core)
        take(self.rows(dy), self.rsem.at[4])
        self.push(self.rows(dy), 9, me.core)

    def last(self):
        me = self.me
        dd = me.dp_of(me.yn, me.xn, me.c)
        take(self.rows(dd), self.rsem.at[6])
        self.push(self.rows(dd), 10, me.core)

    def finish(self):
        me = self.me
        for slot, (y, x) in ((5, (me.y, me.x)), (8, (me.y, me.xn)), (9, (me.yn, me.x)), (10, (me.yn, me.xn))):
            take(self.rows(me.dp_of(y, x, me.cn)), self.rsem.at[slot])
        for slot in (0, 1, 2, 3, 4, 5, 6, 8, 9, 10):
            take(self.rows(0, 0, 1) if slot < 3 else self.rows(0), self.ssem.at[slot])


def pack_vectors(me, sv, g1, b1, qv, pb, g2, b2, b3, b4):
    row = jnp.zeros((1, 256), f32)
    sv[pl.ds(me.block, 1), 0] = row
    pieces = (g1[...], b1[...], qv[0:1, :], qv[1:2, :], pb[...], g2[...], b2[...], b4[...])
    for k, piece in enumerate(pieces):
        sv[pl.ds(me.block, 1), 0, 16 * k : 16 * k + 16] = piece.astype(f32)
    sv[pl.ds(me.block, 1), 0, 128:192] = b3[...].astype(f32)


def spread_vectors(sv, vec):
    v = sv[...].reshape(32, 256).astype(bf)
    lane = lax.broadcasted_iota(i32, (256, C), 1)
    row = lax.broadcasted_iota(i32, (256, C), 0)
    blk = lax.broadcasted_iota(i32, (32, C), 0)
    col = lax.broadcasted_iota(i32, (32, C), 1)
    for k in range(12):
        if k < 8:
            pick, own = row == 16 * k + (lane & 15), blk == (col >> 4)
        else:
            pick, own = row == 128 + (lane & 63), blk == (col >> 6) + 8 * (k - 8)
        y = nn(v, jnp.where(pick, 1.0, 0.0).astype(bf))
        vec[k : k + 1, :] = jnp.sum(jnp.where(own, y, 0.0), axis=0, keepdims=True)


def one_hot(lo, i):
    d = jnp.broadcast_to(lo[pl.ds(i, 1), :], (16, KP)).astype(bf)
    d = d - lax.broadcasted_iota(i32, (16, KP), 0).astype(f32).astype(bf)
    one, zero = jnp.asarray(1, bf), jnp.asarray(0, bf)
    return jnp.concatenate([jnp.where(d == jnp.asarray(16 * c, bf), one, zero) for c in range(16)], axis=0)


def order_index(me, idx, lab, perm, hi, lo, colb, lrow):
    p = perm[...]
    iv = idx[...]
    for dst, part in ((hi, iv >> 8), (lo, iv & 255)):
        rows = nn(p[0:RP, :], part.astype(f32).astype(bf)).astype(bf)
        dst[...] = nt(rows, p)
    own = lab[pl.ds(me.z, 1), :].astype(f32)
    own = jnp.broadcast_to(own, (8, WT)).astype(bf)
    lane = lax.broadcasted_iota(i32, (8, KP), 1)
    lrow[...] = jnp.where(lane < WT, nt(own, p), -1.0)
    colb[...] = jnp.broadcast_to(nt(p[0:RP, :], own)[:, 0:1], (RP, 128))


def table_rows(tbl, tab):
    whole = jnp.concatenate([tbl[s].astype(f32) for s in range(NS)], axis=0)
    for a in range(TA):
        tab[a * 16 : (a + 1) * 16, :] = whole[:, a * TB : (a + 1) * TB].astype(bf)


def gather_rows(first, count, tab, hi, lo, colb, lrow, bias):
    unroll = 20

    def body(t, _):
        for u in range(unroll):
            i = first + t * unroll + u
            y = nn(tab[...], one_hot(lo, i))
            high = jnp.broadcast_to(hi[pl.ds(i, 1), :], (16, KP))
            acc = jnp.zeros((16, KP), f32)
            for a in range(TA):
                acc = jnp.where(high == a, y[a * 16 : (a + 1) * 16], acc)
            acc = acc * LOG2E
            own = colb[pl.ds(i, 1), :]
            r0 = i * HR
            for j in range(4):
                keep = lrow[0:1, j * 128 : (j + 1) * 128] == own
                bias[j, pl.ds(r0, 16), :] = jnp.where(keep, acc[:, j * 128 : (j + 1) * 128], MASKED)
        return 0

    lax.fori_loop(0, count // unroll, body, 0)


def scatter_rows(first, count, g, other, hi, lo, total):
    unroll = 10
    zero = jnp.asarray(0, bf)

    def body(t, _):
        ls, rs = [], []
        for u in range(unroll):
            n = t * unroll + u
            i = first + n
            rs.append(one_hot(lo, i))
            high = jnp.broadcast_to(hi[pl.ds(i, 1), :], (16, KP)).astype(bf)
            own = jnp.concatenate([g[j, pl.ds(i * HR, 16), :] for j in range(4)], axis=1)
            own = (own + other[pl.ds(pl.multiple_of(n * 16, 16), 16), :].astype(f32)).astype(bf)
            ls.append(jnp.concatenate([jnp.where(high == jnp.asarray(a, bf), own, zero) for a in range(TA)], axis=0))
        total[...] += nt(jnp.concatenate(rs, axis=1), jnp.concatenate(ls, axis=1))
        return 0

    lax.fori_loop(0, count // unroll, body, 0)


def load_tokens(src, clip, dst, p):
    for s in range(NS):
        v = src[clip, s].astype(f32).reshape(98, C)
        dst[p * RP + s * 98 : p * RP + (s + 1) * 98, :] = v.astype(dst.dtype)
    dst[p * RP + WT : (p + 1) * RP, :] = jnp.zeros((RP - WT, C), dst.dtype)


def store_tokens(src, clip, dst, slot):
    for s in range(NS):
        v = src[clip, s * 98 : (s + 1) * 98, :]
        dst[slot, s] = v.reshape(49, 2, C).astype(bf).reshape(7, 7, 2, C)


def qkv_phase(p, x, vec, wq, n1, q, k, v):
    r = slice(p * RP, (p + 1) * RP)
    k[p, RP:KP, :] = jnp.zeros((KP - RP, C), bf)
    v[p, RP:KP, :] = jnp.zeros((KP - RP, C), bf)
    n, _ = norm_parts(x[r, :].astype(f32))
    y = (n * vec[0:1, :] + vec[1:2, :]).astype(bf)
    n1[r, :] = y
    q[r, :] = ((nn(y, wq[:, 0:C]) + vec[2:3, :]) * (SCALE * LOG2E)).astype(bf)
    k[p, 0:RP, :] = nn(y, wq[:, C : 2 * C]).astype(bf)
    v[p, 0:RP, :] = (nn(y, wq[:, 2 * C : 3 * C]) + vec[3:4, :]).astype(bf)


def attention_forward(p, q, k, v, bias, e, att, inv, poll):
    lane = lax.broadcasted_iota(i32, (1, 128), 1) // HD

    def body(quad, _):
        l0 = pl.multiple_of(quad * 128, 128)
        r = slice(p * RP, (p + 1) * RP)
        qq = q[r, pl.ds(l0, 128)]
        kk = k[p, :, pl.ds(l0, 128)]
        vv = v[p, :, pl.ds(l0, 128)]
        acc = sums = jnp.zeros((RP, 128), f32)
        for hq in range(4):
            h = quad * 4 + hq
            s = nt(qq, jnp.where(lane == hq, kk, jnp.zeros_like(kk)))
            s = s + jnp.concatenate([bias[j, pl.ds(h, RP, stride=HR), :] for j in range(4)], axis=1)
            w = jnp.exp2(s - jnp.max(s, axis=1, keepdims=True)).astype(bf)
            e[p, h] = w
            o = nn(w, jnp.where(lane == hq, vv, jnp.ones_like(vv)))
            acc = jnp.where(lane == hq, o, acc)
            sums = jnp.where(lane == (hq + 1) % 4, o, sums)
        ainv = 1.0 / pltpu.roll(sums, 128 - HD, 1)
        att[r, pl.ds(l0, 128)] = (acc * ainv).astype(bf)
        inv[r, pl.ds(l0, 128)] = ainv
        poll(quad)
        return 0

    lax.fori_loop(0, 4, body, 0)


def feed_forward(x, att, vec, wp, w1, w2, nm, mid, out, keep):
    for p in range(CL):
        r = slice(p * RP, (p + 1) * RP)
        m = x[r, :].astype(f32) + nn(att[r, :], wp[...]) + vec[4:5, :]
        mid[r, :] = m
        n, _ = norm_parts(m)
        nm[r, :] = (n * vec[5:6, :] + vec[6:7, :]).astype(bf)
        out[p] = m + vec[7:8, :]

    def body(c, _):
        c0 = pl.multiple_of(c * C, C)
        for p in range(CL):
            r = slice(p * RP, (p + 1) * RP)
            hid = nn(nm[r, :], w1[:, pl.ds(c0, C)]) + vec[pl.ds(8 + c, 1), :]
            density = jnp.exp2(hid * hid * (-0.5 * LOG2E)) * (1 / math.sqrt(2 * math.pi))
            phi = 0.5 * (1.0 + lax.erf(hid * (1 / math.sqrt(2.0))))
            act = (hid * phi).astype(bf)
            slope = phi + hid * density
            out[p] += nn(act, w2[pl.ds(c0, C), :])
            for j in range(4):
                t = slice(j * 128, (j + 1) * 128)
                keep[c, j * RT + p * RP : j * RT + (p + 1) * RP, :] = slope[:, t]
                keep[c, (4 + j) * RT + p * RP : (4 + j) * RT + (p + 1) * RP, :] = act[:, t].astype(f32)
        return 0

    lax.fori_loop(0, 4, body, 0)


def feed_backward(dy, w1, w2, nm, acc, gvec, keep, poll):
    acc[...] = jnp.zeros_like(acc)
    gvec[7:8, :] = jnp.sum(dy[...].astype(f32), axis=0, keepdims=True)

    def body(c, _):
        c0 = pl.multiple_of(c * C, C)
        g1 = g2 = gb = None
        for p in range(CL):
            r = slice(p * RP, (p + 1) * RP)

            def kept(n):
                return jnp.concatenate(
                    [keep[c, (n + j) * RT + p * RP : (n + j) * RT + (p + 1) * RP, :] for j in range(4)], axis=1
                )

            dh = (nt(dy[r, :], w2[pl.ds(c0, C), :]) * kept(0)).astype(bf)
            acc[p] += nt(dh, w1[:, pl.ds(c0, C)])
            act = kept(4).astype(bf)
            a2, a1, ab = tn(act, dy[r, :]), tn(nm[r, :], dh), jnp.sum(dh.astype(f32), axis=0, keepdims=True)
            g2, g1, gb = (a2, a1, ab) if p == 0 else (g2 + a2, g1 + a1, gb + ab)
        gvec[pl.ds(8 + c, 1), :] = gb
        w2[pl.ds(c0, C), :] = g2.astype(bf)
        w1[:, pl.ds(c0, C)] = g1.astype(bf)
        poll(c)
        return 0

    lax.fori_loop(0, 4, body, 0)


def middle_backward(dy, att, vec, wp, mid, acc, inv, gvec, do):
    s4 = s5 = s6 = jnp.zeros((1, C), f32)
    parts = []
    for p in range(CL):
        r = slice(p * RP, (p + 1) * RP)
        n, rr = norm_parts(mid[r, :])
        gmn = acc[p]
        s5 += jnp.sum(gmn * n, axis=0, keepdims=True)
        s6 += jnp.sum(gmn, axis=0, keepdims=True)
        g = gmn * vec[5:6, :]
        gm = dy[r, :].astype(f32) + rr * (
            g - jnp.mean(g, axis=-1, keepdims=True) - n * jnp.mean(g * n, axis=-1, keepdims=True)
        )
        mid[r, :] = gm
        gb = gm.astype(bf)
        s4 += jnp.sum(gb.astype(f32), axis=0, keepdims=True)
        parts.append(gb)
        low = (nt(gb, wp[...]) * inv[r, :]).astype(bf)
        do[r, :] = low
        acc[p] = low.astype(f32) * att[r, :].astype(f32)
    gvec[4:5, :] = s4
    gvec[5:6, :] = s5
    gvec[6:7, :] = s6
    wp[...] = tn(att[...], jnp.concatenate(parts, axis=0)).astype(bf)


def attention_backward(q, k, v, e, do, prod, g, dq, dk, dv, poll):
    lane = lax.broadcasted_iota(i32, (1, 128), 1) // HD

    def body(quad, _):
        l0 = pl.multiple_of(quad * 128, 128)
        dqs = [jnp.zeros((RP, 128), f32) for _ in range(CL)]
        dks, dvs = [[], []], [[], []]
        qts = [q[p * RP : (p + 1) * RP, pl.ds(l0, 128)].T for p in range(CL)]
        dots = [do[p * RP : (p + 1) * RP, pl.ds(l0, 128)].T for p in range(CL)]
        for hq in range(4):
            h = quad * 4 + hq
            f = slice(hq * HD, (hq + 1) * HD)
            both = None
            for p in range(CL):
                r = slice(p * RP, (p + 1) * RP)
                kk = k[p, :, pl.ds(l0, 128)]
                vv = v[p, :, pl.ds(l0, 128)]
                dp = nt(do[r, pl.ds(l0, 128)], jnp.where(lane == hq, vv, jnp.zeros_like(vv)))
                inner = jnp.sum(jnp.where(lane == hq, prod[p, :, pl.ds(l0, 128)], 0.0), axis=1, keepdims=True)
                w = e[p, h]
                ds = w.astype(f32) * (dp - inner)
                both = ds if both is None else both + ds
                low = ds.astype(bf)
                dqs[p] = dqs[p] + nn(low, jnp.where(lane == hq, kk, jnp.zeros_like(kk)))
                dks[p].append((nn(qts[p][f], low) * LN2).astype(bf))
                dvs[p].append(nn(dots[p][f], w).astype(bf))
            for j in range(4):
                g[j, pl.ds(h, RP, stride=HR), :] = both[:, j * 128 : (j + 1) * 128]
            if hq == 1:
                poll(quad, 0)
        for p in range(CL):
            r = slice(p * RP, (p + 1) * RP)
            dq[r, pl.ds(l0, 128)] = (dqs[p] * SCALE).astype(bf)
            dk[r, pl.ds(l0, 128)] = jnp.concatenate(dks[p], axis=0).T[0:RP]
            dv[p, 0:RP, pl.ds(l0, 128)] = jnp.concatenate(dvs[p], axis=0).T[0:RP]
        poll(quad, 1)
        return 0

    lax.fori_loop(0, 4, body, 0)


def input_backward(x, n1, vec, wq, dq, dk, dv, mid, dx, gvec):
    s0 = s1 = s3 = jnp.zeros((1, C), f32)
    gvec[2:3, :] = jnp.sum(dq[...].astype(f32), axis=0, keepdims=True)
    for p in range(CL):
        r = slice(p * RP, (p + 1) * RP)
        dvp = dv[p, 0:RP, :]
        s3 += jnp.sum(dvp.astype(f32), axis=0, keepdims=True)
        gn = nt(dq[r, :], wq[:, 0:C]) + nt(dk[r, :], wq[:, C : 2 * C]) + nt(dvp, wq[:, 2 * C : 3 * C])
        n, rr = norm_parts(x[r, :].astype(f32))
        s0 += jnp.sum(gn * n, axis=0, keepdims=True)
        s1 += jnp.sum(gn, axis=0, keepdims=True)
        g = gn * vec[0:1, :]
        dx[p] = mid[r, :] + rr * (
            g - jnp.mean(g, axis=-1, keepdims=True) - n * jnp.mean(g * n, axis=-1, keepdims=True)
        )
    gvec[0:1, :] = s0
    gvec[1:2, :] = s1
    gvec[3:4, :] = s3
    n1t = n1[...].T
    wq[:, 0:C] = nn(n1t, dq[...]).astype(bf)
    wq[:, C : 2 * C] = nn(n1t, dk[...]).astype(bf)
    dva = jnp.concatenate([dv[p, 0:RP, :] for p in range(CL)], axis=0)
    wq[:, 2 * C : 3 * C] = nn(n1t, dva).astype(bf)


class Reduce:
    def __init__(self, me, k, grad, out, ssem, rsem, rc, rx, ry, ra, rz):
        self.me, self.r, self.grad, self.out = me, SHARD[k], grad, out
        self.u = 4 * self.r
        self.h = self.u // 2
        self.ssem, self.rsem = ssem.at[k], rsem.at[k]
        self.rc, self.rx, self.ry, self.ra, self.rz = rc, rx, ry, ra, rz

    def own(self, y, x, c, first=0, count=None):
        return pl.ds(pl.multiple_of(self.me.dp_of(y, x, c) * self.u + first, self.r), self.u if count is None else count)

    def send(self, rows, dst, slot, dev):
        rcopy(self.grad.at[rows], dst, self.ssem.at[slot], self.rsem.at[slot], dev).start()

    def add(self, rows, part, slot):
        take(part, self.rsem.at[slot])
        self.grad[rows, :] = self.grad[rows, :] + part[...]

    def core_part(self, g):
        self.send(self.own(g // 2, g % 2, self.me.cn), self.rc.at[g], g, self.me.core)

    def cores(self):
        for g in range(4):
            self.core_part(g)

    def plane(self):
        me, h = self.me, self.h
        for g in range(4):
            self.add(self.own(g // 2, g % 2, me.c), self.rc.at[g], g)
        for n in range(2):
            self.send(self.own(n, me.xn, me.c, 0, h), self.rx.at[n], 4 + n, me.over_x)
            self.send(self.own(me.yn, n, me.c, h, h), self.ry.at[n], 6 + n, me.over_y)

    def plane_part(self, g):
        me, h = self.me, self.h
        y, x = g // 2, g % 2
        self.add(self.own(y, x, me.c), self.rc.at[g], g)

        def over_x():
            self.send(self.own(y, x, me.c, 0, h), self.rx.at[y], 4 + y, me.over_x)

        def over_y():
            self.send(self.own(y, x, me.c, h, h), self.ry.at[x], 6 + x, me.over_y)

        pl.when(x == me.xn)(over_x)
        pl.when(y == me.yn)(over_y)

    def corner(self):
        me, h = self.me, self.h
        for n in range(2):
            self.add(self.own(n, me.x, me.c, 0, h), self.rx.at[n], 4 + n)
            self.add(self.own(me.y, n, me.c, h, h), self.ry.at[n], 6 + n)
        self.send(self.own(me.yn, me.x, me.c, 0, h), self.ra.at[0], 8, me.over_y)
        self.send(self.own(me.y, me.xn, me.c, h, h), self.ra.at[1], 9, me.over_x)

    def line(self):
        me, h, r = self.me, self.h, self.r
        for n in range(2):
            self.add(self.own(me.y, me.x, me.c, n * h, h), self.ra.at[n], 8 + n)
        for n, z in enumerate((me.z1, me.z3)):
            self.send(self.own(me.y, me.x, me.c, z * r, r), self.rz.at[n], 10 + n, me.seq(me.z1))

    def across(self):
        me, r = self.me, self.r
        rows = self.own(me.y, me.x, me.c, me.z2 * r, r)
        self.add(rows, self.rz.at[1], 11)
        self.send(rows, self.rz.at[2], 12, me.seq(me.z2))

    def finish(self):
        me, r, u, h = self.me, self.r, self.u, self.h
        total = self.grad[self.own(me.y, me.x, me.c, me.z * r, r), :].astype(f32)
        for n, slot in ((0, 10), (2, 12)):
            take(self.rz.at[n], self.rsem.at[slot])
            total = total + self.rz[n].astype(f32)
        self.out[...] = total
        for slot in range(13):
            count = u if slot < 4 else h if slot < 10 else r
            take(self.grad.at[pl.ds(0, count)], self.ssem.at[slot])


SEG = 40
SEGS = RP // 2 // SEG


def block_kernel(
    order, clips, cot, sq, sp, s1, s2, g1, b1, qv, pb, g2, b2, b3, b4, table, lab, idx, perm,
    out_t, dx_t, oq, op, o1, o2, og1, ob1, oqv, opb, og2, ob2, ob3, ob4, otab,
    bg, e, wq, wp, w1, w2, xw, dyw, x, dy, n1, q, k, v, att, inv, nm, mid, out, do,
    hi, lo, sv, tbl, tblb, tab, colb, lrow, vec, gvec, total, tz, tx, vz, vx,
    *rest,
):
    parts = [rest[5 * n : 5 * n + 5] for n in range(4)]
    (xs, xr, xl, ds_, dr, dl, os_, or_, ol, hs, hr, hl, wz, ws, wr, vs, vr, ts, tr, bs, br, free, es, er,
     rs, rr, zs, zr, as_, ar) = rest[20:]
    me = Place()
    me.greet()
    weights = [
        kind(me, n, shard, full, wz, ws, wr)
        for n, (kind, shard, full) in enumerate(
            ((DirectGather, sq, wq), (Gather, sp, wp), (Gather, s1, w1), (Gather, s2, w2))
        )
    ]
    first, later = weights[0], weights[1:]
    for w in weights:
        w.fill()
    pack_vectors(me, sv, g1, b1, qv, pb, g2, b2, b3, b4)
    tblb[pl.ds(me.z, 1), :, 2432:2560] = jnp.zeros((1, 4, 128), bf)
    tblb[pl.ds(me.z, 1), :, 0:TBL] = table[...][None]
    vectors = Vectors(me, sv, vs, vr)
    order_index(me, idx, lab, perm, hi, lo, colb, lrow)
    me.met()
    for d in (1, 2, 3):
        own = tblb.at[me.z]
        rcopy(own, own, ts.at[d - 1], tr.at[d - 1], me.seq(me.far(d))).start()
    first.start()
    vectors.start()
    for p in range(CL):
        send_windows(me, p, clips, xw, xs, xr, xl)
    for w in later:
        w.start()
    for d in (1, 2, 3):
        take(tblb.at[0], tr.at[d - 1])
        take(tblb.at[0], ts.at[d - 1])
    table_rows(tblb, tab)

    def bias_rows(n, half):
        return bg.at[:, pl.ds(pl.multiple_of((half * SEGS + n) * SEG * HR, 8), SEG * HR)]

    def rows(n):
        gather_rows((me.c * SEGS + n) * SEG, SEG, tab, hi, lo, colb, lrow, bg)
        part = bias_rows(n, me.c)
        rcopy(part, part, bs.at[n], br.at[n], me.core).start()

    rows(0)
    for d in (1, 3, 2):
        first.step(d)
    vectors.plane()
    rows(1)
    rows(2)
    vectors.diagonal()
    rows(3)
    first.groups()
    vectors.last()
    rows(4)
    vectors.finish()
    spread_vectors(sv, vec)
    first.finish()

    def first_poll(quad):
        pass

    def second_poll(quad):
        def second():
            for w in later:
                w.step2()

        pl.when(quad == 1)(second)

    for p, poll in enumerate((first_poll, second_poll)):
        take_windows(me, p, xw, xs, xr, xl)
        if p == 1:
            for w in later:
                w.step1()
            for c in range(CL):
                send_windows(me, c, cot, dyw, ds_, dr, dl)
        load_tokens(xw, p, x, p)
        qkv_phase(p, x, vec, wq, n1, q, k, v)
        if p == 0:
            for n in range(SEGS):
                take(bias_rows(n, me.cn), br.at[n])
                take(bias_rows(n, me.c), bs.at[n])
        attention_forward(p, q, k, v, bg, e, att, inv, poll)
    for w in later:
        w.corner()
    for w in later:
        w.last()
    gvec[...] = jnp.zeros_like(gvec)
    for w in later:
        w.finish()
    feed_forward(x, att, vec, wp, w1, w2, nm, mid, out, bg)
    for p in range(CL):
        store_tokens(out, order[0, p], xw, p)
    send_home(me, range(CL), xw, out_t, os_, or_, ol)
    reds = [
        Reduce(me, n, grad, total_out, rs, rr, *parts[n])
        for n, (grad, total_out) in enumerate(((wq, oq), (wp, op), (w1, o1), (w2, o2)))
    ]
    for p in range(CL):
        take_windows(me, p, dyw, ds_, dr, dl)
    for p in range(CL):
        load_tokens(dyw, order[0, p], dy, p)

    def chunk_poll(c):
        reds[3].core_part(c)
        pl.when(c > 0)(lambda: reds[3].plane_part(c - 1))

    feed_backward(dy, w1, w2, nm, out, gvec, bg, chunk_poll)
    reds[2].cores()
    reds[3].plane_part(3)
    middle_backward(dy, att, vec, wp, mid, out, inv, gvec, do)
    reds[1].cores()
    reds[2].plane()

    def backward_poll(quad, half):
        def both(name):
            for n in (2, 1):
                getattr(reds[n], name)()

        def start():
            reds[3].corner()
            reds[1].plane()

        steps = ((0, start), (5, reds[3].line), (6, lambda: both("corner")), (7, reds[3].across))
        for n, step in steps:
            if half == n % 2:
                pl.when(quad == n // 2)(step)

    attention_backward(q, k, v, e, do, out, bg, nm, att, v, backward_poll)
    pl.semaphore_signal(free, inc=1, device_id=me.core, device_id_type=MESH)
    input_backward(x, n1, vec, wq, nm, att, v, mid, out, gvec)
    reds[0].cores()
    for d in (1, 2, 3):
        rcopy(gvec, vz.at[d - 1], zs.at[d - 1], zr.at[d - 1], me.seq(me.far(d))).start()
    for n in (2, 1):
        reds[n].line()
    for p in range(CL):
        store_tokens(out, p, dyw, p)
    send_home(me, (0,), dyw, dx_t, hs, hr, hl)
    halves = ((0, SEG * 8), (1, SEG * 8))
    for n in range(SEGS):

        def lower(i, _, n=n):
            for m in range(2):
                for u in range(2):
                    at = m * SEG // 2 + u * SEG // 4 + i
                    r0 = ((me.cn * SEGS + n) * SEG + at) * HR
                    row = jnp.concatenate([bg[j, pl.ds(r0, 16), :] for j in range(4)], axis=1)
                    e[1, 2 * n + m, pl.ds(pl.multiple_of((u * SEG // 4 + i) * 16, 16), 16), :] = row.astype(bf)
            return 0

        lax.fori_loop(0, SEG // 4, lower, 0)
        if n == 0:
            pl.semaphore_wait(free, 1)
        for m, count in halves:
            rcopy(
                e.at[1, 2 * n + m, pl.ds(0, count)], e.at[0, 2 * n + m, pl.ds(0, count)],
                es.at[2 * n + m], er.at[2 * n + m], me.core,
            ).start()
    total[...] = jnp.zeros_like(total)

    def scatter(n):
        for m, count in halves:
            take(e.at[0, 2 * n + m, pl.ds(0, count)], er.at[2 * n + m])
        first = (me.c * SEGS + n) * SEG
        for m in range(2):
            scatter_rows(first + m * SEG // 2, SEG // 2, bg, e.at[0, 2 * n + m], hi, lo, total)

    reds[0].plane()
    scatter(0)
    for n in (2, 1):
        reds[n].across()
    scatter(1)
    reds[0].corner()
    scatter(2)
    reds[0].line()
    scatter(3)
    scatter(4)
    reds[0].across()
    sums = total[...].T
    for a in range(TA):
        for s in range(NS):
            tbl[s, :, a * TB : (a + 1) * TB] = sums[a * 16 + 4 * s : a * 16 + 4 * s + 4, :]
    tblb[...] = tbl[...].astype(bf)
    for d in (1, 2, 3):
        rcopy(tblb.at[me.far(d)], tz.at[d - 1], zs.at[2 + d], zr.at[2 + d], me.seq(me.far(d))).start()
    send_home(me, (1,), dyw, dx_t, hs, hr, hl)
    table = tbl[pl.ds(me.z, 1)].reshape(4, TA * TB)
    vecs = gvec[...]
    for d in (1, 2, 3):
        take(vz.at[d - 1], zr.at[d - 1])
        vecs = vecs + vz[d - 1]
    for n in (2, 3, 1):
        reds[n].finish()
    for d in (1, 2, 3):
        take(tz.at[d - 1], zr.at[2 + d])
        table = table + tz[d - 1].astype(f32)
    for n, dev in enumerate((me.core, me.over_x, me.over_y)):
        tx[2 * n] = table
        vx[2 * n] = vecs
        rcopy(tx.at[2 * n], tx.at[2 * n + 1], as_.at[2 * n], ar.at[2 * n], dev).start()
        rcopy(vx.at[2 * n], vx.at[2 * n + 1], as_.at[2 * n + 1], ar.at[2 * n + 1], dev).start()
        take(tx.at[2 * n + 1], ar.at[2 * n])
        take(vx.at[2 * n + 1], ar.at[2 * n + 1])
        table = table + tx[2 * n + 1]
        vecs = vecs + vx[2 * n + 1]
    otab[...] = table
    vx[6] = vecs
    part = pltpu.roll(vecs[0:8, :], C - me.block * 16, 1)
    for row, ref in ((0, og1), (1, ob1), (4, opb), (5, og2), (6, ob2), (7, ob4)):
        ref[...] = part[row : row + 1, 0:16]
    oqv[...] = part[2:4, 0:16]
    wide = jnp.broadcast_to(vx[6, pl.ds(8 + me.block // 8, 1), :], (8, C))
    ob3[...] = pltpu.roll(wide, C - lax.rem(me.block, 8) * 64, 1)[0:1, 0:64]
    reds[0].finish()
    for n in range(SEGS):
        for m, count in halves:
            take(e.at[1, 2 * n + m, pl.ds(0, count)], es.at[2 * n + m])
    for n in range(3):
        take(tx.at[0], as_.at[2 * n])
        take(vx.at[0], as_.at[2 * n + 1])
        take(vz.at[0], zs.at[n])
        take(tz.at[0], zs.at[3 + n])
    take_home(me, xw, os_, or_, ol)
    take_home(me, dyw, hs, hr, hl)


def publish_kernel(*refs):
    n = len(refs) // 2
    for source, target in zip(refs[:n], refs[n:]):
        target[...] = source[...]


def windowed(
    clips, out_grad, clip_order, region_label, rel_index, norm1_gain, norm1_bias, qkv_weight, qv_bias,
    bias_table, proj_weight, proj_bias, norm2_gain, norm2_bias, fc1_weight, fc1_bias, fc2_weight, fc2_bias,
):
    at = np.arange(WT)
    canonical = (2 * (at // 98) + at % 2) * 49 + (at % 98) // 2
    perm = np.zeros((KP, WT), np.float32)
    perm[at, canonical] = 1
    perm = jnp.asarray(perm, bf)
    field = lambda a: jnp.transpose(a, (0, 2, 3, 1, 4))
    row = lambda a: a.reshape(1, -1)
    spec = lambda space: pl.BlockSpec(memory_space=space)
    win = (CL, NS, 7, 7, 2, C)
    whole = ((C, 1536), (C, C), (C, 2048), (2048, C))
    rows = (RT, C)
    keys = (CL, KP, C)
    tab = (4, TA * TB)
    reduce_scratch = []
    for r, w in zip(SHARD, WIDTH):
        u, h = 4 * r, 2 * r
        reduce_scratch += [VM((n, m, w), bf) for n, m in ((4, u), (2, h), (2, h), (2, h), (3, r))]
    field_shape = (CL, SIDE, SIDE, 2, C)
    outs = [
        (field_shape, bf), (field_shape, bf), *(((r, w), f32) for r, w in zip(SHARD, WIDTH)),
        ((1, 16), f32), ((1, 16), f32), ((2, 16), f32), ((1, 16), f32), ((1, 16), f32), ((1, 16), f32), ((1, 64), f32),
        ((1, 16), f32), (tab, f32),
    ]
    outs = [jax.ShapeDtypeStruct(s, d) for s, d in outs]
    results = pl.pallas_call(
        block_kernel,
        out_shape=outs,
        in_specs=[spec(pltpu.SMEM)] + [spec(pl.ANY)] * 2 + [spec(VM)] * 16,
        out_specs=[spec(pl.ANY)] * 2 + [spec(VM)] * 13,
        scratch_shapes=[
            VM((4, RP * HR, 128), f32), VM((CL, NHEAD, RP, KP), bf), *(VM(s, bf) for s in whole), VM(win, bf), VM(win, bf),
            VM(rows, bf), VM(rows, bf), VM(rows, bf), VM(rows, bf), VM(keys, bf), VM(keys, bf),
            VM(rows, bf), VM(rows, f32), VM(rows, bf), VM(rows, f32), VM((CL, RP, C), f32), VM(rows, bf),
            VM((RP, KP), f32), VM((RP, KP), f32), VM((32, 1, 256), f32), VM((NS, *tab), f32), VM((NS, *tab), bf), VM((TA * 16, TB), bf),
            VM((RP, 128), f32), VM((8, KP), f32), VM((16, C), f32), VM((16, C), f32), VM((TB, TA * 16), f32),
            VM((3, *tab), bf), VM((6, *tab), f32), VM((3, 16, C), f32), VM((7, 16, C), f32),
            *reduce_scratch,
            *(DMA((2, 3)), DMA((2, 3)), DMA((2,))) * 2, *(DMA((3,)), DMA((3,)), DMA) * 2,
            DMA((4,)), DMA((4,)), DMA((4, 23)), DMA((11,)), DMA((11,)), DMA((3,)), DMA((3,)),
            DMA((SEGS,)), DMA((SEGS,)), pltpu.SemaphoreType.REGULAR, DMA((2 * SEGS,)), DMA((2 * SEGS,)),
            DMA((4, 13)), DMA((4, 13)), DMA((6,)), DMA((6,)), DMA((6,)), DMA((6,)),
        ],
        compiler_params=pltpu.CompilerParams(
            collective_id=0, has_side_effects=True, vmem_limit_bytes=64 * 1024 * 1024 - 64 * 1024
        ),
    )(
        clip_order, field(clips), field(out_grad), qkv_weight, proj_weight, fc1_weight, fc2_weight,
        row(norm1_gain), row(norm1_bias), qv_bias, row(proj_bias), row(norm2_gain), row(norm2_bias),
        row(fc1_bias), row(fc2_bias), bias_table, region_label, rel_index, perm,
    )
    out_t, dx_t, oq, op, o1, o2, og1, ob1, oqv, opb, og2, ob2, ob3, ob4, otab = pl.pallas_call(
        publish_kernel,
        out_shape=outs,
        in_specs=[spec(VM)] * 15,
        out_specs=[spec(VM)] * 15,
    )(*results)
    back = lambda a: jnp.transpose(a, (0, 3, 1, 2, 4))
    flat = lambda a: a.reshape(-1)
    return (
        back(out_t), back(dx_t), flat(og1), flat(ob1), oq, oqv, otab[:, :TBL], op, flat(opb), flat(og2), flat(ob2),
        o1, flat(ob3), o2, flat(ob4),
    )


def solution(mesh):
    in_specs = (
        P("dp", "seq", None, None, None),
        P("dp", "seq", None, None, None),
        P("dp", None),
        P(),
        P(),
        P(("dp", "seq")),
        P(("dp", "seq")),
        P(("dp", "seq"), None),
        P(None, ("dp", "seq")),
        P("seq", None),
        P(("dp", "seq"), None),
        P(("dp", "seq")),
        P(("dp", "seq")),
        P(("dp", "seq")),
        P(("dp", "seq"), None),
        P(("dp", "seq")),
        P(("dp", "seq"), None),
        P(("dp", "seq")),
    )
    out_specs = (
        P("dp", "seq", None, None, None),
        P("dp", "seq", None, None, None),
        P(("dp", "seq")),
        P(("dp", "seq")),
        P(("dp", "seq"), None),
        P(None, ("dp", "seq")),
        P("seq", None),
        P(("dp", "seq"), None),
        P(("dp", "seq")),
        P(("dp", "seq")),
        P(("dp", "seq")),
        P(("dp", "seq"), None),
        P(("dp", "seq")),
        P(("dp", "seq"), None),
        P(("dp", "seq")),
    )
    local = windowed if mesh.shape["dp"] == 8 and mesh.shape["seq"] == NS else shards
    return jax.shard_map(local, mesh=mesh, in_specs=in_specs, out_specs=out_specs, check_vma=False)
```
